32 devices in a mesh: dp: 8 (over z, x), head: 4 (over y, core).
Axes of the slice: x: 2, y: 2, z: 4, core: 2. Of those that a mesh axis runs over, the one named last changes fastest.
Arguments:
- tokens: bfloat16 [4096, 1024], P('dp'), may hold values from -6 to 6
- query_weight: bfloat16 [1024, 1024], P(None, 'head'), may hold values from -0.1875 to 0.1875
- key_weight: bfloat16 [1024, 1024], P(None, 'head'), may hold values from -0.1875 to 0.1875
- value_weight: bfloat16 [1024, 1024], P(None, 'head'), may hold values from -0.1875 to 0.1875
- output_weight: bfloat16 [1024, 1024], P('head'), may hold values from -0.75 to 0.75
- inner_weight: bfloat16 [1024, 4096], P(None, 'head'), may hold values from -0.1875 to 0.1875
- inner_bias: bfloat16 [4096], P('head'), may hold values from -3 to 3
- outer_weight: bfloat16 [4096, 1024], P('head'), may hold values from -0.125 to 0.125
- norm1_gain: float32 [1024], replicated, may hold values from 0.5 to 1.5
- norm1_shift: float32 [1024], replicated, may hold values from -1.75 to 1.75
- norm2_gain: float32 [1024], replicated, may hold values from 0.5 to 1.5
- norm2_shift: float32 [1024], replicated, may hold values from -1.75 to 1.75
- position_bias: float32 [8, 32], P('head'), may hold values from -6 to 6
- gate_logit: float32 [8], P('head'), may hold values from -2 to 2
- cache_keys: bfloat16 [4096, 1024], P('dp', 'head'), may hold values from -6 to 6
- cache_values: bfloat16 [4096, 1024], P('dp', 'head'), may hold values from -6 to 6
- memory_keys: bfloat16 [8, 1024, 1024], P('dp', None, 'head'), may hold values from -6 to 6
- memory_values: bfloat16 [8, 1024, 1024], P('dp', None, 'head'), may hold values from -6 to 6
- memory_index: int32 [4096, 8, 32], P('dp', 'head'), may hold values from 0 to 1023
- memory_fill: int32 [8], P('dp'), may hold values from 128 to 1024, as said below
- output_grad: bfloat16 [4096, 1024], P('dp'), may hold values from -6 to 6
Outputs:
- block_output: bfloat16 [4096, 1024], P('dp')
- grad_tokens: bfloat16 [4096, 1024], P('dp')
- grad_query_weight: float32 [1024, 1024], P(None, 'head')
- grad_key_weight: float32 [1024, 1024], P(None, 'head')
- grad_value_weight: float32 [1024, 1024], P(None, 'head')
- grad_output_weight: float32 [1024, 1024], P('head')
- grad_inner_weight: float32 [1024, 4096], P(None, 'head')
- grad_inner_bias: float32 [4096], P('head')
- grad_outer_weight: float32 [4096, 1024], P('head')
- grad_norm1_gain: float32 [1024], replicated
- grad_norm1_shift: float32 [1024], replicated
- grad_norm2_gain: float32 [1024], replicated
- grad_norm2_shift: float32 [1024], replicated
- grad_position_bias: float32 [8, 32], P('head')
- grad_gate_logit: float32 [8], P('head')
The draws below stay inside these ranges and needn't reach their ends.
Inputs may be any that keep to these rules, and one draw needn't show every extreme that they name: `memory_fill`: slots at or past a stream's fill count are empty and retrieved indices pointing there are ignored.
All inputs are finite; a program needn't handle non-finite values.
Results may differ from the reference program's by a relative error of at most 0.02.
Values may be sent and summed in bfloat16 or wider, within the bound.
A program may use at most 192 MiB of HBM per device.

```python
import jax
import jax.numpy as jnp
import numpy as np
from jax import lax

D = 1024
H = 8
DH = 128
FF = 4096
WIN = 512
NB = 32
MAXD = 128
TOPK = 32
MEM = 1024
STREAMS = 8
TOKENS = 4096
N_HEAD = 4


def draw_memory_fill(key, part):
    key = jax.random.fold_in(key, 11)
    draw_key, pick_key = jax.random.split(key)
    counts = jax.random.randint(draw_key, (STREAMS,), MEM // 8, MEM + 1)
    placing = jax.random.permutation(pick_key, STREAMS)
    counts = counts.at[placing[0]].set(MEM)
    counts = counts.at[placing[1]].set(MEM // 8)
    return counts.astype(jnp.int32)


def place_ends(values, own_key, low, largest):
    shape = values.shape
    place = [jax.random.randint(jax.random.fold_in(own_key, axis), (), 0, shape[axis]) for axis in range(len(shape))]
    values = values.at[tuple(place)].set(low)
    longest = shape.index(max(shape))
    place[longest] = (place[longest] + 1) % shape[longest]
    return values.at[tuple(place)].set(largest)


def levels(key, shape, cuts, low, largest):
    level, own = 1.0, jax.random.fold_in(key, 6)
    for dim, parts in cuts:
        steps = jnp.exp(jax.random.uniform(jax.random.fold_in(own, dim), (parts,), jnp.float32, low / len(cuts), largest / len(cuts)))
        level = level * jnp.repeat(steps, shape[dim] // parts).reshape([-1 if axis == dim else 1 for axis in range(len(shape))])
    return level


def bell_draw(rng, dims, spread, limit, cuts=(), kind=jnp.bfloat16):
    array = jax.random.normal(rng, dims, jnp.float32) * spread
    if len(cuts) > 0:
        array = levels(rng, dims, cuts, -0.22, 0.18) * array
    return jnp.clip(array, min=-limit, max=limit).astype(kind)


def setup_inputs(seed: int = 0) -> dict:
    keys = jax.random.split(jax.random.key(seed), 22)
    tokens = bell_draw(keys[0], (TOKENS, D), 1.0, 6.0, ((0, 8),))
    query_weight = bell_draw(keys[1], (D, H * DH), D ** -0.5, 0.1875, ((1, 4),))
    key_weight = bell_draw(keys[2], (D, H * DH), D ** -0.5, 0.1875, ((1, 4),))
    value_weight = bell_draw(keys[3], (D, H * DH), D ** -0.5, 0.1875, ((1, 4),))
    output_weight = bell_draw(keys[4], (H * DH, D), (H * DH // 16) ** -0.5, 0.75, ((0, 4),))
    inner_weight = bell_draw(keys[5], (D, FF), D ** -0.5, 0.1875, ((1, 4),))
    inner_bias = bell_draw(keys[6], (FF,), 0.5, 3.0, ((0, 4),))
    outer_weight = bell_draw(keys[7], (FF, D), (FF // 2) ** -0.5, 0.125, ((0, 4),))
    norm1_gain = jnp.clip(1.0 + 0.1 * jax.random.normal(keys[8], (D,), jnp.float32), 0.5, 1.5)
    norm1_shift = bell_draw(keys[9], (D,), 0.3, 1.75, (), jnp.float32)
    norm2_gain = jnp.clip(1.0 + 0.1 * jax.random.normal(keys[10], (D,), jnp.float32), 0.5, 1.5)
    norm2_shift = bell_draw(keys[11], (D,), 0.3, 1.75, (), jnp.float32)
    position_bias = bell_draw(keys[12], (H, NB), 1.0, 6.0, ((0, 4),), jnp.float32)
    gate_logit = jnp.clip(jax.random.uniform(keys[13], (H,), jnp.float32, -2.0, 2.0) * levels(keys[13], (H,), ((0, 4),), -0.4, 0.0), -2.0, 2.0)
    cache_keys = bell_draw(keys[14], (TOKENS, H * DH), 1.0, 6.0, ((0, 8), (1, 4)))
    cache_values = bell_draw(keys[15], (TOKENS, H * DH), 1.0, 6.0, ((0, 8), (1, 4)))
    memory_keys = bell_draw(keys[16], (STREAMS, MEM, H * DH), 1.0, 6.0, ((0, 8), (2, 4)))
    memory_values = bell_draw(keys[17], (STREAMS, MEM, H * DH), 1.0, 6.0, ((0, 8), (2, 4)))
    memory_index = place_ends(jax.random.randint(keys[18], (TOKENS, H, TOPK), 0, MEM), jax.random.fold_in(keys[18], 1), 0, MEM - 1).astype(jnp.int32)
    memory_fill = draw_memory_fill(jax.random.fold_in(keys[21], 71), 0)
    output_grad = bell_draw(keys[20], (TOKENS, D), 1.0, 6.0, ((0, 8),))
    return {"tokens": tokens, "query_weight": query_weight, "key_weight": key_weight, "value_weight": value_weight, "output_weight": output_weight, "inner_weight": inner_weight, "inner_bias": inner_bias, "outer_weight": outer_weight, "norm1_gain": norm1_gain, "norm1_shift": norm1_shift, "norm2_gain": norm2_gain, "norm2_shift": norm2_shift, "position_bias": position_bias, "gate_logit": gate_logit, "cache_keys": cache_keys, "cache_values": cache_values, "memory_keys": memory_keys, "memory_values": memory_values, "memory_index": memory_index, "memory_fill": memory_fill, "output_grad": output_grad}


@jax.custom_vjp
def low(v):
    return lax.optimization_barrier(v.astype(jnp.bfloat16)).astype(jnp.float32)

@jax.custom_vjp
def low_back(v):
    return v

def low_keep(v):
    return (low(v), None)

def low_pass(kept, grad):
    return (grad,)

def back_keep(v):
    return (v, None)

def back_low(kept, grad):
    return (low(grad),)
low.defvjp(low_keep, low_pass)
low_back.defvjp(back_keep, back_low)
EPSILON = 1e-05
FULL_PRECISION = lax.Precision.HIGHEST
NEGATIVE = -1e+30

def bucket_grid(length):
    rows_at = np.arange(length)[:, None] + length
    cols_at = np.arange(2 * length)[None, :]
    distance = rows_at - cols_at
    allowed = (distance >= 0) & (distance < length)
    span_abs = np.maximum(distance, 0)
    exact_count = NB // 2
    log_ratio = np.log(np.maximum(span_abs, 1) / exact_count) / np.log(MAXD / exact_count)
    larger = np.minimum(exact_count + (log_ratio * (NB - exact_count)).astype(np.int32), NB - 1)
    bucket = np.where(span_abs < exact_count, span_abs, larger).astype(np.int32)
    return (bucket, allowed)

def norm_rows(values, gain_row, shift_row):
    mean_row = lax.optimization_barrier(jnp.mean(values, axis=-1, keepdims=True))
    centered = values - mean_row
    variance = lax.optimization_barrier(jnp.mean(centered * centered, axis=-1, keepdims=True))
    return centered * lax.rsqrt(variance + EPSILON) * gain_row + shift_row

def attention_heads(query_rows, keys_now, values_now, past_keys, past_values, retrieved_keys, retrieved_values, slot_index, slot_valid, bias_table, gate_part):
    bucket_ids, allowed_pairs = bucket_grid(query_rows.shape[0])
    score_scale = 1.0 / np.sqrt(query_rows.shape[2])
    keys_all = jnp.concatenate([past_keys, keys_now], axis=0)
    values_all = jnp.concatenate([past_values, values_now], axis=0)
    raw_scores = low_back(jnp.einsum('ihd,jhd->hij', query_rows, keys_all, precision=FULL_PRECISION))
    scores = jnp.where(allowed_pairs, raw_scores * score_scale + bias_table[:, bucket_ids], NEGATIVE)
    row_peak = lax.optimization_barrier(jnp.max(scores, axis=-1, keepdims=True))
    exponent = jnp.exp(scores - row_peak)
    local_probs = low(exponent / lax.optimization_barrier(jnp.sum(exponent, axis=-1, keepdims=True)))
    local_out = low_back(jnp.einsum('hij,jhd->ihd', local_probs, values_all, precision=FULL_PRECISION))
    head_ids = jnp.arange(query_rows.shape[1], dtype=jnp.int32)[None, :, None]
    picked_keys = retrieved_keys[slot_index, head_ids]
    picked_values = retrieved_values[slot_index, head_ids]
    slot_scores = low_back(jnp.einsum('ihd,ihkd->ihk', query_rows, picked_keys, precision=FULL_PRECISION)) * score_scale
    slot_peak = jnp.maximum(lax.optimization_barrier(jnp.max(jnp.where(slot_valid, slot_scores, NEGATIVE), axis=-1, keepdims=True)), 0.0)
    slot_exp = jnp.exp(jnp.where(slot_valid, slot_scores - slot_peak, NEGATIVE))
    slot_total = jnp.exp(-slot_peak) + lax.optimization_barrier(jnp.sum(slot_exp, axis=-1, keepdims=True))
    slot_probs = low(slot_exp / slot_total)
    memory_output = low_back(jnp.einsum('ihk,ihkd->ihd', slot_probs, picked_values, precision=FULL_PRECISION))
    mixing = jax.nn.sigmoid(gate_part)[None, :, None]
    return mixing * memory_output + (1.0 - mixing) * local_out

def stream_forward(params, rows_in, extras):
    query_weight, key_weight, value_weight, output_weight, inner_weight, inner_bias, outer_weight, norm1_gain, norm1_shift, norm2_gain, norm2_shift, position_bias, gate_logit = params
    past_keys, past_values, retrieved_keys, retrieved_values, slot_index, slot_fill = extras
    row_count = rows_in.shape[0]
    group_heads = H // N_HEAD
    group_width = group_heads * DH
    group_inner = FF // N_HEAD
    normed = low(norm_rows(rows_in, norm1_gain, norm1_shift))
    slot_valid = slot_index < slot_fill
    attended = jnp.zeros_like(rows_in)
    for group_at in range(N_HEAD):
        col_from, col_to = (group_at * group_width, (group_at + 1) * group_width)
        head_from, head_to = (group_at * group_heads, (group_at + 1) * group_heads)
        shared = low_back(normed)
        query_rows = low_back(low(jnp.dot(shared, query_weight[:, col_from:col_to], precision=FULL_PRECISION))).reshape(row_count, group_heads, DH)
        keys_now = low_back(low(jnp.dot(shared, key_weight[:, col_from:col_to], precision=FULL_PRECISION))).reshape(row_count, group_heads, DH)
        values_now = low_back(low(jnp.dot(shared, value_weight[:, col_from:col_to], precision=FULL_PRECISION))).reshape(row_count, group_heads, DH)
        mixed = attention_heads(query_rows, keys_now, values_now, past_keys[:, col_from:col_to].reshape(row_count, group_heads, DH), past_values[:, col_from:col_to].reshape(row_count, group_heads, DH), retrieved_keys[:, col_from:col_to].reshape(-1, group_heads, DH), retrieved_values[:, col_from:col_to].reshape(-1, group_heads, DH), slot_index[:, head_from:head_to], slot_valid[:, head_from:head_to], position_bias[head_from:head_to], gate_logit[head_from:head_to])
        joined = low(mixed).reshape(row_count, group_width)
        attended = attended + low_back(low(jnp.dot(joined, output_weight[col_from:col_to], precision=FULL_PRECISION)))
    residual = rows_in + attended
    normed_two = low(norm_rows(residual, norm2_gain, norm2_shift))
    fed_sum = jnp.zeros_like(rows_in)
    for group_at in range(N_HEAD):
        unit_from, unit_to = (group_at * group_inner, (group_at + 1) * group_inner)
        shared = low_back(normed_two)
        inner_pre = low_back(jnp.dot(shared, inner_weight[:, unit_from:unit_to], precision=FULL_PRECISION) + inner_bias[unit_from:unit_to])
        active = low(jax.nn.gelu(inner_pre))
        fed_sum = fed_sum + low_back(low(jnp.dot(active, outer_weight[unit_from:unit_to], precision=FULL_PRECISION)))
    return residual + fed_sum

def reference(tokens, query_weight, key_weight, value_weight, output_weight, inner_weight, inner_bias, outer_weight, norm1_gain, norm1_shift, norm2_gain, norm2_shift, position_bias, gate_logit, cache_keys, cache_values, memory_keys, memory_values, memory_index, memory_fill, output_grad):
    params = tuple((entry.astype(jnp.float32) for entry in (query_weight, key_weight, value_weight, output_weight, inner_weight, inner_bias, outer_weight, norm1_gain, norm1_shift, norm2_gain, norm2_shift, position_bias, gate_logit)))
    stream_items = (tokens.reshape(STREAMS, WIN, D), cache_keys.reshape(STREAMS, WIN, H * DH), cache_values.reshape(STREAMS, WIN, H * DH), memory_keys, memory_values, memory_index.reshape(STREAMS, WIN, H, TOPK), memory_fill, output_grad.reshape(STREAMS, WIN, D))

    def step(totals, stream_item):
        rows_in, past_keys, past_values, retrieved_keys, retrieved_values, slot_index, slot_fill, grad_rows = stream_item
        extras = (past_keys.astype(jnp.float32), past_values.astype(jnp.float32), retrieved_keys.astype(jnp.float32), retrieved_values.astype(jnp.float32), slot_index, slot_fill)
        result, pullback = jax.vjp(lambda chosen, inputs: stream_forward(chosen, inputs, extras), params, rows_in.astype(jnp.float32))
        grad_params, grad_input = pullback(grad_rows.astype(jnp.float32))
        totals = jax.tree.map(lambda running, added: running + added, totals, grad_params)
        return (totals, (result.astype(jnp.bfloat16), grad_input.astype(jnp.bfloat16)))
    zero_grads = jax.tree.map(jnp.zeros_like, params)
    totals, (outputs, grad_inputs) = lax.scan(step, zero_grads, stream_items)
    return (outputs.reshape(TOKENS, D), grad_inputs.reshape(TOKENS, D), totals[0], totals[1], totals[2], totals[3], totals[4], totals[5], totals[6], totals[7], totals[8], totals[9], totals[10], totals[11], totals[12])
```

```python
import functools
import math
from types import SimpleNamespace as Space

import jax
import jax.numpy as jnp
import numpy as np
from jax import lax
from jax.experimental import pallas as pl
from jax.experimental.pallas import tpu as pltpu
from jax.sharding import PartitionSpec as P

NB = 32
MAXD = 128
EPSILON = 1e-05
NEGATIVE = -1e30
EXACT = lax.Precision.HIGHEST
BF = jnp.bfloat16
F32 = jnp.float32
LANES = 128
TILE = 256
SUBS = 2
MIB = 1 << 20
GELU_A = math.sqrt(2.0 / math.pi)
GELU_B = 0.044715


def bucket_rows(length):
    span = np.arange(length)
    exact = NB // 2
    ratio = np.log(np.maximum(span, 1) / exact) / np.log(MAXD / exact)
    larger = np.minimum(exact + (ratio * (NB - exact)).astype(np.int32), NB - 1)
    bucket = np.where(span < exact, span, larger).astype(np.int32)
    table = np.zeros((NB, length + length // 2), np.float32)
    for u in range(1, length + 1):
        table[bucket[length - u], u] = 1.0
    return table


def nn(a, b):
    return lax.dot_general(a, b, (((1,), (0,)), ((), ())), preferred_element_type=F32)


def nt(a, b):
    return lax.dot_general(a, b, (((1,), (1,)), ((), ())), preferred_element_type=F32)


def tn(a, b):
    return lax.dot_general(a, b, (((0,), (0,)), ((), ())), preferred_element_type=F32)


def row_stats(x):
    mean = jnp.mean(x, axis=-1, keepdims=True)
    c = x - mean
    var = jnp.mean(c * c, axis=-1, keepdims=True)
    return c, lax.rsqrt(var + EPSILON)


def stage_list(n):
    stages, stride, left = [], 1, n
    if left >= 2:
        stages.append((1, 2))
        stride, left = 2, left // 2
    while left >= 4:
        stages.append((stride, 4))
        stride, left = stride * 4, left // 4
    if left == 2:
        stages.append((stride, 2))
    return stages


def kernel(cfg, *refs):
    n = cfg.n
    R = Space(**dict(zip(cfg.names, refs)))
    T, D, G, U, M, NH = cfg.T, cfg.D, cfg.G, cfg.U, cfg.M, cfg.NH
    DH = G // NH
    HB = T // 2
    KW = T + HB
    scale = 1.0 / math.sqrt(DH)
    me = lax.axis_index("dp")
    hid = lax.axis_index("head")
    core = lax.rem(hid, 2)
    mate = {"head": hid + 1 - 2 * core}
    across = {"head": lax.rem(hid + 2, 4)}
    is0, is1 = core == 0, core == 1
    sub = HB // SUBS

    peers = []
    for stride, r in cfg.stages:
        d = lax.rem(me // stride, r)
        peers.append((d > 0, me - stride))
        peers.append((d < r - 1, me + stride))
    for s in cfg.doubling:
        covered = False
        for stride, r in cfg.stages:
            if s == stride:
                covered = True
        if not covered:
            b = lax.rem(me // s, 2)
            peers.append((True, me + s - 2 * s * b))
    barrier = pltpu.get_barrier_semaphore()
    want = 2
    pl.semaphore_signal(barrier, inc=1, device_id=mate)
    pl.semaphore_signal(barrier, inc=1, device_id=across)
    for cond, who in peers:
        if cond is True:
            pl.semaphore_signal(barrier, inc=1, device_id={"dp": who})
            want = want + 1
        else:

            @pl.when(cond)
            def _(who=who):
                pl.semaphore_signal(barrier, inc=1, device_id={"dp": who})

            want = want + jnp.where(cond, 1, 0).astype(jnp.int32)

    W3 = 3 * G
    loads = Space()

    def load(src, dst, sem):
        copy = pltpu.make_async_copy(src, dst, R.in_sem.at[sem])
        copy.start()
        return copy

    loads.tok = load(R.tok, R.tokv, 0)
    loads.idx = load(R.idx, R.idxv, 1)
    loads.wq = load(R.wq, R.wqkv.at[:, pl.ds(0, G)], 2)
    loads.wk = load(R.wk, R.wqkv.at[:, pl.ds(G, G)], 3)
    loads.wv = load(R.wv, R.wqkv.at[:, pl.ds(2 * G, G)], 4)
    loads.ck = load(R.ck, R.kext.at[pl.ds(0, T)], 5)
    loads.cv = load(R.cv, R.vext.at[pl.ds(0, T)], 6)
    loads.mk = load(R.mk.at[0], R.mkv, 7)
    loads.mv = load(R.mv.at[0], R.mvv, 8)
    loads.wo = load(R.wo, R.wov, 9)
    loads.og = load(R.og, R.ogv, 10)
    loads.wu = load(R.wu, R.wuv, 11)
    loads.wi = load(R.wi, R.wiv, 12)

    def push_desc(p, k):
        return pltpu.make_async_remote_copy(
            src_ref=R.part.at[p % 2, pl.ds(k * sub + (1 - core) * HB, sub)],
            dst_ref=R.cbuf.at[p % 2, pl.ds(k * sub, sub)],
            send_sem=R.c_send.at[p, k],
            recv_sem=R.c_recv.at[p, k],
            device_id=mate,
            device_id_type=pl.DeviceIdType.MESH,
        )

    def cross_desc(p, k):
        return pltpu.make_async_remote_copy(
            src_ref=R.part.at[p % 2, pl.ds(core * HB + k * sub, sub)],
            dst_ref=R.ybuf.at[p % 2, pl.ds(k * sub, sub)],
            send_sem=R.y_send.at[p, k],
            recv_sem=R.y_recv.at[p, k],
            device_id=across,
            device_id_type=pl.DeviceIdType.MESH,
        )

    def share_desc(p, k, buf, cc):
        rows = pl.ds(cc * HB + k * sub, sub)
        return pltpu.make_async_remote_copy(
            src_ref=buf.at[rows],
            dst_ref=buf.at[rows],
            send_sem=R.a_send.at[p, k],
            recv_sem=R.a_recv.at[p, k],
            device_id=mate,
            device_id_type=pl.DeviceIdType.MESH,
        )

    def push(p, rb):
        @pl.when(core != rb)
        def _():
            for k in range(SUBS):
                push_desc(p, k).start()

    def mid(p):
        for k in range(SUBS):
            push_desc(p, k).wait_recv()
            rows = pl.ds(core * HB + k * sub, sub)
            total = R.part[p % 2, rows, :].astype(F32) + R.cbuf[p % 2, pl.ds(k * sub, sub), :].astype(F32)
            R.part[p % 2, rows, :] = total.astype(BF)
            cross_desc(p, k).start()

    def sent(p):
        for k in range(SUBS):
            push_desc(p, k).wait_send()
            cross_desc(p, k).wait_send()

    def fin(p, k):
        cross_desc(p, k).wait_recv()
        rows = pl.ds(core * HB + k * sub, sub)
        return R.part[p % 2, rows, :].astype(F32) + R.ybuf[p % 2, pl.ds(k * sub, sub), :].astype(F32)

    RS_R, RS_S, AG_R, AG_S = R.rs_recv, R.rs_send, R.ag_recv, R.ag_send
    g, res, rbuf = R.g, R.res, R.rbuf
    SEG = cfg.seg

    plans = []
    for order in cfg.orders:
        base, length, off, plan = 0, SEG, 0, []
        for stride, r in order:
            d = lax.rem(me // stride, r)
            length = length // r
            left = off
            right = off if r == 2 else off + (r - 1) * length
            off = right + (r - 1) * length
            plan.append(Space(stride=stride, r=r, d=d, base=base, size=length, left=left, right=right))
            base = base + d * length
        plans.append(Space(stages=plan, own=base, own_len=length))

    def piece(st, o):
        at = st.base + o * st.size
        return pl.ds(at if isinstance(at, int) else pl.multiple_of(at, 16), st.size)

    def hop(st, right):
        return {"dp": me + st.stride if right else me - st.stride}

    def rs_desc(seg, t, st, right, o):
        slot = st.left + (o - 1) * st.size if right else st.right + o * st.size
        return pltpu.make_async_remote_copy(
            src_ref=g.at[seg, piece(st, o)],
            dst_ref=rbuf.at[seg, pl.ds(slot, st.size)],
            send_sem=RS_S.at[seg, t, int(right), o],
            recv_sem=RS_R.at[seg, t, int(right), o],
            device_id=hop(st, right),
            device_id_type=pl.DeviceIdType.MESH,
        )

    def ag_desc(seg, t, st, right, o):
        return pltpu.make_async_remote_copy(
            src_ref=res.at[seg, piece(st, o)],
            dst_ref=res.at[seg, piece(st, o)],
            send_sem=AG_S.at[seg, t, int(right), o],
            recv_sem=AG_R.at[seg, t, int(right), o],
            device_id=hop(st, right),
            device_id_type=pl.DeviceIdType.MESH,
        )

    def add_in(seg, st, right, o):
        slot = st.left + (o - 1) * st.size if right else st.right + o * st.size
        step = min(128, st.size)
        for i in range(st.size // step):
            at = st.base + o * st.size + i * step
            rows = pl.ds(at if isinstance(at, int) else pl.multiple_of(at, 16), step)
            total = g[seg, rows, :].astype(F32) + rbuf[seg, pl.ds(slot + i * step, step), :].astype(F32)
            g[seg, rows, :] = total.astype(BF)

    def each(segs, fn):
        lo, hi = segs
        if hi - lo == 1:
            fn(lo)
        elif hi > lo:
            lax.fori_loop(lo, hi, lambda s, c: (fn(s), c)[1], 0)

    def rs_first(plan, t, seg):
        st = plan.stages[t]
        r, d = st.r, st.d

        @pl.when(d == 0)
        def _():
            for o in range(r - 1, 0, -1):
                rs_desc(seg, t, st, True, o).start()

        @pl.when(d == r - 1)
        def _():
            for o in range(r - 1):
                rs_desc(seg, t, st, False, o).start()

    def rs_relay(plan, t, seg):
        st = plan.stages[t]
        r, d = st.r, st.d
        for j in range(r - 1):
            o = r - 1 - j

            @pl.when((d > 0) & (d <= o))
            def _(o=o):
                rs_desc(seg, t, st, True, o).wait_recv()
                add_in(seg, st, True, o)

            @pl.when((d > 0) & (d < o))
            def _(o=o):
                rs_desc(seg, t, st, True, o).start()

            @pl.when((d < r - 1) & (d >= j))
            def _(o=j):
                rs_desc(seg, t, st, False, o).wait_recv()
                add_in(seg, st, False, o)

            @pl.when((d < r - 1) & (d > j))
            def _(o=j):
                rs_desc(seg, t, st, False, o).start()

    def ag_first(plan, t, seg):
        st = plan.stages[t]
        r, d = st.r, st.d

        @pl.when(d < r - 1)
        def _():
            ag_desc(seg, t, st, True, d).start()

        @pl.when(d > 0)
        def _():
            ag_desc(seg, t, st, False, d).start()

    def ag_relay(plan, t, seg):
        st = plan.stages[t]
        r, d = st.r, st.d
        for j in range(1, r):

            @pl.when(d >= j)
            def _(j=j):
                ag_desc(seg, t, st, True, d - j).wait_recv()

            @pl.when((d >= j) & (d < r - 1))
            def _(j=j):
                ag_desc(seg, t, st, True, d - j).start()

            @pl.when(d + j <= r - 1)
            def _(j=j):
                ag_desc(seg, t, st, False, d + j).wait_recv()

            @pl.when((d + j <= r - 1) & (d > 0))
            def _(j=j):
                ag_desc(seg, t, st, False, d + j).start()

    def dp_start(segs, which):
        each(segs, lambda s: rs_first(plans[which], 0, s))

    def dp_step(segs, which, k):
        plan = plans[which]
        S = len(plan.stages)

        def one(seg):
            if k < S:
                rs_relay(plan, k, seg)
                if k + 1 < S:
                    rs_first(plan, k + 1, seg)
                else:
                    own = pl.ds(pl.multiple_of(plan.own, 16), plan.own_len)
                    res[seg, own, :] = g[seg, own, :]
                    ag_first(plan, S - 1, seg)
            else:
                t = 2 * S - 1 - k
                ag_relay(plan, t, seg)
                if t > 0:
                    ag_first(plan, t - 1, seg)

        each(segs, one)

    def dp_close(segs, which):
        plan = plans[which]

        def one(seg):
            for t, st in enumerate(plan.stages):
                r, d = st.r, st.d
                for o in range(1, r):

                    @pl.when(d < o)
                    def _(o=o):
                        rs_desc(seg, t, st, True, o).wait_send()

                    @pl.when((d <= o) & (d > 0))
                    def _(o=o):
                        ag_desc(seg, t, st, False, o).wait_send()

                for o in range(r - 1):

                    @pl.when(d > o)
                    def _(o=o):
                        rs_desc(seg, t, st, False, o).wait_send()

                    @pl.when((d >= o) & (d < r - 1))
                    def _(o=o):
                        ag_desc(seg, t, st, True, o).wait_send()

        each(segs, one)

    FA, FB, LA, LB = cfg.segs
    STEPS = 2 * len(cfg.stages)

    fill = R.fill[0]
    topk = cfg.K
    accs = M // LANES // 4
    loads.idx.wait()
    for h in range(NH):
        at = R.idxv[h]
        hi = at // LANES
        lo = at - hi * LANES
        fld = lax.rem(hi, 4)
        one = jnp.where(fld == 0, 1, jnp.where(fld == 1, 1 << 8, jnp.where(fld == 2, 1 << 16, 1 << 24)))
        R.lo[...] = lo
        for a in range(accs):
            ok = (at < fill) & (hi >= 4 * a) & (hi < 4 * a + 4)
            R.inc[a] = jnp.where(ok, one, 0)

        def count_block(b, c):
            lane = lax.broadcasted_iota(jnp.int32, (16, T), 0) + b * 16
            got = [jnp.zeros((16, T), jnp.int32) for _ in range(accs)]
            for k in range(topk):
                hit = jnp.broadcast_to(R.lo[pl.ds(k, 1), :], (16, T)) == lane
                for a in range(accs):
                    got[a] = got[a] + jnp.where(hit, jnp.broadcast_to(R.inc[a, pl.ds(k, 1), :], (16, T)), 0)
            for a in range(accs):
                R.cntt[a, pl.ds(pl.multiple_of(b * 16, 16), 16), :] = got[a]
            return c

        lax.fori_loop(0, LANES // 16, count_block, 0)
        for a in range(accs):
            R.cnt[h, a] = R.cntt[a].T

    loads.tok.wait()

    def norm_one(i, c):
        rows = pl.ds(pl.multiple_of(i * 128, 128), 128)
        cen, rstd = row_stats(R.tokv[rows, :].astype(F32))
        R.nrm[rows, :] = (cen * rstd * R.g1[...] + R.s1[...]).astype(BF)
        return c

    lax.fori_loop(0, T // 128, norm_one, 0)
    for copy in (loads.wq, loads.wk, loads.wv):
        copy.wait()
    for rb in range(2):
        rows = pl.ds(rb * HB, HB)
        low = R.nrm[rows, :]
        R.q[rows, :] = nn(low, R.wqkv[:, 0:G]).astype(BF)
        R.kext[pl.ds(T + rb * HB, HB), :] = nn(low, R.wqkv[:, G : 2 * G]).astype(BF)
        R.vext[pl.ds(T + rb * HB, HB), :] = nn(low, R.wqkv[:, 2 * G : W3]).astype(BF)

    band_row = lax.dot_general(
        R.table[...], R.oh[...], (((1,), (0,)), ((), ())), precision=EXACT, preferred_element_type=F32
    )
    u_at = lax.broadcasted_iota(jnp.int32, (NH, KW), 1)
    band_row = jnp.where((u_at >= 1) & (u_at <= T), band_row, NEGATIVE)
    for h in range(NH):
        wide = jnp.broadcast_to(band_row[h : h + 1, :], (HB, KW))
        R.band[h] = pltpu.roll(wide, 0, 1, stride=1, stride_axis=0)

    mix = jax.nn.sigmoid(R.gate[...])
    pl.semaphore_wait(barrier, want)

    for copy in (loads.ck, loads.cv, loads.mk, loads.mv, loads.wo):
        copy.wait()

    def attend(rb, h):
        rows = pl.ds(rb * HB, HB)
        cols = slice(h * DH, (h + 1) * DH)
        wide = pl.ds(rb * HB, KW)
        q = R.q[rows, cols]
        s = nt(q, R.kext[wide, cols]) * scale + R.band[h]
        e = jnp.exp(s - jnp.max(s, axis=-1, keepdims=True))
        p = (e * (1.0 / jnp.sum(e, axis=-1, keepdims=True))).astype(BF)
        R.pl[h, rows, :] = p
        near = nn(p, R.vext[wide, cols])
        s = nt(q, R.mkv[:, cols]) * scale
        parts = []
        for f in range(M // LANES):
            field = (R.cnt[h, f // 4, rows, :] >> (8 * (f % 4))) & 255
            parts.append(field.astype(F32))
        c = jnp.concatenate(parts, axis=1)
        s = jnp.where(c > 0.0, s, NEGATIVE)
        top = jnp.maximum(jnp.max(s, axis=-1, keepdims=True), 0.0)
        e = jnp.exp(s - top) * c
        total = jnp.exp(-top) + jnp.sum(e, axis=-1, keepdims=True)
        p = (e * (1.0 / total)).astype(BF)
        R.pm[h, rows, :] = p
        far = nn(p, R.mvv[:, cols])
        m = mix[:, h : h + 1]
        R.diff[rows, cols] = far - near
        R.joined[rows, cols] = (m * far + (1.0 - m) * near).astype(BF)

    def project(rb):
        rows = pl.ds(rb * HB, HB)
        for j in range(D // TILE):
            cols = slice(j * TILE, (j + 1) * TILE)
            R.part[0, rows, cols] = nn(R.joined[rows, :], R.wov[:, cols]).astype(BF)

    for h in range(NH):
        attend(0, h)
    project(0)
    push(0, 0)
    for h in range(NH):
        attend(1, h)
        if h == 0:

            @pl.when(is0)
            def _():
                mid(0)

    project(1)
    push(0, 1)

    @pl.when(is1)
    def _():
        mid(0)

    for copy in (loads.og, loads.wu, loads.wi):
        copy.wait()

    def tiles(count, fn):
        lax.fori_loop(0, count, lambda j, c: (fn(pl.ds(pl.multiple_of(j * TILE, TILE), TILE)), c)[1], 0)

    for rb in range(2):
        rows = pl.ds(rb * HB, HB)

        def back_one(cols, rows=rows):
            R.ga[rows, cols] = nt(R.ogv[rows, :], R.wuv[cols, :])

        tiles(U // TILE, back_one)

    own = pl.ds(pl.multiple_of(core * HB, HB), HB)

    def second_norm():
        for k in range(SUBS):
            rows = pl.ds(pl.multiple_of(core * HB + k * sub, sub), sub)
            x = R.tokv[rows, :].astype(F32) + fin(0, k)
            R.resid[pl.ds(k * sub, sub), :] = x
            cen, rstd = row_stats(x)
            R.ntl[rows, :] = (cen * rstd * R.g2[...] + R.s2[...]).astype(BF)
            share_desc(0, k, R.ntl, core).start()

    def feed(rb):
        rows = pl.ds(rb * HB, HB)

        def unit(cols):
            x = nn(R.ntl[rows, :], R.wiv[:, cols]) + R.ib[:, cols].astype(F32)
            x2 = x * x
            t = jnp.tanh(GELU_A * (x + GELU_B * x * x2))
            R.act[rows, cols] = (0.5 * x * (1.0 + t)).astype(BF)
            slope = 0.5 * (1.0 + t) + 0.5 * x * (1.0 - t * t) * (GELU_A * (1.0 + 3.0 * GELU_B * x2))
            gi = (R.ga[rows, cols] * slope).astype(BF)
            R.gi[rows, cols] = gi
            R.gib[pl.ds(rb, 1), cols] = jnp.sum(gi.astype(F32), axis=0, keepdims=True)

        tiles(U // TILE, unit)

        def back(cols):
            R.part[1, rows, cols] = nt(R.gi[rows, :], R.wiv[cols, :]).astype(BF)

        tiles(D // TILE, back)

    @pl.when(is0)
    def _():
        second_norm()

    @pl.when(is1)
    def _():
        for k in range(SUBS):
            share_desc(0, k, R.ntl, 0).wait_recv()

    feed(0)
    push(1, 0)

    @pl.when(is1)
    def _():
        second_norm()

    @pl.when(is0)
    def _():
        for k in range(SUBS):
            share_desc(0, k, R.ntl, 1).wait_recv()

    feed(1)
    push(1, 1)
    mid(1)

    R.tr[...] = R.act[...].T

    def outer_seg(j, c):
        g[j] = nn(R.tr[...], R.ogv[:, pl.ds(pl.multiple_of(j * TILE, TILE), TILE)]).astype(BF)
        return c

    def inner_seg(j, c):
        g[D // TILE + j] = nn(R.tr[...], R.gi[:, pl.ds(pl.multiple_of(j * TILE, TILE), TILE)]).astype(BF)
        return c

    lax.fori_loop(0, D // TILE, outer_seg, 0)
    outers = D // TILE
    dp_start((0, min(FA[1], outers)), 0)
    dp_start((FB[0], outers), 1)
    R.tr[...] = R.ntl[...].T
    lax.fori_loop(0, U // TILE, inner_seg, 0)
    dp_start((outers, FA[1]), 0)
    dp_start((max(FB[0], outers), FB[1]), 1)

    sent(0)
    for rb in range(2):
        rows = pl.ds(rb * HB, HB)

        def fed(cols, rows=rows):
            R.part[0, rows, cols] = nn(R.act[rows, :], R.wuv[:, cols]).astype(BF)

        tiles(D // TILE, fed)
        push(2, rb)

    sg2 = jnp.zeros((1, D), F32)
    ss2 = jnp.zeros((1, D), F32)
    for k in range(SUBS):
        rows = pl.ds(pl.multiple_of(core * HB + k * sub, sub), sub)
        dy = fin(1, k)
        cen, rstd = row_stats(R.resid[pl.ds(k * sub, sub), :])
        xh = cen * rstd
        sg2 = sg2 + jnp.sum(dy * xh, axis=0, keepdims=True)
        ss2 = ss2 + jnp.sum(dy, axis=0, keepdims=True)
        dx = dy * R.g2[...]
        dx = rstd * (
            dx - jnp.mean(dx, axis=-1, keepdims=True) - xh * jnp.mean(dx * xh, axis=-1, keepdims=True)
        )
        gr = R.ogv[rows, :].astype(F32) + dx
        R.gres[pl.ds(k * sub, sub), :] = gr
        R.gat[rows, :] = gr.astype(BF)
        share_desc(1, k, R.gat, core).start()
    R.small[0, 2:3, :] = sg2
    R.small[0, 3:4, :] = ss2
    mid(2)
    for k in range(SUBS):
        share_desc(1, k, R.gat, 1 - core).wait_recv()

    for h in range(NH):
        R.band[h] = jnp.zeros((HB, KW), F32)
    R.gkv[...] = jnp.zeros((2, T, G), F32)
    gate_sums = [jnp.zeros((1, 1), F32) for _ in range(NH)]
    for rb in range(2):
        rows = pl.ds(rb * HB, HB)
        wide = pl.ds(rb * HB, KW)
        gj_all = nt(R.gat[rows, :], R.wov[...])
        own_at = T - rb * HB
        own_rows = pl.ds(0, KW - own_at)
        for h in range(NH):
            cols = slice(h * DH, (h + 1) * DH)
            gj = gj_all[:, cols]
            m = mix[:, h : h + 1]
            gate_sums[h] = gate_sums[h] + jnp.sum(
                jnp.sum(gj * R.diff[rows, cols], axis=0, keepdims=True), axis=1, keepdims=True
            )
            gl = ((1.0 - m) * gj).astype(BF)
            gm = (m * gj).astype(BF)
            kx, vx = R.kext[wide, cols], R.vext[wide, cols]
            low = R.pl[h, rows, :]
            p = low.astype(F32)
            dp = nt(gl, vx)
            ds = p * (dp - jnp.sum(p * dp, axis=-1, keepdims=True))
            R.band[h] += ds
            raw = (ds * scale).astype(BF)
            gq = nn(raw, kx)
            R.gkv[0, own_rows, cols] += tn(raw[:, own_at:], R.q[rows, cols])
            R.gkv[1, own_rows, cols] += tn(low[:, own_at:], gl)
            p = R.pm[h, rows, :].astype(F32)
            dp = nt(gm, R.mvv[:, cols])
            ds = p * (dp - jnp.sum(p * dp, axis=-1, keepdims=True))
            gq = gq + nn((ds * scale).astype(BF), R.mkv[:, cols])
            R.gqkv[rows, cols] = gq.astype(BF)
    R.gqkv[:, G : 2 * G] = R.gkv[0].astype(BF)
    R.gqkv[:, 2 * G : W3] = R.gkv[1].astype(BF)

    tr = R.tr
    for j in range(D // TILE):
        g[cfg.seg_out, j * G : (j + 1) * G, :] = tn(
            R.joined[...], R.gat[:, j * TILE : (j + 1) * TILE]
        ).astype(BF)
    tr[...] = R.nrm[...].T

    def qkv_seg(j, c):
        g[cfg.seg_qkv + j] = nn(tr[...], R.gqkv[:, pl.ds(pl.multiple_of(j * TILE, TILE), TILE)]).astype(BF)
        return c

    lax.fori_loop(0, W3 // TILE, qkv_seg, 0)
    dp_start(LA, 0)
    dp_start(LB, 1)
    sent(1)
    for rb in range(2):
        rows = pl.ds(rb * HB, HB)

        def back_in(cols, rows=rows):
            R.part[1, rows, cols] = nt(R.gqkv[rows, :], R.wqkv[cols, :]).astype(BF)

        tiles(D // TILE, back_in)
        push(3, rb)

    for k in range(SUBS):
        rows = pl.ds(pl.multiple_of(core * HB + k * sub, sub), sub)
        R.bo[rows, :] = (R.resid[pl.ds(k * sub, sub), :] + fin(2, k)).astype(BF)
        share_desc(2, k, R.bo, core).start()

    mid(3)

    smalls = R.small
    at_row = lax.broadcasted_iota(jnp.int32, (8, KW), 0)
    table_grads = []
    for h in range(NH):
        half = HB
        cur = R.band[h]
        while half > 8:
            half //= 2
            cur = cur[:half] + pltpu.roll(cur[half:], KW - half, 1)
        for bit in (1, 2, 4):
            cur = jnp.where(lax.rem(at_row // bit, 2) == 1, pltpu.roll(cur, KW - bit, 1), cur)
        diag = jnp.sum(cur, axis=0, keepdims=True)
        table_grads.append(
            lax.dot_general(diag, R.oh[...], (((1,), (1,)), ((), ())), precision=EXACT, preferred_element_type=F32)
        )
    smalls[0, 4:5, :] = R.gib[0:1, :] + R.gib[1:2, :]
    smalls[0, 5:8, :] = jnp.zeros((3, D), F32)
    for h in range(NH):
        s = mix[:, h : h + 1]
        smalls[0, 5:6, h * LANES : h * LANES + NB] = table_grads[h]
        smalls[0, 6:7, h * LANES : (h + 1) * LANES] = jnp.broadcast_to(gate_sums[h] * s * (1.0 - s), (1, LANES))

    sg1 = jnp.zeros((1, D), F32)
    ss1 = jnp.zeros((1, D), F32)
    for k in range(SUBS):
        rows = pl.ds(pl.multiple_of(core * HB + k * sub, sub), sub)
        dy = fin(3, k)
        cen, rstd = row_stats(R.tokv[rows, :].astype(F32))
        xh = cen * rstd
        sg1 = sg1 + jnp.sum(dy * xh, axis=0, keepdims=True)
        ss1 = ss1 + jnp.sum(dy, axis=0, keepdims=True)
        dx = dy * R.g1[...]
        dx = rstd * (
            dx - jnp.mean(dx, axis=-1, keepdims=True) - xh * jnp.mean(dx * xh, axis=-1, keepdims=True)
        )
        R.gt[rows, :] = (R.gres[pl.ds(k * sub, sub), :] + dx).astype(BF)
        share_desc(3, k, R.gt, core).start()
    smalls[0, 0:1, :] = sg1
    smalls[0, 1:2, :] = ss1

    def small_desc(i, who):
        return pltpu.make_async_remote_copy(
            src_ref=smalls.at[i],
            dst_ref=R.sbuf.at[i],
            send_sem=R.s_send.at[i],
            recv_sem=R.s_recv.at[i],
            device_id=who,
            device_id_type=pl.DeviceIdType.MESH,
        )

    small_desc(0, mate).start()
    small_desc(0, mate).wait_recv()
    in_norm = lax.broadcasted_iota(jnp.int32, (8, D), 0) < 4
    smalls[1] = smalls[0] + jnp.where(in_norm, R.sbuf[0], 0.0)
    partners = []
    for i, s in enumerate(cfg.doubling):
        b = lax.rem(me // s, 2)
        who = {"dp": me + s - 2 * s * b}
        partners.append(who)
        small_desc(i + 1, who).start()
        small_desc(i + 1, who).wait_recv()
        smalls[i + 2] = smalls[i + 1] + R.sbuf[i + 1]

    for k in range(STEPS):
        dp_step(FB, 1, k)
        dp_step(FA, 0, k)
    for k in range(STEPS):
        dp_step(LB, 1, k)
        dp_step(LA, 0, k)

    outs = []

    def emit(src, dst):
        c = pltpu.make_async_copy(src, dst, R.out_sem.at[len(outs)])
        c.start()
        outs.append(c)

    for k in range(SUBS):
        share_desc(2, k, R.bo, 1 - core).wait_recv()
        share_desc(3, k, R.gt, 1 - core).wait_recv()
    emit(R.bo, R.block_out)
    emit(R.gt, R.gtok)
    for j in range(D // TILE):
        emit(res.at[j], R.gwu.at[:, pl.ds(j * TILE, TILE)])
        emit(res.at[cfg.seg_out, pl.ds(j * G, G)], R.gwo.at[:, pl.ds(j * TILE, TILE)])
    for j in range(U // TILE):
        emit(res.at[D // TILE + j], R.gwi.at[:, pl.ds(j * TILE, TILE)])
    emit(res.at[cfg.seg_qkv], R.gwq)
    emit(res.at[cfg.seg_qkv + 1], R.gwk)
    emit(res.at[cfg.seg_qkv + 2], R.gwv)
    emit(smalls.at[len(partners) + 1], R.gsmall)

    sent(2)
    sent(3)
    for p in range(4):
        for k in range(SUBS):
            share_desc(p, k, (R.ntl, R.gat, R.bo, R.gt)[p], core).wait_send()
    small_desc(0, mate).wait_send()
    for i, who in enumerate(partners):
        small_desc(i + 1, who).wait_send()
    dp_close(FA, 0)
    dp_close(FB, 1)
    dp_close(LA, 0)
    dp_close(LB, 1)
    for c in outs:
        c.wait()


def local(n, tokens, wq, wk, wv, wo, wi, ib, wu, g1, s1, g2, s2, table, gate, ck, cv, mk, mv, idx, fill, og):
    T, D = tokens.shape
    NH = table.shape[0]
    G = wq.shape[1]
    U = wi.shape[1]
    M = mk.shape[1]
    K = idx.shape[2]
    HB = T // 2
    KW = T + HB
    stages = stage_list(n)
    doubling = []
    s = 1
    while s < n:
        doubling.append(s)
        s *= 2
    ffn = (D + U) // TILE
    late = 1 + 3 * G // TILE
    nseg = ffn + late
    fa, la = 5 * ffn // 8, late // 2
    seg = D
    orders = (stages, stages[::-1])
    rows_needed = 0
    for order in orders:
        off, length = 0, seg
        for _, r in order:
            length //= r
            off += (1 if r == 2 else 2 * (r - 1)) * length
        rows_needed = max(rows_needed, off)
    inputs = dict(
        tok=tokens, idx=idx.transpose(1, 2, 0), wq=wq, wk=wk, wv=wv, wo=wo, wi=wi, wu=wu, ck=ck, cv=cv, mk=mk, mv=mv, og=og
    )
    vectors = dict(
        ib=ib.reshape(1, U), g1=g1.reshape(1, D), s1=s1.reshape(1, D), g2=g2.reshape(1, D), s2=s2.reshape(1, D),
        table=table, gate=gate.reshape(1, NH), oh=jnp.asarray(bucket_rows(T)),
    )
    outputs = dict(
        block_out=((T, D), BF), gtok=((T, D), BF), gwq=((D, G), BF), gwk=((D, G), BF), gwv=((D, G), BF),
        gwo=((G, D), BF), gwi=((D, U), BF), gwu=((U, D), BF), gsmall=((8, D), F32),
    )
    S = len(stages)
    sem = pltpu.SemaphoreType.DMA
    scratch = dict(
        tokv=pltpu.VMEM((T, D), BF), ogv=pltpu.VMEM((T, D), BF), idxv=pltpu.VMEM((NH, K, T), jnp.int32),
        wqkv=pltpu.VMEM((D, 3 * G), BF), wov=pltpu.VMEM((G, D), BF), wiv=pltpu.VMEM((D, U), BF),
        wuv=pltpu.VMEM((U, D), BF), kext=pltpu.VMEM((2 * T, G), BF), vext=pltpu.VMEM((2 * T, G), BF),
        mkv=pltpu.VMEM((M, G), BF), mvv=pltpu.VMEM((M, G), BF),
        lo=pltpu.VMEM((K, T), jnp.int32), inc=pltpu.VMEM((M // LANES // 4, K, T), jnp.int32),
        cntt=pltpu.VMEM((M // LANES // 4, LANES, T), jnp.int32),
        cnt=pltpu.VMEM((NH, M // LANES // 4, T, LANES), jnp.int32),
        nrm=pltpu.VMEM((T, D), BF), q=pltpu.VMEM((T, G), BF), band=pltpu.VMEM((NH, HB, KW), F32),
        pl=pltpu.VMEM((NH, T, KW), BF), pm=pltpu.VMEM((NH, T, M), BF), diff=pltpu.VMEM((T, G), F32),
        joined=pltpu.VMEM((T, G), BF), ga=pltpu.VMEM((T, U), F32), ntl=pltpu.VMEM((T, D), BF),
        resid=pltpu.VMEM((HB, D), F32), act=pltpu.VMEM((T, U), BF), gi=pltpu.VMEM((T, U), BF),
        gib=pltpu.VMEM((8, U), F32), tr=pltpu.VMEM((D, T), BF), gres=pltpu.VMEM((HB, D), F32),
        gat=pltpu.VMEM((T, D), BF), gkv=pltpu.VMEM((2, T, G), F32),
        gqkv=pltpu.VMEM((T, 3 * G), BF), bo=pltpu.VMEM((T, D), BF), gt=pltpu.VMEM((T, D), BF),
        part=pltpu.VMEM((2, T, D), BF), cbuf=pltpu.VMEM((2, HB, D), BF), ybuf=pltpu.VMEM((2, HB, D), BF),
        small=pltpu.VMEM((len(doubling) + 2, 8, D), F32), sbuf=pltpu.VMEM((len(doubling) + 1, 8, D), F32),
        g=pltpu.VMEM((nseg, seg, TILE), BF), res=pltpu.VMEM((nseg, seg, TILE), BF),
        rbuf=pltpu.VMEM((nseg, rows_needed, TILE), BF),
        in_sem=sem((13,)), out_sem=sem((2 + 2 * (D // TILE) + U // TILE + 4,)),
        c_send=sem((4, SUBS)), c_recv=sem((4, SUBS)), y_send=sem((4, SUBS)), y_recv=sem((4, SUBS)),
        a_send=sem((4, SUBS)), a_recv=sem((4, SUBS)),
        s_send=sem((len(doubling) + 1,)), s_recv=sem((len(doubling) + 1,)),
        rs_send=sem((nseg, S, 2, 4)), rs_recv=sem((nseg, S, 2, 4)),
        ag_send=sem((nseg, S, 2, 4)), ag_recv=sem((nseg, S, 2, 4)),
    )
    cfg = Space(
        n=n, T=T, D=D, G=G, U=U, M=M, NH=NH, K=K, stages=stages, doubling=doubling, orders=orders, seg=seg,
        segs=((0, fa), (fa, ffn), (ffn, ffn + la), (ffn + la, nseg)), seg_out=ffn, seg_qkv=ffn + 1,
        names=[*inputs, *vectors, "fill", *outputs, *scratch],
    )
    any_spec = pl.BlockSpec(memory_space=pl.ANY)
    vec_spec = pl.BlockSpec(memory_space=pltpu.VMEM)
    outs = pl.pallas_call(
        functools.partial(kernel, cfg),
        out_shape=[jax.ShapeDtypeStruct(*v) for v in outputs.values()],
        in_specs=[any_spec] * len(inputs) + [vec_spec] * len(vectors) + [pl.BlockSpec(memory_space=pltpu.SMEM)],
        out_specs=[any_spec] * len(outputs),
        scratch_shapes=list(scratch.values()),
        compiler_params=pltpu.CompilerParams(
            collective_id=0, has_side_effects=True, vmem_limit_bytes=63 * MIB
        ),
        cost_estimate=pl.CostEstimate(flops=12 * 10**9, bytes_accessed=20 * 10**6, transcendentals=3 * 10**6),
    )(
        *inputs.values(), *vectors.values(), fill,
    )
    block_out, gtok, gwq, gwk, gwv, gwo, gwi, gwu, small = outs
    bias = jnp.stack([small[5, h * LANES : h * LANES + NB] for h in range(NH)])
    gates = jnp.stack([small[6, h * LANES] for h in range(NH)])
    return (
        block_out, gtok, gwq.astype(F32), gwk.astype(F32), gwv.astype(F32), gwo.astype(F32), gwi.astype(F32),
        small[4], gwu.astype(F32), small[0], small[1], small[2], small[3], bias, gates,
    )


def solution(mesh):
    return jax.shard_map(
        functools.partial(local, mesh.shape["dp"]),
        mesh=mesh,
        in_specs=(
            P("dp", None), P(None, "head"), P(None, "head"), P(None, "head"), P("head", None), P(None, "head"),
            P("head"), P("head", None), P(), P(), P(), P(), P("head", None), P("head"), P("dp", "head"),
            P("dp", "head"), P("dp", None, "head"), P("dp", None, "head"), P("dp", "head", None), P("dp"),
            P("dp", None),
        ),
        out_specs=(
            P("dp", None), P("dp", None), P(None, "head"), P(None, "head"), P(None, "head"), P("head", None),
            P(None, "head"), P("head"), P("head", None), P(), P(), P(), P(), P("head", None), P("head"),
        ),
        check_vma=False,
    )
```

```python
import functools
import math
from types import SimpleNamespace as Space

import jax
import jax.numpy as jnp
import numpy as np
from jax import lax
from jax.experimental import pallas as pl
from jax.experimental.pallas import tpu as pltpu
from jax.sharding import PartitionSpec as P

NB = 32
MAXD = 128
EPSILON = 1e-05
NEGATIVE = -1e30
EXACT = lax.Precision.HIGHEST
BF = jnp.bfloat16
F32 = jnp.float32
LANES = 128
TILE = 256
SUBS = 2
MIB = 1 << 20
GELU_A = math.sqrt(2.0 / math.pi)
GELU_B = 0.044715


def bucket_rows(length):
    span = np.arange(length)
    exact = NB // 2
    ratio = np.log(np.maximum(span, 1) / exact) / np.log(MAXD / exact)
    larger = np.minimum(exact + (ratio * (NB - exact)).astype(np.int32), NB - 1)
    bucket = np.where(span < exact, span, larger).astype(np.int32)
    table = np.zeros((NB, length + length // 2), np.float32)
    for u in range(1, length + 1):
        table[bucket[length - u], u] = 1.0
    return table


def nn(a, b):
    return lax.dot_general(a, b, (((1,), (0,)), ((), ())), preferred_element_type=F32)


def nt(a, b):
    return lax.dot_general(a, b, (((1,), (1,)), ((), ())), preferred_element_type=F32)


def tn(a, b):
    return lax.dot_general(a, b, (((0,), (0,)), ((), ())), preferred_element_type=F32)


def row_stats(x):
    mean = jnp.mean(x, axis=-1, keepdims=True)
    c = x - mean
    var = jnp.mean(c * c, axis=-1, keepdims=True)
    return c, lax.rsqrt(var + EPSILON)


def stage_list(n):
    stages, stride, left = [], 1, n
    if left >= 2:
        stages.append((1, 2))
        stride, left = 2, left // 2
    while left >= 4:
        stages.append((stride, 4))
        stride, left = stride * 4, left // 4
    if left == 2:
        stages.append((stride, 2))
    return stages


def kernel(cfg, *refs):
    n = cfg.n
    R = Space(**dict(zip(cfg.names, refs)))
    T, D, G, U, M, NH = cfg.T, cfg.D, cfg.G, cfg.U, cfg.M, cfg.NH
    DH = G // NH
    HB = T // 2
    KW = T + HB
    scale = 1.0 / math.sqrt(DH)
    me = lax.axis_index("dp")
    hid = lax.axis_index("head")
    core = lax.rem(hid, 2)
    mate = {"head": hid + 1 - 2 * core}
    across = {"head": lax.rem(hid + 2, 4)}
    is0, is1 = core == 0, core == 1
    sub = HB // SUBS

    peers = []
    for stride, r in cfg.stages:
        d = lax.rem(me // stride, r)
        peers.append((d > 0, me - stride))
        peers.append((d < r - 1, me + stride))
    for s in cfg.doubling:
        covered = False
        for stride, r in cfg.stages:
            if s == stride:
                covered = True
        if not covered:
            b = lax.rem(me // s, 2)
            peers.append((True, me + s - 2 * s * b))
    barrier = pltpu.get_barrier_semaphore()
    want = 2
    pl.semaphore_signal(barrier, inc=1, device_id=mate)
    pl.semaphore_signal(barrier, inc=1, device_id=across)
    for cond, who in peers:
        if cond is True:
            pl.semaphore_signal(barrier, inc=1, device_id={"dp": who})
            want = want + 1
        else:

            @pl.when(cond)
            def _(who=who):
                pl.semaphore_signal(barrier, inc=1, device_id={"dp": who})

            want = want + jnp.where(cond, 1, 0).astype(jnp.int32)

    W3 = 3 * G
    loads = Space()

    def load(src, dst, sem):
        copy = pltpu.make_async_copy(src, dst, R.in_sem.at[sem])
        copy.start()
        return copy

    loads.tok = load(R.tok, R.tokv, 0)
    loads.idx = load(R.idx, R.idxv, 1)
    loads.wq = load(R.wq, R.wqkv.at[:, pl.ds(0, G)], 2)
    loads.wk = load(R.wk, R.wqkv.at[:, pl.ds(G, G)], 3)
    loads.wv = load(R.wv, R.wqkv.at[:, pl.ds(2 * G, G)], 4)
    loads.ck = load(R.ck, R.kext.at[pl.ds(0, T)], 5)
    loads.cv = load(R.cv, R.vext.at[pl.ds(0, T)], 6)
    loads.mk = load(R.mk.at[0], R.mkv, 7)
    loads.mv = load(R.mv.at[0], R.mvv, 8)
    loads.wo = load(R.wo, R.wov, 9)
    loads.og = load(R.og, R.ogv, 10)
    loads.wu = load(R.wu, R.wuv, 11)
    loads.wi = load(R.wi, R.wiv, 12)

    def push_desc(p, k):
        return pltpu.make_async_remote_copy(
            src_ref=R.part.at[p % 2, pl.ds(k * sub + (1 - core) * HB, sub)],
            dst_ref=R.cbuf.at[p % 2, pl.ds(k * sub, sub)],
            send_sem=R.c_send.at[p, k],
            recv_sem=R.c_recv.at[p, k],
            device_id=mate,
            device_id_type=pl.DeviceIdType.MESH,
        )

    def cross_desc(p, k):
        return pltpu.make_async_remote_copy(
            src_ref=R.part.at[p % 2, pl.ds(core * HB + k * sub, sub)],
            dst_ref=R.ybuf.at[p % 2, pl.ds(k * sub, sub)],
            send_sem=R.y_send.at[p, k],
            recv_sem=R.y_recv.at[p, k],
            device_id=across,
            device_id_type=pl.DeviceIdType.MESH,
        )

    def share_desc(p, k, buf, cc):
        rows = pl.ds(cc * HB + k * sub, sub)
        return pltpu.make_async_remote_copy(
            src_ref=buf.at[rows],
            dst_ref=buf.at[rows],
            send_sem=R.a_send.at[p, k],
            recv_sem=R.a_recv.at[p, k],
            device_id=mate,
            device_id_type=pl.DeviceIdType.MESH,
        )

    def push(p, rb):
        @pl.when(core != rb)
        def _():
            for k in range(SUBS):
                push_desc(p, k).start()

    def mid(p):
        for k in range(SUBS):
            push_desc(p, k).wait_recv()
            rows = pl.ds(core * HB + k * sub, sub)
            total = R.part[p % 2, rows, :].astype(F32) + R.cbuf[p % 2, pl.ds(k * sub, sub), :].astype(F32)
            R.part[p % 2, rows, :] = total.astype(BF)
            cross_desc(p, k).start()

    def sent(p):
        for k in range(SUBS):
            push_desc(p, k).wait_send()
            cross_desc(p, k).wait_send()

    def fin(p, k):
        cross_desc(p, k).wait_recv()
        rows = pl.ds(core * HB + k * sub, sub)
        return R.part[p % 2, rows, :].astype(F32) + R.ybuf[p % 2, pl.ds(k * sub, sub), :].astype(F32)

    RS_R, RS_S, AG_R, AG_S = R.rs_recv, R.rs_send, R.ag_recv, R.ag_send
    g, res, rbuf = R.g, R.res, R.rbuf
    SEG = cfg.seg

    plans = []
    for order in cfg.orders:
        base, length, off, plan = 0, SEG, 0, []
        for stride, r in order:
            d = lax.rem(me // stride, r)
            length = length // r
            left = off
            right = off if r == 2 else off + (r - 1) * length
            off = right + (r - 1) * length
            plan.append(Space(stride=stride, r=r, d=d, base=base, size=length, left=left, right=right))
            base = base + d * length
        plans.append(Space(stages=plan, own=base, own_len=length))

    def piece(st, o):
        at = st.base + o * st.size
        return pl.ds(at if isinstance(at, int) else pl.multiple_of(at, 16), st.size)

    def hop(st, right):
        return {"dp": me + st.stride if right else me - st.stride}

    def rs_desc(seg, t, st, right, o):
        slot = st.left + (o - 1) * st.size if right else st.right + o * st.size
        return pltpu.make_async_remote_copy(
            src_ref=g.at[seg, piece(st, o)],
            dst_ref=rbuf.at[seg, pl.ds(slot, st.size)],
            send_sem=RS_S.at[seg, t, int(right), o],
            recv_sem=RS_R.at[seg, t, int(right), o],
            device_id=hop(st, right),
            device_id_type=pl.DeviceIdType.MESH,
        )

    def ag_desc(seg, t, st, right, o):
        return pltpu.make_async_remote_copy(
            src_ref=res.at[seg, piece(st, o)],
            dst_ref=res.at[seg, piece(st, o)],
            send_sem=AG_S.at[seg, t, int(right), o],
            recv_sem=AG_R.at[seg, t, int(right), o],
            device_id=hop(st, right),
            device_id_type=pl.DeviceIdType.MESH,
        )

    def add_in(seg, st, right, o):
        slot = st.left + (o - 1) * st.size if right else st.right + o * st.size
        step = min(128, st.size)
        for i in range(st.size // step):
            at = st.base + o * st.size + i * step
            rows = pl.ds(at if isinstance(at, int) else pl.multiple_of(at, 16), step)
            total = g[seg, rows, :].astype(F32) + rbuf[seg, pl.ds(slot + i * step, step), :].astype(F32)
            g[seg, rows, :] = total.astype(BF)

    def each(segs, fn):
        lo, hi = segs
        if hi - lo == 1:
            fn(lo)
        elif hi > lo:
            lax.fori_loop(lo, hi, lambda s, c: (fn(s), c)[1], 0)

    def rs_first(plan, t, seg):
        st = plan.stages[t]
        r, d = st.r, st.d

        @pl.when(d == 0)
        def _():
            for o in range(r - 1, 0, -1):
                rs_desc(seg, t, st, True, o).start()

        @pl.when(d == r - 1)
        def _():
            for o in range(r - 1):
                rs_desc(seg, t, st, False, o).start()

    def rs_relay(plan, t, seg):
        st = plan.stages[t]
        r, d = st.r, st.d
        for j in range(r - 1):
            o = r - 1 - j

            @pl.when((d > 0) & (d <= o))
            def _(o=o):
                rs_desc(seg, t, st, True, o).wait_recv()
                add_in(seg, st, True, o)

            @pl.when((d > 0) & (d < o))
            def _(o=o):
                rs_desc(seg, t, st, True, o).start()

            @pl.when((d < r - 1) & (d >= j))
            def _(o=j):
                rs_desc(seg, t, st, False, o).wait_recv()
                add_in(seg, st, False, o)

            @pl.when((d < r - 1) & (d > j))
            def _(o=j):
                rs_desc(seg, t, st, False, o).start()

    def ag_first(plan, t, seg):
        st = plan.stages[t]
        r, d = st.r, st.d

        @pl.when(d < r - 1)
        def _():
            ag_desc(seg, t, st, True, d).start()

        @pl.when(d > 0)
        def _():
            ag_desc(seg, t, st, False, d).start()

    def ag_relay(plan, t, seg):
        st = plan.stages[t]
        r, d = st.r, st.d
        for j in range(1, r):

            @pl.when(d >= j)
            def _(j=j):
                ag_desc(seg, t, st, True, d - j).wait_recv()

            @pl.when((d >= j) & (d < r - 1))
            def _(j=j):
                ag_desc(seg, t, st, True, d - j).start()

            @pl.when(d + j <= r - 1)
            def _(j=j):
                ag_desc(seg, t, st, False, d + j).wait_recv()

            @pl.when((d + j <= r - 1) & (d > 0))
            def _(j=j):
                ag_desc(seg, t, st, False, d + j).start()

    def dp_start(segs, which):
        each(segs, lambda s: rs_first(plans[which], 0, s))

    def dp_step(segs, which, k):
        plan = plans[which]
        S = len(plan.stages)

        def one(seg):
            if k < S:
                rs_relay(plan, k, seg)
                if k + 1 < S:
                    rs_first(plan, k + 1, seg)
                else:
                    own = pl.ds(pl.multiple_of(plan.own, 16), plan.own_len)
                    res[seg, own, :] = g[seg, own, :]
                    ag_first(plan, S - 1, seg)
            else:
                t = 2 * S - 1 - k
                ag_relay(plan, t, seg)
                if t > 0:
                    ag_first(plan, t - 1, seg)

        each(segs, one)

    def dp_close(segs, which):
        plan = plans[which]

        def one(seg):
            for t, st in enumerate(plan.stages):
                r, d = st.r, st.d
                for o in range(1, r):

                    @pl.when(d < o)
                    def _(o=o):
                        rs_desc(seg, t, st, True, o).wait_send()

                    @pl.when((d <= o) & (d > 0))
                    def _(o=o):
                        ag_desc(seg, t, st, False, o).wait_send()

                for o in range(r - 1):

                    @pl.when(d > o)
                    def _(o=o):
                        rs_desc(seg, t, st, False, o).wait_send()

                    @pl.when((d >= o) & (d < r - 1))
                    def _(o=o):
                        ag_desc(seg, t, st, True, o).wait_send()

        each(segs, one)

    FA, FB, LA, LB = cfg.segs
    STEPS = 2 * len(cfg.stages)
    outs = []

    def emit(src, dst):
        c = pltpu.make_async_copy(src, dst, R.out_sem.at[len(outs)])
        c.start()
        outs.append(c)

    def emit_seg(j):
        if j < D // TILE:
            emit(g_out(j), R.gwu.at[:, pl.ds(j * TILE, TILE)])
        elif j < cfg.seg_out:
            emit(g_out(j), R.gwi.at[:, pl.ds((j - D // TILE) * TILE, TILE)])
        elif j == cfg.seg_out:
            for i in range(D // TILE):
                emit(res.at[j, pl.ds(i * G, G)], R.gwo.at[:, pl.ds(i * TILE, TILE)])
        else:
            emit(g_out(j), (R.gwq, R.gwk, R.gwv)[j - cfg.seg_qkv])

    def g_out(j):
        return res.at[j]

    def spread(lo, hi, k, m):
        return lo + (hi - lo) * k // m, lo + (hi - lo) * (k + 1) // m

    fill = R.fill[0]
    topk = cfg.K
    accs = M // LANES // 4
    loads.idx.wait()
    for h in range(NH):
        at = R.idxv[h]
        hi = at // LANES
        lo = at - hi * LANES
        fld = lax.rem(hi, 4)
        one = jnp.where(fld == 0, 1, jnp.where(fld == 1, 1 << 8, jnp.where(fld == 2, 1 << 16, 1 << 24)))
        R.lo[...] = lo
        for a in range(accs):
            ok = (at < fill) & (hi >= 4 * a) & (hi < 4 * a + 4)
            R.inc[a] = jnp.where(ok, one, 0)

        def count_block(b, c):
            lane = lax.broadcasted_iota(jnp.int32, (16, T), 0) + b * 16
            got = [jnp.zeros((16, T), jnp.int32) for _ in range(accs)]
            for k in range(topk):
                hit = jnp.broadcast_to(R.lo[pl.ds(k, 1), :], (16, T)) == lane
                for a in range(accs):
                    got[a] = got[a] + jnp.where(hit, jnp.broadcast_to(R.inc[a, pl.ds(k, 1), :], (16, T)), 0)
            for a in range(accs):
                R.cntt[a, pl.ds(pl.multiple_of(b * 16, 16), 16), :] = got[a]
            return c

        lax.fori_loop(0, LANES // 16, count_block, 0)
        for a in range(accs):
            R.cnt[h, a] = R.cntt[a].T

    loads.tok.wait()

    def norm_one(i, c):
        rows = pl.ds(pl.multiple_of(i * 128, 128), 128)
        cen, rstd = row_stats(R.tokv[rows, :].astype(F32))
        R.nrm[rows, :] = (cen * rstd * R.g1[...] + R.s1[...]).astype(BF)
        return c

    lax.fori_loop(0, T // 128, norm_one, 0)
    for copy in (loads.wq, loads.wk, loads.wv):
        copy.wait()
    for rb in range(2):
        rows = pl.ds(rb * HB, HB)
        low = R.nrm[rows, :]
        R.q[rows, :] = nn(low, R.wqkv[:, 0:G]).astype(BF)
        R.kext[pl.ds(T + rb * HB, HB), :] = nn(low, R.wqkv[:, G : 2 * G]).astype(BF)
        R.vext[pl.ds(T + rb * HB, HB), :] = nn(low, R.wqkv[:, 2 * G : W3]).astype(BF)

    band_row = lax.dot_general(
        R.table[...], R.oh[...], (((1,), (0,)), ((), ())), precision=EXACT, preferred_element_type=F32
    )
    u_at = lax.broadcasted_iota(jnp.int32, (NH, KW), 1)
    band_row = jnp.where((u_at >= 1) & (u_at <= T), band_row, NEGATIVE)
    for h in range(NH):
        wide = jnp.broadcast_to(band_row[h : h + 1, :], (HB, KW))
        R.band[h] = pltpu.roll(wide, 0, 1, stride=1, stride_axis=0)

    for j in range(U // LANES):
        R.ibv[:, j * LANES : (j + 1) * LANES] = R.ib[j : j + 1, :].astype(F32)
    mix = jax.nn.sigmoid(R.gate[...])
    pl.semaphore_wait(barrier, want)

    for copy in (loads.ck, loads.cv, loads.mk, loads.mv, loads.wo):
        copy.wait()

    def attend(rb, h):
        rows = pl.ds(rb * HB, HB)
        cols = slice(h * DH, (h + 1) * DH)
        wide = pl.ds(rb * HB, KW)
        q = R.q[rows, cols]
        s = nt(q, R.kext[wide, cols]) * scale + R.band[h]
        e = jnp.exp(s - jnp.max(s, axis=-1, keepdims=True))
        p = (e * (1.0 / jnp.sum(e, axis=-1, keepdims=True))).astype(BF)
        R.pl[h, rows, :] = p
        near = nn(p, R.vext[wide, cols])
        s = nt(q, R.mkv[:, cols]) * scale
        parts = []
        for f in range(M // LANES):
            field = (R.cnt[h, f // 4, rows, :] >> (8 * (f % 4))) & 255
            parts.append(field.astype(F32))
        c = jnp.concatenate(parts, axis=1)
        s = jnp.where(c > 0.0, s, NEGATIVE)
        top = jnp.maximum(jnp.max(s, axis=-1, keepdims=True), 0.0)
        e = jnp.exp(s - top) * c
        total = jnp.exp(-top) + jnp.sum(e, axis=-1, keepdims=True)
        p = (e * (1.0 / total)).astype(BF)
        R.pm[h, rows, :] = p
        far = nn(p, R.mvv[:, cols])
        m = mix[:, h : h + 1]
        R.diff[rows, cols] = far - near
        R.joined[rows, cols] = (m * far + (1.0 - m) * near).astype(BF)

    def project(rb):
        rows = pl.ds(rb * HB, HB)
        for j in range(D // TILE):
            cols = slice(j * TILE, (j + 1) * TILE)
            R.part[0, rows, cols] = nn(R.joined[rows, :], R.wov[:, cols]).astype(BF)

    for h in range(NH):
        attend(0, h)
    project(0)
    push(0, 0)
    for h in range(NH):
        attend(1, h)
        if h == 0:

            @pl.when(is0)
            def _():
                mid(0)

    project(1)
    push(0, 1)

    @pl.when(is1)
    def _():
        mid(0)

    for copy in (loads.og, loads.wu, loads.wi):
        copy.wait()

    def tiles(count, fn):
        lax.fori_loop(0, count, lambda j, c: (fn(pl.ds(pl.multiple_of(j * TILE, TILE), TILE)), c)[1], 0)

    for rb in range(2):
        rows = pl.ds(rb * HB, HB)

        def back_one(cols, rows=rows):
            R.ga[rows, cols] = nt(R.ogv[rows, :], R.wuv[cols, :])

        tiles(U // TILE, back_one)

    own = pl.ds(pl.multiple_of(core * HB, HB), HB)

    def second_norm():
        for k in range(SUBS):
            rows = pl.ds(pl.multiple_of(core * HB + k * sub, sub), sub)
            x = R.tokv[rows, :].astype(F32) + fin(0, k)
            R.resid[pl.ds(k * sub, sub), :] = x
            cen, rstd = row_stats(x)
            R.ntl[rows, :] = (cen * rstd * R.g2[...] + R.s2[...]).astype(BF)
            share_desc(0, k, R.ntl, core).start()

    def feed(rb):
        rows = pl.ds(rb * HB, HB)

        def unit(cols):
            x = nn(R.ntl[rows, :], R.wiv[:, cols]) + R.ibv[:, cols]
            x2 = x * x
            t = jnp.tanh(GELU_A * (x + GELU_B * x * x2))
            R.act[rows, cols] = (0.5 * x * (1.0 + t)).astype(BF)
            slope = 0.5 * (1.0 + t) + 0.5 * x * (1.0 - t * t) * (GELU_A * (1.0 + 3.0 * GELU_B * x2))
            gi = (R.ga[rows, cols] * slope).astype(BF)
            R.gi[rows, cols] = gi
            R.gib[pl.ds(rb, 1), cols] = jnp.sum(gi.astype(F32), axis=0, keepdims=True)

        tiles(U // TILE, unit)

        def back(cols):
            R.part[1, rows, cols] = nt(R.gi[rows, :], R.wiv[cols, :]).astype(BF)

        tiles(D // TILE, back)

    @pl.when(is0)
    def _():
        second_norm()

    @pl.when(is1)
    def _():
        for k in range(SUBS):
            share_desc(0, k, R.ntl, 0).wait_recv()

    feed(0)
    push(1, 0)

    @pl.when(is1)
    def _():
        second_norm()

    @pl.when(is0)
    def _():
        for k in range(SUBS):
            share_desc(0, k, R.ntl, 1).wait_recv()

    feed(1)
    push(1, 1)
    mid(1)

    R.tr[...] = R.act[...].T

    def outer_seg(j, c):
        g[j] = nn(R.tr[...], R.ogv[:, pl.ds(pl.multiple_of(j * TILE, TILE), TILE)]).astype(BF)
        return c

    def inner_seg(j, c):
        g[D // TILE + j] = nn(R.tr[...], R.gi[:, pl.ds(pl.multiple_of(j * TILE, TILE), TILE)]).astype(BF)
        return c

    lax.fori_loop(0, D // TILE, outer_seg, 0)
    outers = D // TILE
    dp_start((0, min(FA[1], outers)), 0)
    dp_start((FB[0], outers), 1)
    R.tr[...] = R.ntl[...].T
    lax.fori_loop(0, U // TILE, inner_seg, 0)
    dp_start((outers, FA[1]), 0)
    dp_start((max(FB[0], outers), FB[1]), 1)

    sent(0)
    for rb in range(2):
        rows = pl.ds(rb * HB, HB)

        def fed(cols, rows=rows):
            R.part[0, rows, cols] = nn(R.act[rows, :], R.wuv[:, cols]).astype(BF)

        tiles(D // TILE, fed)
        push(2, rb)

    sg2 = jnp.zeros((1, D), F32)
    ss2 = jnp.zeros((1, D), F32)
    for k in range(SUBS):
        rows = pl.ds(pl.multiple_of(core * HB + k * sub, sub), sub)
        dy = fin(1, k)
        cen, rstd = row_stats(R.resid[pl.ds(k * sub, sub), :])
        xh = cen * rstd
        sg2 = sg2 + jnp.sum(dy * xh, axis=0, keepdims=True)
        ss2 = ss2 + jnp.sum(dy, axis=0, keepdims=True)
        dx = dy * R.g2[...]
        dx = rstd * (
            dx - jnp.mean(dx, axis=-1, keepdims=True) - xh * jnp.mean(dx * xh, axis=-1, keepdims=True)
        )
        gr = R.ogv[rows, :].astype(F32) + dx
        R.gres[pl.ds(k * sub, sub), :] = gr
        R.gat[rows, :] = gr.astype(BF)
        share_desc(1, k, R.gat, core).start()
    R.small[0, 2:3, :] = sg2
    R.small[0, 3:4, :] = ss2
    mid(2)
    dp_step(spread(*FA, 0, 3), 0, 0)
    for k in range(SUBS):
        share_desc(1, k, R.gat, 1 - core).wait_recv()

    for h in range(NH):
        R.band[h] = jnp.zeros((HB, KW), F32)
    R.gkv[...] = jnp.zeros((2, T, G), F32)
    gate_sums = [jnp.zeros((1, 1), F32) for _ in range(NH)]
    for rb in range(2):
        rows = pl.ds(rb * HB, HB)
        wide = pl.ds(rb * HB, KW)
        gj_all = nt(R.gat[rows, :], R.wov[...])
        own_at = T - rb * HB
        own_rows = pl.ds(0, KW - own_at)
        for h in range(NH):
            cols = slice(h * DH, (h + 1) * DH)
            gj = gj_all[:, cols]
            m = mix[:, h : h + 1]
            gate_sums[h] = gate_sums[h] + jnp.sum(
                jnp.sum(gj * R.diff[rows, cols], axis=0, keepdims=True), axis=1, keepdims=True
            )
            gl = ((1.0 - m) * gj).astype(BF)
            gm = (m * gj).astype(BF)
            kx, vx = R.kext[wide, cols], R.vext[wide, cols]
            low = R.pl[h, rows, :]
            p = low.astype(F32)
            dp = nt(gl, vx)
            ds = p * (dp - jnp.sum(p * dp, axis=-1, keepdims=True))
            R.band[h] += ds
            raw = (ds * scale).astype(BF)
            gq = nn(raw, kx)
            R.gkv[0, own_rows, cols] += tn(raw[:, own_at:], R.q[rows, cols])
            R.gkv[1, own_rows, cols] += tn(low[:, own_at:], gl)
            p = R.pm[h, rows, :].astype(F32)
            dp = nt(gm, R.mvv[:, cols])
            ds = p * (dp - jnp.sum(p * dp, axis=-1, keepdims=True))
            gq = gq + nn((ds * scale).astype(BF), R.mkv[:, cols])
            R.gqkv[rows, cols] = gq.astype(BF)
            spot = (rb * NH + h) * 4 // (2 * NH)
            if spot == 0:
                dp_step(FB, 1, 0)
            elif spot == 1:
                dp_step(spread(*FA, 1, 3), 0, 0)
            elif spot == 2:
                dp_step(spread(*FA, 2, 3), 0, 0)
                dp_step(FB, 1, 1)
            else:
                dp_step(spread(*FA, 0, 2), 0, 1)
    R.gqkv[:, G : 2 * G] = R.gkv[0].astype(BF)
    R.gqkv[:, 2 * G : W3] = R.gkv[1].astype(BF)

    tr = R.tr
    for j in range(D // TILE):
        g[cfg.seg_out, j * G : (j + 1) * G, :] = tn(
            R.joined[...], R.gat[:, j * TILE : (j + 1) * TILE]
        ).astype(BF)
    tr[...] = R.nrm[...].T

    def qkv_seg(j, c):
        g[cfg.seg_qkv + j] = nn(tr[...], R.gqkv[:, pl.ds(pl.multiple_of(j * TILE, TILE), TILE)]).astype(BF)
        return c

    lax.fori_loop(0, W3 // TILE, qkv_seg, 0)
    dp_start(LA, 0)
    dp_start(LB, 1)
    dp_step(spread(*FA, 1, 2), 0, 1)
    sent(1)
    for rb in range(2):
        rows = pl.ds(rb * HB, HB)

        def back_in(cols, rows=rows):
            R.part[1, rows, cols] = nt(R.gqkv[rows, :], R.wqkv[cols, :]).astype(BF)

        tiles(D // TILE, back_in)
        push(3, rb)

    for k in range(2, STEPS - 1):
        dp_step(FB, 1, k)

    for k in range(SUBS):
        rows = pl.ds(pl.multiple_of(core * HB + k * sub, sub), sub)
        R.bo[rows, :] = (R.resid[pl.ds(k * sub, sub), :] + fin(2, k)).astype(BF)
        share_desc(2, k, R.bo, core).start()

    mid(3)
    for k in range(2, STEPS - 1):
        dp_step(FA, 0, k)

    smalls = R.small
    at_row = lax.broadcasted_iota(jnp.int32, (8, KW), 0)
    table_grads = []
    for h in range(NH):
        half = HB
        cur = R.band[h]
        while half > 8:
            half //= 2
            cur = cur[:half] + pltpu.roll(cur[half:], KW - half, 1)
        for bit in (1, 2, 4):
            cur = jnp.where(lax.rem(at_row // bit, 2) == 1, pltpu.roll(cur, KW - bit, 1), cur)
        diag = jnp.sum(cur, axis=0, keepdims=True)
        table_grads.append(
            lax.dot_general(diag, R.oh[...], (((1,), (1,)), ((), ())), precision=EXACT, preferred_element_type=F32)
        )
    smalls[0, 4:5, :] = R.gib[0:1, :] + R.gib[1:2, :]
    smalls[0, 5:8, :] = jnp.zeros((3, D), F32)
    for h in range(NH):
        s = mix[:, h : h + 1]
        smalls[0, 5:6, h * LANES : h * LANES + NB] = table_grads[h]
        smalls[0, 6:7, h * LANES : (h + 1) * LANES] = jnp.broadcast_to(gate_sums[h] * s * (1.0 - s), (1, LANES))

    sg1 = jnp.zeros((1, D), F32)
    ss1 = jnp.zeros((1, D), F32)
    for k in range(SUBS):
        rows = pl.ds(pl.multiple_of(core * HB + k * sub, sub), sub)
        dy = fin(3, k)
        cen, rstd = row_stats(R.tokv[rows, :].astype(F32))
        xh = cen * rstd
        sg1 = sg1 + jnp.sum(dy * xh, axis=0, keepdims=True)
        ss1 = ss1 + jnp.sum(dy, axis=0, keepdims=True)
        dx = dy * R.g1[...]
        dx = rstd * (
            dx - jnp.mean(dx, axis=-1, keepdims=True) - xh * jnp.mean(dx * xh, axis=-1, keepdims=True)
        )
        R.gt[rows, :] = (R.gres[pl.ds(k * sub, sub), :] + dx).astype(BF)
        share_desc(3, k, R.gt, core).start()
    smalls[0, 0:1, :] = sg1
    smalls[0, 1:2, :] = ss1

    def small_desc(i, who):
        return pltpu.make_async_remote_copy(
            src_ref=smalls.at[i],
            dst_ref=R.sbuf.at[i],
            send_sem=R.s_send.at[i],
            recv_sem=R.s_recv.at[i],
            device_id=who,
            device_id_type=pl.DeviceIdType.MESH,
        )

    small_desc(0, mate).start()
    small_desc(0, mate).wait_recv()
    in_norm = lax.broadcasted_iota(jnp.int32, (8, D), 0) < 4
    smalls[1] = smalls[0] + jnp.where(in_norm, R.sbuf[0], 0.0)
    partners = []
    for i, s in enumerate(cfg.doubling):
        b = lax.rem(me // s, 2)
        who = {"dp": me + s - 2 * s * b}
        partners.append(who)
        small_desc(i + 1, who).start()
        small_desc(i + 1, who).wait_recv()
        smalls[i + 2] = smalls[i + 1] + R.sbuf[i + 1]

    for k in range(SUBS):
        share_desc(2, k, R.bo, 1 - core).wait_recv()
        share_desc(3, k, R.gt, 1 - core).wait_recv()
    emit(R.bo, R.block_out)
    emit(R.gt, R.gtok)
    emit(smalls.at[len(partners) + 1], R.gsmall)
    dp_step(LB, 1, 0)
    dp_step(LA, 0, 0)
    dp_step(FB, 1, STEPS - 1)
    for j in range(*FB):
        emit_seg(j)
    dp_step(LB, 1, 1)
    dp_step(LA, 0, 1)
    dp_step(FA, 0, STEPS - 1)
    for j in range(*FA):
        emit_seg(j)
    for k in range(2, STEPS):
        dp_step(LB, 1, k)
        dp_step(LA, 0, k)
    for j in range(LA[0], LB[1]):
        emit_seg(j)

    sent(2)
    sent(3)
    for p in range(4):
        for k in range(SUBS):
            share_desc(p, k, (R.ntl, R.gat, R.bo, R.gt)[p], core).wait_send()
    small_desc(0, mate).wait_send()
    for i, who in enumerate(partners):
        small_desc(i + 1, who).wait_send()
    dp_close(FA, 0)
    dp_close(FB, 1)
    dp_close(LA, 0)
    dp_close(LB, 1)
    for c in outs:
        c.wait()


def local(n, tokens, wq, wk, wv, wo, wi, ib, wu, g1, s1, g2, s2, table, gate, ck, cv, mk, mv, idx, fill, og):
    T, D = tokens.shape
    NH = table.shape[0]
    G = wq.shape[1]
    U = wi.shape[1]
    M = mk.shape[1]
    K = idx.shape[2]
    HB = T // 2
    KW = T + HB
    stages = stage_list(n)
    doubling = []
    s = 1
    while s < n:
        doubling.append(s)
        s *= 2
    ffn = (D + U) // TILE
    late = 1 + 3 * G // TILE
    nseg = ffn + late
    fa, la = 5 * ffn // 8, late // 2
    seg = D
    orders = (stages, stages[::-1])
    rows_needed = 0
    for order in orders:
        off, length = 0, seg
        for _, r in order:
            length //= r
            off += (1 if r == 2 else 2 * (r - 1)) * length
        rows_needed = max(rows_needed, off)
    inputs = dict(
        tok=tokens, idx=idx.transpose(1, 2, 0), wq=wq, wk=wk, wv=wv, wo=wo, wi=wi, wu=wu, ck=ck, cv=cv, mk=mk, mv=mv, og=og
    )
    vectors = dict(
        ib=ib.reshape(U // LANES, LANES), g1=g1.reshape(1, D), s1=s1.reshape(1, D), g2=g2.reshape(1, D), s2=s2.reshape(1, D),
        table=table, gate=gate.reshape(1, NH), oh=jnp.asarray(bucket_rows(T)),
    )
    outputs = dict(
        block_out=((T, D), BF), gtok=((T, D), BF), gwq=((D, G), BF), gwk=((D, G), BF), gwv=((D, G), BF),
        gwo=((G, D), BF), gwi=((D, U), BF), gwu=((U, D), BF), gsmall=((8, D), F32),
    )
    S = len(stages)
    sem = pltpu.SemaphoreType.DMA
    scratch = dict(
        tokv=pltpu.VMEM((T, D), BF), ogv=pltpu.VMEM((T, D), BF), idxv=pltpu.VMEM((NH, K, T), jnp.int32),
        wqkv=pltpu.VMEM((D, 3 * G), BF), wov=pltpu.VMEM((G, D), BF), wiv=pltpu.VMEM((D, U), BF),
        wuv=pltpu.VMEM((U, D), BF), kext=pltpu.VMEM((2 * T, G), BF), vext=pltpu.VMEM((2 * T, G), BF),
        mkv=pltpu.VMEM((M, G), BF), mvv=pltpu.VMEM((M, G), BF),
        lo=pltpu.VMEM((K, T), jnp.int32), inc=pltpu.VMEM((M // LANES // 4, K, T), jnp.int32),
        cntt=pltpu.VMEM((M // LANES // 4, LANES, T), jnp.int32),
        cnt=pltpu.VMEM((NH, M // LANES // 4, T, LANES), jnp.int32),
        nrm=pltpu.VMEM((T, D), BF), q=pltpu.VMEM((T, G), BF), band=pltpu.VMEM((NH, HB, KW), F32),
        pl=pltpu.VMEM((NH, T, KW), BF), pm=pltpu.VMEM((NH, T, M), BF), diff=pltpu.VMEM((T, G), F32),
        joined=pltpu.VMEM((T, G), BF), ga=pltpu.VMEM((T, U), F32), ntl=pltpu.VMEM((T, D), BF),
        resid=pltpu.VMEM((HB, D), F32), act=pltpu.VMEM((T, U), BF), gi=pltpu.VMEM((T, U), BF),
        gib=pltpu.VMEM((8, U), F32), ibv=pltpu.VMEM((1, U), F32), tr=pltpu.VMEM((D, T), BF), gres=pltpu.VMEM((HB, D), F32),
        gat=pltpu.VMEM((T, D), BF), gkv=pltpu.VMEM((2, T, G), F32),
        gqkv=pltpu.VMEM((T, 3 * G), BF), bo=pltpu.VMEM((T, D), BF), gt=pltpu.VMEM((T, D), BF),
        part=pltpu.VMEM((2, T, D), BF), cbuf=pltpu.VMEM((2, HB, D), BF), ybuf=pltpu.VMEM((2, HB, D), BF),
        small=pltpu.VMEM((len(doubling) + 2, 8, D), F32), sbuf=pltpu.VMEM((len(doubling) + 1, 8, D), F32),
        g=pltpu.VMEM((nseg, seg, TILE), BF), res=pltpu.VMEM((nseg, seg, TILE), BF),
        rbuf=pltpu.VMEM((nseg, rows_needed, TILE), BF),
        in_sem=sem((13,)), out_sem=sem((2 + 2 * (D // TILE) + U // TILE + 4,)),
        c_send=sem((4, SUBS)), c_recv=sem((4, SUBS)), y_send=sem((4, SUBS)), y_recv=sem((4, SUBS)),
        a_send=sem((4, SUBS)), a_recv=sem((4, SUBS)),
        s_send=sem((len(doubling) + 1,)), s_recv=sem((len(doubling) + 1,)),
        rs_send=sem((nseg, S, 2, 4)), rs_recv=sem((nseg, S, 2, 4)),
        ag_send=sem((nseg, S, 2, 4)), ag_recv=sem((nseg, S, 2, 4)),
    )
    cfg = Space(
        n=n, T=T, D=D, G=G, U=U, M=M, NH=NH, K=K, stages=stages, doubling=doubling, orders=orders, seg=seg,
        segs=((0, fa), (fa, ffn), (ffn, ffn + la), (ffn + la, nseg)), seg_out=ffn, seg_qkv=ffn + 1,
        names=[*inputs, *vectors, "fill", *outputs, *scratch],
    )
    any_spec = pl.BlockSpec(memory_space=pl.ANY)
    vec_spec = pl.BlockSpec(memory_space=pltpu.VMEM)
    outs = pl.pallas_call(
        functools.partial(kernel, cfg),
        out_shape=[jax.ShapeDtypeStruct(*v) for v in outputs.values()],
        in_specs=[any_spec] * len(inputs) + [vec_spec] * len(vectors) + [pl.BlockSpec(memory_space=pltpu.SMEM)],
        out_specs=[any_spec] * len(outputs),
        scratch_shapes=list(scratch.values()),
        compiler_params=pltpu.CompilerParams(
            collective_id=0, has_side_effects=True, vmem_limit_bytes=63 * MIB
        ),
        cost_estimate=pl.CostEstimate(flops=12 * 10**9, bytes_accessed=20 * 10**6, transcendentals=3 * 10**6),
    )(
        *inputs.values(), *vectors.values(), fill,
    )
    return widen(outs, NH)


def widen_kernel(NH, *refs):
    ins, outs = refs[:9], refs[9:]
    for src, dst in zip(ins[:8], outs[:8]):
        dst[...] = src[...].astype(dst.dtype)

    @pl.when(pl.program_id(0) == 0)
    def _():
        small = ins[8]
        for i in range(5):
            outs[8 + i][...] = small[i : i + 1, :]
        for h in range(NH):
            outs[13][h : h + 1, :] = small[5:6, h * LANES : h * LANES + NB]
            outs[14][:, h : h + 1] = small[6:7, h * LANES : h * LANES + 1]


def widen(sums, NH):
    steps = 8
    small = sums[8]
    D = small.shape[1]

    def split(x):
        return pl.BlockSpec((x.shape[0] // steps, x.shape[1]), lambda i: (i, 0))

    def whole(shape):
        return pl.BlockSpec(shape, lambda i: (0, 0))

    shapes = [jax.ShapeDtypeStruct(x.shape, BF if i < 2 else F32) for i, x in enumerate(sums[:8])]
    tiny = [(1, D)] * 5 + [(NH, NB), (1, NH)]
    got = pl.pallas_call(
        functools.partial(widen_kernel, NH),
        grid=(steps,),
        in_specs=[split(x) for x in sums[:8]] + [whole(small.shape)],
        out_specs=[split(x) for x in sums[:8]] + [whole(x) for x in tiny],
        out_shape=shapes + [jax.ShapeDtypeStruct(x, F32) for x in tiny],
        compiler_params=pltpu.CompilerParams(vmem_limit_bytes=60 * MIB),
        cost_estimate=pl.CostEstimate(flops=0, bytes_accessed=22 * 10**6, transcendentals=0),
    )(*sums)
    block_out, gtok, gwq, gwk, gwv, gwo, gwi, gwu, g1, s1, g2, s2, ib, bias, gates = got
    return (
        block_out, gtok, gwq, gwk, gwv, gwo, gwi, ib.reshape(-1), gwu, g1.reshape(D), s1.reshape(D), g2.reshape(D),
        s2.reshape(D), bias, gates.reshape(NH),
    )


def solution(mesh):
    return jax.shard_map(
        functools.partial(local, mesh.shape["dp"]),
        mesh=mesh,
        in_specs=(
            P("dp", None), P(None, "head"), P(None, "head"), P(None, "head"), P("head", None), P(None, "head"),
            P("head"), P("head", None), P(), P(), P(), P(), P("head", None), P("head"), P("dp", "head"),
            P("dp", "head"), P("dp", None, "head"), P("dp", None, "head"), P("dp", "head", None), P("dp"),
            P("dp", None),
        ),
        out_specs=(
            P("dp", None), P("dp", None), P(None, "head"), P(None, "head"), P(None, "head"), P("head", None),
            P(None, "head"), P("head"), P("head", None), P(), P(), P(), P(), P("head", None), P("head"),
        ),
        check_vma=False,
    )
```

```python
import functools
import math
from types import SimpleNamespace as Space

import jax
import jax.numpy as jnp
import numpy as np
from jax import lax
from jax.experimental import pallas as pl
from jax.experimental.pallas import tpu as pltpu
from jax.sharding import PartitionSpec as P

NB = 32
MAXD = 128
EPSILON = 1e-05
NEGATIVE = -1e30
EXACT = lax.Precision.HIGHEST
BF = jnp.bfloat16
F32 = jnp.float32
LANES = 128
TILE = 256
SUBS = 2
MIB = 1 << 20
GELU_A = math.sqrt(2.0 / math.pi)
GELU_B = 0.044715


def bucket_rows(length):
    span = np.arange(length)
    exact = NB // 2
    ratio = np.log(np.maximum(span, 1) / exact) / np.log(MAXD / exact)
    larger = np.minimum(exact + (ratio * (NB - exact)).astype(np.int32), NB - 1)
    bucket = np.where(span < exact, span, larger).astype(np.int32)
    table = np.zeros((NB, length + length // 2), np.float32)
    for u in range(1, length + 1):
        table[bucket[length - u], u] = 1.0
    return table


def nn(a, b):
    return lax.dot_general(a, b, (((1,), (0,)), ((), ())), preferred_element_type=F32)


def nt(a, b):
    return lax.dot_general(a, b, (((1,), (1,)), ((), ())), preferred_element_type=F32)


def tn(a, b):
    return lax.dot_general(a, b, (((0,), (0,)), ((), ())), preferred_element_type=F32)


def row_stats(x):
    mean = jnp.mean(x, axis=-1, keepdims=True)
    c = x - mean
    var = jnp.mean(c * c, axis=-1, keepdims=True)
    return c, lax.rsqrt(var + EPSILON)


def stage_list(n):
    stages, stride, left = [], 1, n
    if left >= 2:
        stages.append((1, 2))
        stride, left = 2, left // 2
    while left >= 4:
        stages.append((stride, 4))
        stride, left = stride * 4, left // 4
    if left == 2:
        stages.append((stride, 2))
    return stages


def kernel(cfg, *refs):
    n = cfg.n
    R = Space(**dict(zip(cfg.names, refs)))
    T, D, G, U, M, NH = cfg.T, cfg.D, cfg.G, cfg.U, cfg.M, cfg.NH
    DH = G // NH
    HB = T // 2
    KW = T + HB
    scale = 1.0 / math.sqrt(DH)
    me = lax.axis_index("dp")
    hid = lax.axis_index("head")
    core = lax.rem(hid, 2)
    mate = {"head": hid + 1 - 2 * core}
    across = {"head": lax.rem(hid + 2, 4)}
    is0, is1 = core == 0, core == 1
    sub = HB // SUBS

    peers = []
    for stride, r in cfg.stages:
        d = lax.rem(me // stride, r)
        peers.append((d > 0, me - stride))
        peers.append((d < r - 1, me + stride))
    for s in cfg.doubling:
        covered = False
        for stride, r in cfg.stages:
            if s == stride:
                covered = True
        if not covered:
            b = lax.rem(me // s, 2)
            peers.append((True, me + s - 2 * s * b))
    barrier = pltpu.get_barrier_semaphore()
    want = 2
    pl.semaphore_signal(barrier, inc=1, device_id=mate)
    pl.semaphore_signal(barrier, inc=1, device_id=across)
    for cond, who in peers:
        if cond is True:
            pl.semaphore_signal(barrier, inc=1, device_id={"dp": who})
            want = want + 1
        else:

            @pl.when(cond)
            def _(who=who):
                pl.semaphore_signal(barrier, inc=1, device_id={"dp": who})

            want = want + jnp.where(cond, 1, 0).astype(jnp.int32)

    W3 = 3 * G
    loads = Space()

    def load(src, dst, sem):
        copy = pltpu.make_async_copy(src, dst, R.in_sem.at[sem])
        copy.start()
        return copy

    loads.tok = load(R.tok, R.tokv, 0)
    loads.idx = load(R.idx, R.idxv, 1)
    loads.wq = load(R.wq, R.wqkv.at[:, pl.ds(0, G)], 2)
    loads.wk = load(R.wk, R.wqkv.at[:, pl.ds(G, G)], 3)
    loads.wv = load(R.wv, R.wqkv.at[:, pl.ds(2 * G, G)], 4)
    loads.ck = load(R.ck, R.kext.at[pl.ds(0, T)], 5)
    loads.cv = load(R.cv, R.vext.at[pl.ds(0, T)], 6)
    loads.mk = load(R.mk.at[0], R.mkv, 7)
    loads.mv = load(R.mv.at[0], R.mvv, 8)
    loads.wo = load(R.wo, R.wov, 9)
    loads.og = load(R.og, R.ogv, 10)
    loads.wu = load(R.wu, R.wuv, 11)
    loads.wi = load(R.wi, R.wiv, 12)

    def push_desc(p, k):
        return pltpu.make_async_remote_copy(
            src_ref=R.part.at[p % 2, pl.ds(k * sub + (1 - core) * HB, sub)],
            dst_ref=R.cbuf.at[p % 2, pl.ds(k * sub, sub)],
            send_sem=R.c_send.at[p, k],
            recv_sem=R.c_recv.at[p, k],
            device_id=mate,
            device_id_type=pl.DeviceIdType.MESH,
        )

    def cross_desc(p, k):
        return pltpu.make_async_remote_copy(
            src_ref=R.part.at[p % 2, pl.ds(core * HB + k * sub, sub)],
            dst_ref=R.ybuf.at[p % 2, pl.ds(k * sub, sub)],
            send_sem=R.y_send.at[p, k],
            recv_sem=R.y_recv.at[p, k],
            device_id=across,
            device_id_type=pl.DeviceIdType.MESH,
        )

    def share_desc(p, k, buf, cc):
        rows = pl.ds(cc * HB + k * sub, sub)
        return pltpu.make_async_remote_copy(
            src_ref=buf.at[rows],
            dst_ref=buf.at[rows],
            send_sem=R.a_send.at[p, k],
            recv_sem=R.a_recv.at[p, k],
            device_id=mate,
            device_id_type=pl.DeviceIdType.MESH,
        )

    def push(p, rb):
        @pl.when(core != rb)
        def _():
            for k in range(SUBS):
                push_desc(p, k).start()

    def mid(p):
        for k in range(SUBS):
            push_desc(p, k).wait_recv()
            rows = pl.ds(core * HB + k * sub, sub)
            total = R.part[p % 2, rows, :].astype(F32) + R.cbuf[p % 2, pl.ds(k * sub, sub), :].astype(F32)
            R.part[p % 2, rows, :] = total.astype(BF)
            cross_desc(p, k).start()

    def sent(p):
        for k in range(SUBS):
            push_desc(p, k).wait_send()
            cross_desc(p, k).wait_send()

    def fin(p, k):
        cross_desc(p, k).wait_recv()
        rows = pl.ds(core * HB + k * sub, sub)
        return R.part[p % 2, rows, :].astype(F32) + R.ybuf[p % 2, pl.ds(k * sub, sub), :].astype(F32)

    RS_R, RS_S, AG_R, AG_S = R.rs_recv, R.rs_send, R.ag_recv, R.ag_send
    g, res, rbuf = R.g, R.res, R.rbuf
    SEG = cfg.seg

    plans = []
    for order in cfg.orders:
        base, length, off, plan = 0, SEG, 0, []
        for stride, r in order:
            d = lax.rem(me // stride, r)
            length = length // r
            left = off
            right = off if r == 2 else off + (r - 1) * length
            off = right + (r - 1) * length
            plan.append(Space(stride=stride, r=r, d=d, base=base, size=length, left=left, right=right))
            base = base + d * length
        plans.append(Space(stages=plan, own=base, own_len=length))

    def piece(st, o):
        at = st.base + o * st.size
        return pl.ds(at if isinstance(at, int) else pl.multiple_of(at, 16), st.size)

    def hop(st, right):
        return {"dp": me + st.stride if right else me - st.stride}

    def rs_desc(seg, t, st, right, o):
        slot = st.left + (o - 1) * st.size if right else st.right + o * st.size
        return pltpu.make_async_remote_copy(
            src_ref=g.at[seg, piece(st, o)],
            dst_ref=rbuf.at[seg, pl.ds(slot, st.size)],
            send_sem=RS_S.at[seg, t, int(right), o],
            recv_sem=RS_R.at[seg, t, int(right), o],
            device_id=hop(st, right),
            device_id_type=pl.DeviceIdType.MESH,
        )

    def ag_desc(seg, t, st, right, o):
        return pltpu.make_async_remote_copy(
            src_ref=res.at[seg, piece(st, o)],
            dst_ref=res.at[seg, piece(st, o)],
            send_sem=AG_S.at[seg, t, int(right), o],
            recv_sem=AG_R.at[seg, t, int(right), o],
            device_id=hop(st, right),
            device_id_type=pl.DeviceIdType.MESH,
        )

    def add_in(seg, st, right, o):
        slot = st.left + (o - 1) * st.size if right else st.right + o * st.size
        step = min(128, st.size)
        for i in range(st.size // step):
            at = st.base + o * st.size + i * step
            rows = pl.ds(at if isinstance(at, int) else pl.multiple_of(at, 16), step)
            total = g[seg, rows, :].astype(F32) + rbuf[seg, pl.ds(slot + i * step, step), :].astype(F32)
            g[seg, rows, :] = total.astype(BF)

    def each(segs, fn):
        lo, hi = segs
        if hi - lo == 1:
            fn(lo)
        elif hi > lo:
            lax.fori_loop(lo, hi, lambda s, c: (fn(s), c)[1], 0)

    def rs_first(plan, t, seg):
        st = plan.stages[t]
        r, d = st.r, st.d

        @pl.when(d == 0)
        def _():
            for o in range(r - 1, 0, -1):
                rs_desc(seg, t, st, True, o).start()

        @pl.when(d == r - 1)
        def _():
            for o in range(r - 1):
                rs_desc(seg, t, st, False, o).start()

    def take(seg, t, st, right, o, onward):
        rs_desc(seg, t, st, right, o).wait_recv()
        add_in(seg, st, right, o)
        if onward:
            rs_desc(seg, t, st, right, o).start()

    def rs_phase(plan, t, part, seg):
        st = plan.stages[t]
        if st.r == 2:
            work = {0: [(False, 0, False)], 1: [(True, 1, False)]}
        elif part == 0:
            work = {1: [(True, 3, True), (True, 2, True)], 2: [(False, 0, True), (False, 1, True)]}
        elif part == 1:
            work = {1: [(False, 0, True)], 2: [(True, 3, True)]}
        else:
            work = {
                0: [(False, 0, False)], 1: [(True, 1, False), (False, 1, False)],
                2: [(False, 2, False), (True, 2, False)], 3: [(True, 3, False)],
            }
        for at, todo in work.items():

            @pl.when(st.d == at)
            def _(todo=todo):
                for right, o, onward in todo:
                    take(seg, t, st, right, o, onward)

    def ag_first(plan, t, seg):
        st = plan.stages[t]
        r, d = st.r, st.d

        @pl.when(d < r - 1)
        def _():
            ag_desc(seg, t, st, True, d).start()

        @pl.when(d > 0)
        def _():
            ag_desc(seg, t, st, False, d).start()

    def ag_phase(plan, t, part, seg):
        st = plan.stages[t]
        r, d = st.r, st.d
        j = part + 1

        @pl.when(d >= j)
        def _():
            ag_desc(seg, t, st, True, d - j).wait_recv()

        @pl.when((d >= j) & (d < r - 1))
        def _():
            ag_desc(seg, t, st, True, d - j).start()

        @pl.when(d + j <= r - 1)
        def _():
            ag_desc(seg, t, st, False, d + j).wait_recv()

        @pl.when((d + j <= r - 1) & (d > 0))
        def _():
            ag_desc(seg, t, st, False, d + j).start()

    def dp_start(segs, which):
        each(segs, lambda s: rs_first(plans[which], 0, s))

    def dp_phase(segs, which, k):
        plan = plans[which]
        hops = [st.r - 1 for st in plan.stages]
        S = len(hops)
        scatter = [(t, part) for t in range(S) for part in range(hops[t])]
        gather = [(t, part) for t in range(S - 1, -1, -1) for part in range(hops[t])]

        def one(seg):
            if k < len(scatter):
                t, part = scatter[k]
                rs_phase(plan, t, part, seg)
                if part == hops[t] - 1:
                    if t + 1 < S:
                        rs_first(plan, t + 1, seg)
                    else:
                        own = pl.ds(pl.multiple_of(plan.own, 16), plan.own_len)
                        res[seg, own, :] = g[seg, own, :]
                        ag_first(plan, S - 1, seg)
            else:
                t, part = gather[k - len(scatter)]
                ag_phase(plan, t, part, seg)
                if part == hops[t] - 1 and t > 0:
                    ag_first(plan, t - 1, seg)

        each(segs, one)

    PHASES = 2 * sum(r - 1 for _, r in cfg.stages)

    def advance(group, k):
        for i in range(PHASES * (k - 1) // 8, PHASES * k // 8):
            for which in (1, 0):
                dp_phase(group[which], which, i)

    def dp_begin(group):
        for which in (0, 1):
            dp_start(group[which], which)

    def dp_close(segs, which):
        plan = plans[which]

        def one(seg):
            for t, st in enumerate(plan.stages):
                r, d = st.r, st.d
                for o in range(1, r):

                    @pl.when(d < o)
                    def _(o=o):
                        rs_desc(seg, t, st, True, o).wait_send()

                    @pl.when((d <= o) & (d > 0))
                    def _(o=o):
                        ag_desc(seg, t, st, False, o).wait_send()

                for o in range(r - 1):

                    @pl.when(d > o)
                    def _(o=o):
                        rs_desc(seg, t, st, False, o).wait_send()

                    @pl.when((d >= o) & (d < r - 1))
                    def _(o=o):
                        ag_desc(seg, t, st, True, o).wait_send()

        each(segs, one)

    G1, G2, G3 = cfg.groups
    outs = []

    def emit(src, dst):
        c = pltpu.make_async_copy(src, dst, R.out_sem.at[len(outs)])
        c.start()
        outs.append(c)

    def emit_seg(j):
        if j < D // TILE:
            emit(g_out(j), R.gwu.at[:, pl.ds(j * TILE, TILE)])
        elif j < cfg.seg_out:
            emit(g_out(j), R.gwi.at[:, pl.ds((j - D // TILE) * TILE, TILE)])
        elif j == cfg.seg_out:
            for i in range(D // TILE):
                emit(res.at[j, pl.ds(i * G, G)], R.gwo.at[:, pl.ds(i * TILE, TILE)])
        else:
            emit(g_out(j), (R.gwq, R.gwk, R.gwv)[j - cfg.seg_qkv])

    def g_out(j):
        return res.at[j]

    def emit_group(group):
        for j in range(group[0][0], group[1][1]):
            emit_seg(j)

    fill = R.fill[0]
    topk = cfg.K
    accs = M // LANES // 4
    loads.idx.wait()
    for h in range(NH):
        at = R.idxv[h]
        hi = at // LANES
        lo = at - hi * LANES
        fld = lax.rem(hi, 4)
        one = jnp.where(fld == 0, 1, jnp.where(fld == 1, 1 << 8, jnp.where(fld == 2, 1 << 16, 1 << 24)))
        R.lo[...] = lo
        for a in range(accs):
            ok = (at < fill) & (hi >= 4 * a) & (hi < 4 * a + 4)
            R.inc[a] = jnp.where(ok, one, 0)

        def count_block(b, c):
            lane = lax.broadcasted_iota(jnp.int32, (16, T), 0) + b * 16
            got = [jnp.zeros((16, T), jnp.int32) for _ in range(accs)]
            for k in range(topk):
                hit = jnp.broadcast_to(R.lo[pl.ds(k, 1), :], (16, T)) == lane
                for a in range(accs):
                    got[a] = got[a] + jnp.where(hit, jnp.broadcast_to(R.inc[a, pl.ds(k, 1), :], (16, T)), 0)
            for a in range(accs):
                R.cntt[a, pl.ds(pl.multiple_of(b * 16, 16), 16), :] = got[a]
            return c

        lax.fori_loop(0, LANES // 16, count_block, 0)
        for a in range(accs):
            R.cnt[h, a] = R.cntt[a].T

    loads.tok.wait()

    def norm_one(i, c):
        rows = pl.ds(pl.multiple_of(i * 128, 128), 128)
        cen, rstd = row_stats(R.tokv[rows, :].astype(F32))
        R.nrm[rows, :] = (cen * rstd * R.g1[...] + R.s1[...]).astype(BF)
        return c

    lax.fori_loop(0, T // 128, norm_one, 0)
    for copy in (loads.wq, loads.wk, loads.wv):
        copy.wait()
    for rb in range(2):
        rows = pl.ds(rb * HB, HB)
        low = R.nrm[rows, :]
        R.q[rows, :] = nn(low, R.wqkv[:, 0:G]).astype(BF)
        R.kext[pl.ds(T + rb * HB, HB), :] = nn(low, R.wqkv[:, G : 2 * G]).astype(BF)
        R.vext[pl.ds(T + rb * HB, HB), :] = nn(low, R.wqkv[:, 2 * G : W3]).astype(BF)

    band_row = lax.dot_general(
        R.table[...], R.oh[...], (((1,), (0,)), ((), ())), precision=EXACT, preferred_element_type=F32
    )
    u_at = lax.broadcasted_iota(jnp.int32, (NH, KW), 1)
    band_row = jnp.where((u_at >= 1) & (u_at <= T), band_row, NEGATIVE)
    for h in range(NH):
        wide = jnp.broadcast_to(band_row[h : h + 1, :], (HB, KW))
        R.band[h] = pltpu.roll(wide, 0, 1, stride=1, stride_axis=0)

    for j in range(U // LANES):
        R.ibv[:, j * LANES : (j + 1) * LANES] = R.ib[j : j + 1, :].astype(F32)
    mix = jax.nn.sigmoid(R.gate[...])
    pl.semaphore_wait(barrier, want)

    for copy in (loads.ck, loads.cv, loads.mk, loads.mv, loads.wo):
        copy.wait()

    def attend(rb, h):
        rows = pl.ds(rb * HB, HB)
        cols = slice(h * DH, (h + 1) * DH)
        wide = pl.ds(rb * HB, KW)
        q = R.q[rows, cols]
        s = nt(q, R.kext[wide, cols]) * scale + R.band[h]
        e = jnp.exp(s - jnp.max(s, axis=-1, keepdims=True))
        p = (e * (1.0 / jnp.sum(e, axis=-1, keepdims=True))).astype(BF)
        R.pl[h, rows, :] = p
        near = nn(p, R.vext[wide, cols])
        s = nt(q, R.mkv[:, cols]) * scale
        parts = []
        for f in range(M // LANES):
            field = (R.cnt[h, f // 4, rows, :] >> (8 * (f % 4))) & 255
            parts.append(field.astype(F32))
        c = jnp.concatenate(parts, axis=1)
        s = jnp.where(c > 0.0, s, NEGATIVE)
        top = jnp.maximum(jnp.max(s, axis=-1, keepdims=True), 0.0)
        e = jnp.exp(s - top) * c
        total = jnp.exp(-top) + jnp.sum(e, axis=-1, keepdims=True)
        p = (e * (1.0 / total)).astype(BF)
        R.pm[h, rows, :] = p
        far = nn(p, R.mvv[:, cols])
        m = mix[:, h : h + 1]
        R.diff[rows, cols] = far - near
        R.joined[rows, cols] = (m * far + (1.0 - m) * near).astype(BF)

    def project(rb):
        rows = pl.ds(rb * HB, HB)
        for j in range(D // TILE):
            cols = slice(j * TILE, (j + 1) * TILE)
            R.part[0, rows, cols] = nn(R.joined[rows, :], R.wov[:, cols]).astype(BF)

    for h in range(NH):
        attend(0, h)
    project(0)
    push(0, 0)
    for h in range(NH):
        attend(1, h)
        if h == 0:

            @pl.when(is0)
            def _():
                mid(0)

    project(1)
    push(0, 1)

    @pl.when(is1)
    def _():
        mid(0)

    for copy in (loads.og, loads.wu, loads.wi):
        copy.wait()

    def tiles(count, fn):
        lax.fori_loop(0, count, lambda j, c: (fn(pl.ds(pl.multiple_of(j * TILE, TILE), TILE)), c)[1], 0)

    for rb in range(2):
        rows = pl.ds(rb * HB, HB)

        def back_one(cols, rows=rows):
            R.ga[rows, cols] = nt(R.ogv[rows, :], R.wuv[cols, :])

        tiles(U // TILE, back_one)

    own = pl.ds(pl.multiple_of(core * HB, HB), HB)

    def second_norm():
        for k in range(SUBS):
            rows = pl.ds(pl.multiple_of(core * HB + k * sub, sub), sub)
            x = R.tokv[rows, :].astype(F32) + fin(0, k)
            R.resid[pl.ds(k * sub, sub), :] = x
            cen, rstd = row_stats(x)
            R.ntl[rows, :] = (cen * rstd * R.g2[...] + R.s2[...]).astype(BF)
            share_desc(0, k, R.ntl, core).start()

    def feed(rb):
        rows = pl.ds(rb * HB, HB)

        def unit(cols):
            x = nn(R.ntl[rows, :], R.wiv[:, cols]) + R.ibv[:, cols]
            x2 = x * x
            t = jnp.tanh(GELU_A * (x + GELU_B * x * x2))
            R.act[rows, cols] = (0.5 * x * (1.0 + t)).astype(BF)
            slope = 0.5 * (1.0 + t) + 0.5 * x * (1.0 - t * t) * (GELU_A * (1.0 + 3.0 * GELU_B * x2))
            gi = (R.ga[rows, cols] * slope).astype(BF)
            R.gi[rows, cols] = gi
            R.gib[pl.ds(rb, 1), cols] = jnp.sum(gi.astype(F32), axis=0, keepdims=True)

        tiles(U // TILE, unit)

        def back(cols):
            R.part[1, rows, cols] = nt(R.gi[rows, :], R.wiv[cols, :]).astype(BF)

        tiles(D // TILE, back)

    @pl.when(is0)
    def _():
        second_norm()

    @pl.when(is1)
    def _():
        for k in range(SUBS):
            share_desc(0, k, R.ntl, 0).wait_recv()

    feed(0)
    push(1, 0)

    @pl.when(is1)
    def _():
        second_norm()

    @pl.when(is0)
    def _():
        for k in range(SUBS):
            share_desc(0, k, R.ntl, 1).wait_recv()

    feed(1)
    push(1, 1)
    mid(1)

    R.tr[...] = R.act[...].T

    def outer_seg(j, c):
        g[j] = nn(R.tr[...], R.ogv[:, pl.ds(pl.multiple_of(j * TILE, TILE), TILE)]).astype(BF)
        return c

    def inner_seg(j, c):
        g[D // TILE + j] = nn(R.tr[...], R.gi[:, pl.ds(pl.multiple_of(j * TILE, TILE), TILE)]).astype(BF)
        return c

    lax.fori_loop(0, D // TILE, outer_seg, 0)
    dp_begin(G1)
    R.tr[...] = R.ntl[...].T
    lax.fori_loop(0, U // TILE, inner_seg, 0)
    dp_begin(G2)

    sent(0)
    for rb in range(2):
        rows = pl.ds(rb * HB, HB)

        def fed(cols, rows=rows):
            R.part[0, rows, cols] = nn(R.act[rows, :], R.wuv[:, cols]).astype(BF)

        tiles(D // TILE, fed)
        push(2, rb)

    sg2 = jnp.zeros((1, D), F32)
    ss2 = jnp.zeros((1, D), F32)
    for k in range(SUBS):
        rows = pl.ds(pl.multiple_of(core * HB + k * sub, sub), sub)
        dy = fin(1, k)
        cen, rstd = row_stats(R.resid[pl.ds(k * sub, sub), :])
        xh = cen * rstd
        sg2 = sg2 + jnp.sum(dy * xh, axis=0, keepdims=True)
        ss2 = ss2 + jnp.sum(dy, axis=0, keepdims=True)
        dx = dy * R.g2[...]
        dx = rstd * (
            dx - jnp.mean(dx, axis=-1, keepdims=True) - xh * jnp.mean(dx * xh, axis=-1, keepdims=True)
        )
        gr = R.ogv[rows, :].astype(F32) + dx
        R.gres[pl.ds(k * sub, sub), :] = gr
        R.gat[rows, :] = gr.astype(BF)
        share_desc(1, k, R.gat, core).start()
    R.small[0, 2:3, :] = sg2
    R.small[0, 3:4, :] = ss2
    mid(2)
    advance(G1, 1)
    for k in range(SUBS):
        share_desc(1, k, R.gat, 1 - core).wait_recv()

    for h in range(NH):
        R.band[h] = jnp.zeros((HB, KW), F32)
    R.gkv[...] = jnp.zeros((2, T, G), F32)
    gate_sums = [jnp.zeros((1, 1), F32) for _ in range(NH)]
    for rb in range(2):
        rows = pl.ds(rb * HB, HB)
        wide = pl.ds(rb * HB, KW)
        gj_all = nt(R.gat[rows, :], R.wov[...])
        own_at = T - rb * HB
        own_rows = pl.ds(0, KW - own_at)
        for h in range(NH):
            cols = slice(h * DH, (h + 1) * DH)
            gj = gj_all[:, cols]
            m = mix[:, h : h + 1]
            gate_sums[h] = gate_sums[h] + jnp.sum(
                jnp.sum(gj * R.diff[rows, cols], axis=0, keepdims=True), axis=1, keepdims=True
            )
            gl = ((1.0 - m) * gj).astype(BF)
            gm = (m * gj).astype(BF)
            kx, vx = R.kext[wide, cols], R.vext[wide, cols]
            low = R.pl[h, rows, :]
            p = low.astype(F32)
            dp = nt(gl, vx)
            ds = p * (dp - jnp.sum(p * dp, axis=-1, keepdims=True))
            R.band[h] += ds
            raw = (ds * scale).astype(BF)
            gq = nn(raw, kx)
            R.gkv[0, own_rows, cols] += tn(raw[:, own_at:], R.q[rows, cols])
            R.gkv[1, own_rows, cols] += tn(low[:, own_at:], gl)
            p = R.pm[h, rows, :].astype(F32)
            dp = nt(gm, R.mvv[:, cols])
            ds = p * (dp - jnp.sum(p * dp, axis=-1, keepdims=True))
            gq = gq + nn((ds * scale).astype(BF), R.mkv[:, cols])
            R.gqkv[rows, cols] = gq.astype(BF)
            spot = (rb * NH + h) * 4 // (2 * NH)
            advance(G1, spot + 2)
            advance(G2, spot + 1)
    R.gqkv[:, G : 2 * G] = R.gkv[0].astype(BF)
    R.gqkv[:, 2 * G : W3] = R.gkv[1].astype(BF)

    tr = R.tr
    for j in range(D // TILE):
        g[cfg.seg_out, j * G : (j + 1) * G, :] = tn(
            R.joined[...], R.gat[:, j * TILE : (j + 1) * TILE]
        ).astype(BF)
    tr[...] = R.nrm[...].T

    def qkv_seg(j, c):
        g[cfg.seg_qkv + j] = nn(tr[...], R.gqkv[:, pl.ds(pl.multiple_of(j * TILE, TILE), TILE)]).astype(BF)
        return c

    lax.fori_loop(0, W3 // TILE, qkv_seg, 0)
    dp_begin(G3)
    advance(G1, 6)
    advance(G2, 5)
    sent(1)
    for rb in range(2):
        rows = pl.ds(rb * HB, HB)

        def back_in(cols, rows=rows):
            R.part[1, rows, cols] = nt(R.gqkv[rows, :], R.wqkv[cols, :]).astype(BF)

        tiles(D // TILE, back_in)
        push(3, rb)

    advance(G1, 7)
    advance(G2, 6)
    advance(G3, 1)

    for k in range(SUBS):
        rows = pl.ds(pl.multiple_of(core * HB + k * sub, sub), sub)
        R.bo[rows, :] = (R.resid[pl.ds(k * sub, sub), :] + fin(2, k)).astype(BF)
        share_desc(2, k, R.bo, core).start()

    mid(3)
    advance(G1, 8)
    emit_group(G1)
    advance(G2, 7)
    advance(G3, 2)

    smalls = R.small
    at_row = lax.broadcasted_iota(jnp.int32, (8, KW), 0)
    table_grads = []
    for h in range(NH):
        half = HB
        cur = R.band[h]
        while half > 8:
            half //= 2
            cur = cur[:half] + pltpu.roll(cur[half:], KW - half, 1)
        for bit in (1, 2, 4):
            cur = jnp.where(lax.rem(at_row // bit, 2) == 1, pltpu.roll(cur, KW - bit, 1), cur)
        diag = jnp.sum(cur, axis=0, keepdims=True)
        table_grads.append(
            lax.dot_general(diag, R.oh[...], (((1,), (1,)), ((), ())), precision=EXACT, preferred_element_type=F32)
        )
    smalls[0, 4:5, :] = R.gib[0:1, :] + R.gib[1:2, :]
    smalls[0, 5:8, :] = jnp.zeros((3, D), F32)
    for h in range(NH):
        s = mix[:, h : h + 1]
        smalls[0, 5:6, h * LANES : h * LANES + NB] = table_grads[h]
        smalls[0, 6:7, h * LANES : (h + 1) * LANES] = jnp.broadcast_to(gate_sums[h] * s * (1.0 - s), (1, LANES))

    sg1 = jnp.zeros((1, D), F32)
    ss1 = jnp.zeros((1, D), F32)
    for k in range(SUBS):
        rows = pl.ds(pl.multiple_of(core * HB + k * sub, sub), sub)
        dy = fin(3, k)
        cen, rstd = row_stats(R.tokv[rows, :].astype(F32))
        xh = cen * rstd
        sg1 = sg1 + jnp.sum(dy * xh, axis=0, keepdims=True)
        ss1 = ss1 + jnp.sum(dy, axis=0, keepdims=True)
        dx = dy * R.g1[...]
        dx = rstd * (
            dx - jnp.mean(dx, axis=-1, keepdims=True) - xh * jnp.mean(dx * xh, axis=-1, keepdims=True)
        )
        R.gt[rows, :] = (R.gres[pl.ds(k * sub, sub), :] + dx).astype(BF)
        share_desc(3, k, R.gt, core).start()
    smalls[0, 0:1, :] = sg1
    smalls[0, 1:2, :] = ss1

    def small_desc(i, who):
        return pltpu.make_async_remote_copy(
            src_ref=smalls.at[i],
            dst_ref=R.sbuf.at[i],
            send_sem=R.s_send.at[i],
            recv_sem=R.s_recv.at[i],
            device_id=who,
            device_id_type=pl.DeviceIdType.MESH,
        )

    small_desc(0, mate).start()
    small_desc(0, mate).wait_recv()
    in_norm = lax.broadcasted_iota(jnp.int32, (8, D), 0) < 4
    smalls[1] = smalls[0] + jnp.where(in_norm, R.sbuf[0], 0.0)
    partners = []
    for i, s in enumerate(cfg.doubling):
        b = lax.rem(me // s, 2)
        who = {"dp": me + s - 2 * s * b}
        partners.append(who)
        small_desc(i + 1, who).start()
        small_desc(i + 1, who).wait_recv()
        smalls[i + 2] = smalls[i + 1] + R.sbuf[i + 1]

    for k in range(SUBS):
        share_desc(2, k, R.bo, 1 - core).wait_recv()
        share_desc(3, k, R.gt, 1 - core).wait_recv()
    emit(R.bo, R.block_out)
    emit(R.gt, R.gtok)
    emit(smalls.at[len(partners) + 1], R.gsmall)
    advance(G3, 3)
    advance(G2, 8)
    emit_group(G2)
    for k in range(4, 9):
        advance(G3, k)
    emit_group(G3)

    sent(2)
    sent(3)
    for p in range(4):
        for k in range(SUBS):
            share_desc(p, k, (R.ntl, R.gat, R.bo, R.gt)[p], core).wait_send()
    small_desc(0, mate).wait_send()
    for i, who in enumerate(partners):
        small_desc(i + 1, who).wait_send()
    for group in cfg.groups:
        for which in (0, 1):
            dp_close(group[which], which)
    for c in outs:
        c.wait()


def local(n, tokens, wq, wk, wv, wo, wi, ib, wu, g1, s1, g2, s2, table, gate, ck, cv, mk, mv, idx, fill, og):
    T, D = tokens.shape
    NH = table.shape[0]
    G = wq.shape[1]
    U = wi.shape[1]
    M = mk.shape[1]
    K = idx.shape[2]
    HB = T // 2
    KW = T + HB
    stages = stage_list(n)
    doubling = []
    s = 1
    while s < n:
        doubling.append(s)
        s *= 2
    ffn = (D + U) // TILE
    late = 1 + 3 * G // TILE
    nseg = ffn + late
    groups = []
    for lo, count in ((0, D // TILE), (D // TILE, U // TILE), (ffn, late)):
        cut = lo + count // 2
        groups.append(((lo, cut), (cut, lo + count)))
    seg = D
    orders = (stages, stages[::-1])
    rows_needed = 0
    for order in orders:
        off, length = 0, seg
        for _, r in order:
            length //= r
            off += (1 if r == 2 else 2 * (r - 1)) * length
        rows_needed = max(rows_needed, off)
    inputs = dict(
        tok=tokens, idx=idx.transpose(1, 2, 0), wq=wq, wk=wk, wv=wv, wo=wo, wi=wi, wu=wu, ck=ck, cv=cv, mk=mk, mv=mv, og=og
    )
    vectors = dict(
        ib=ib.reshape(U // LANES, LANES), g1=g1.reshape(1, D), s1=s1.reshape(1, D), g2=g2.reshape(1, D), s2=s2.reshape(1, D),
        table=table, gate=gate.reshape(1, NH), oh=jnp.asarray(bucket_rows(T)),
    )
    outputs = dict(
        block_out=((T, D), BF), gtok=((T, D), BF), gwq=((D, G), BF), gwk=((D, G), BF), gwv=((D, G), BF),
        gwo=((G, D), BF), gwi=((D, U), BF), gwu=((U, D), BF), gsmall=((8, D), F32),
    )
    S = len(stages)
    sem = pltpu.SemaphoreType.DMA
    scratch = dict(
        tokv=pltpu.VMEM((T, D), BF), ogv=pltpu.VMEM((T, D), BF), idxv=pltpu.VMEM((NH, K, T), jnp.int32),
        wqkv=pltpu.VMEM((D, 3 * G), BF), wov=pltpu.VMEM((G, D), BF), wiv=pltpu.VMEM((D, U), BF),
        wuv=pltpu.VMEM((U, D), BF), kext=pltpu.VMEM((2 * T, G), BF), vext=pltpu.VMEM((2 * T, G), BF),
        mkv=pltpu.VMEM((M, G), BF), mvv=pltpu.VMEM((M, G), BF),
        lo=pltpu.VMEM((K, T), jnp.int32), inc=pltpu.VMEM((M // LANES // 4, K, T), jnp.int32),
        cntt=pltpu.VMEM((M // LANES // 4, LANES, T), jnp.int32),
        cnt=pltpu.VMEM((NH, M // LANES // 4, T, LANES), jnp.int32),
        nrm=pltpu.VMEM((T, D), BF), q=pltpu.VMEM((T, G), BF), band=pltpu.VMEM((NH, HB, KW), F32),
        pl=pltpu.VMEM((NH, T, KW), BF), pm=pltpu.VMEM((NH, T, M), BF), diff=pltpu.VMEM((T, G), F32),
        joined=pltpu.VMEM((T, G), BF), ga=pltpu.VMEM((T, U), F32), ntl=pltpu.VMEM((T, D), BF),
        resid=pltpu.VMEM((HB, D), F32), act=pltpu.VMEM((T, U), BF), gi=pltpu.VMEM((T, U), BF),
        gib=pltpu.VMEM((8, U), F32), ibv=pltpu.VMEM((1, U), F32), tr=pltpu.VMEM((D, T), BF), gres=pltpu.VMEM((HB, D), F32),
        gat=pltpu.VMEM((T, D), BF), gkv=pltpu.VMEM((2, T, G), F32),
        gqkv=pltpu.VMEM((T, 3 * G), BF), bo=pltpu.VMEM((T, D), BF), gt=pltpu.VMEM((T, D), BF),
        part=pltpu.VMEM((2, T, D), BF), cbuf=pltpu.VMEM((2, HB, D), BF), ybuf=pltpu.VMEM((2, HB, D), BF),
        small=pltpu.VMEM((len(doubling) + 2, 8, D), F32), sbuf=pltpu.VMEM((len(doubling) + 1, 8, D), F32),
        g=pltpu.VMEM((nseg, seg, TILE), BF), res=pltpu.VMEM((nseg, seg, TILE), BF),
        rbuf=pltpu.VMEM((nseg, rows_needed, TILE), BF),
        in_sem=sem((13,)), out_sem=sem((2 + 2 * (D // TILE) + U // TILE + 4,)),
        c_send=sem((4, SUBS)), c_recv=sem((4, SUBS)), y_send=sem((4, SUBS)), y_recv=sem((4, SUBS)),
        a_send=sem((4, SUBS)), a_recv=sem((4, SUBS)),
        s_send=sem((len(doubling) + 1,)), s_recv=sem((len(doubling) + 1,)),
        rs_send=sem((nseg, S, 2, 4)), rs_recv=sem((nseg, S, 2, 4)),
        ag_send=sem((nseg, S, 2, 4)), ag_recv=sem((nseg, S, 2, 4)),
    )
    cfg = Space(
        n=n, T=T, D=D, G=G, U=U, M=M, NH=NH, K=K, stages=stages, doubling=doubling, seg=seg, orders=orders,
        groups=groups, seg_out=ffn, seg_qkv=ffn + 1,
        names=[*inputs, *vectors, "fill", *outputs, *scratch],
    )
    any_spec = pl.BlockSpec(memory_space=pl.ANY)
    vec_spec = pl.BlockSpec(memory_space=pltpu.VMEM)
    outs = pl.pallas_call(
        functools.partial(kernel, cfg),
        out_shape=[jax.ShapeDtypeStruct(*v) for v in outputs.values()],
        in_specs=[any_spec] * len(inputs) + [vec_spec] * len(vectors) + [pl.BlockSpec(memory_space=pltpu.SMEM)],
        out_specs=[any_spec] * len(outputs),
        scratch_shapes=list(scratch.values()),
        compiler_params=pltpu.CompilerParams(
            collective_id=0, has_side_effects=True, vmem_limit_bytes=63 * MIB
        ),
        cost_estimate=pl.CostEstimate(flops=12 * 10**9, bytes_accessed=20 * 10**6, transcendentals=3 * 10**6),
    )(
        *inputs.values(), *vectors.values(), fill,
    )
    return widen(outs, NH)


def widen_kernel(NH, *refs):
    ins, outs = refs[:9], refs[9:]
    for src, dst in zip(ins[:8], outs[:8]):
        dst[...] = src[...].astype(dst.dtype)

    @pl.when(pl.program_id(0) == 0)
    def _():
        small = ins[8]
        for i in range(5):
            outs[8 + i][...] = small[i : i + 1, :]
        for h in range(NH):
            outs[13][h : h + 1, :] = small[5:6, h * LANES : h * LANES + NB]
            outs[14][:, h : h + 1] = small[6:7, h * LANES : h * LANES + 1]


def widen(sums, NH):
    steps = 8
    small = sums[8]
    D = small.shape[1]

    def split(x):
        return pl.BlockSpec((x.shape[0] // steps, x.shape[1]), lambda i: (i, 0))

    def whole(shape):
        return pl.BlockSpec(shape, lambda i: (0, 0))

    shapes = [jax.ShapeDtypeStruct(x.shape, BF if i < 2 else F32) for i, x in enumerate(sums[:8])]
    tiny = [(1, D)] * 5 + [(NH, NB), (1, NH)]
    got = pl.pallas_call(
        functools.partial(widen_kernel, NH),
        grid=(steps,),
        in_specs=[split(x) for x in sums[:8]] + [whole(small.shape)],
        out_specs=[split(x) for x in sums[:8]] + [whole(x) for x in tiny],
        out_shape=shapes + [jax.ShapeDtypeStruct(x, F32) for x in tiny],
        compiler_params=pltpu.CompilerParams(vmem_limit_bytes=60 * MIB),
        cost_estimate=pl.CostEstimate(flops=0, bytes_accessed=22 * 10**6, transcendentals=0),
    )(*sums)
    block_out, gtok, gwq, gwk, gwv, gwo, gwi, gwu, g1, s1, g2, s2, ib, bias, gates = got
    return (
        block_out, gtok, gwq, gwk, gwv, gwo, gwi, ib.reshape(-1), gwu, g1.reshape(D), s1.reshape(D), g2.reshape(D),
        s2.reshape(D), bias, gates.reshape(NH),
    )


def solution(mesh):
    return jax.shard_map(
        functools.partial(local, mesh.shape["dp"]),
        mesh=mesh,
        in_specs=(
            P("dp", None), P(None, "head"), P(None, "head"), P(None, "head"), P("head", None), P(None, "head"),
            P("head"), P("head", None), P(), P(), P(), P(), P("head", None), P("head"), P("dp", "head"),
            P("dp", "head"), P("dp", None, "head"), P("dp", None, "head"), P("dp", "head", None), P("dp"),
            P("dp", None),
        ),
        out_specs=(
            P("dp", None), P("dp", None), P(None, "head"), P(None, "head"), P(None, "head"), P("head", None),
            P(None, "head"), P("head"), P("head", None), P(), P(), P(), P(), P("head", None), P("head"),
        ),
        check_vma=False,
    )
```

```python
import functools
import math
from types import SimpleNamespace as Space

import jax
import jax.numpy as jnp
import numpy as np
from jax import lax
from jax.experimental import pallas as pl
from jax.experimental.pallas import tpu as pltpu
from jax.sharding import PartitionSpec as P

NB = 32
MAXD = 128
EPSILON = 1e-05
NEGATIVE = -1e30
EXACT = lax.Precision.HIGHEST
BF = jnp.bfloat16
F32 = jnp.float32
LANES = 128
TILE = 256
HALVES = 2
CHUNK = 32
MIB = 1 << 20
SMALL = -1
SCHEDULE = (
    (5, 0, 1), (7, 0, 2), (7, 1, 1), (7, 0, 3), (9, 1, 2), (9, 0, 4), (9, 2, 1), (9, 1, 3), (9, 0, 5), (10, 2, 2),
    (10, 1, 4), (11, 2, 3), (13, 0, 6), (14, 0, 7), (14, 2, 4), (14, 1, 5), (15, 3, 1), (15, 3, 2), (15, 2, 5), (15, 1, 6),
    (16, 3, 3), (16, 0, 8), (16, 3, 4), (16, SMALL, 0), (16, 1, 7), (16, 2, 6), (16, SMALL, 0), (17, 2, 7), (17, 3, 5),
    (17, SMALL, 0), (17, 1, 8), (17, 2, 8), (17, SMALL, 0), (17, 3, 6), (17, 3, 7), (17, 3, 8),
)
GELU_A = math.sqrt(2.0 / math.pi)
GELU_B = 0.044715


def bucket_rows(length):
    span = np.arange(length)
    exact = NB // 2
    ratio = np.log(np.maximum(span, 1) / exact) / np.log(MAXD / exact)
    larger = np.minimum(exact + (ratio * (NB - exact)).astype(np.int32), NB - 1)
    bucket = np.where(span < exact, span, larger).astype(np.int32)
    table = np.zeros((NB, length + length // 2), np.float32)
    for u in range(1, length + 1):
        table[bucket[length - u], u] = 1.0
    return table


def nn(a, b):
    return lax.dot_general(a, b, (((1,), (0,)), ((), ())), preferred_element_type=F32)


def nt(a, b):
    return lax.dot_general(a, b, (((1,), (1,)), ((), ())), preferred_element_type=F32)


def tn(a, b):
    return lax.dot_general(a, b, (((0,), (0,)), ((), ())), preferred_element_type=F32)


def row_stats(x):
    mean = jnp.mean(x, axis=-1, keepdims=True)
    c = x - mean
    var = jnp.mean(c * c, axis=-1, keepdims=True)
    return c, lax.rsqrt(var + EPSILON)


def stage_list(n):
    stages, stride, left = [], 1, n
    if left >= 2:
        stages.append((1, 2))
        stride, left = 2, left // 2
    while left >= 4:
        stages.append((stride, 4))
        stride, left = stride * 4, left // 4
    if left == 2:
        stages.append((stride, 2))
    return stages


def kernel(cfg, *refs):
    n = cfg.n
    R = Space(**dict(zip(cfg.names, refs)))
    T, D, G, U, M, NH = cfg.T, cfg.D, cfg.G, cfg.U, cfg.M, cfg.NH
    DH = G // NH
    HB = T // 2
    KW = T + HB
    scale = 1.0 / math.sqrt(DH)
    me = lax.axis_index("dp")
    hid = lax.axis_index("head")
    core = lax.rem(hid, 2)
    mate = {"head": hid + 1 - 2 * core}
    across = {"head": lax.rem(hid + 2, 4)}
    sub = HB // 2

    peers = []
    for stride, r in cfg.stages:
        d = lax.rem(me // stride, r)
        peers.append((d > 0, me - stride))
        peers.append((d < r - 1, me + stride))
    for s in cfg.doubling:
        covered = False
        for stride, r in cfg.stages:
            if s == stride:
                covered = True
        if not covered:
            b = lax.rem(me // s, 2)
            peers.append((True, me + s - 2 * s * b))
    barrier = pltpu.get_barrier_semaphore()
    want = 2
    pl.semaphore_signal(barrier, inc=1, device_id=mate)
    pl.semaphore_signal(barrier, inc=1, device_id=across)
    for cond, who in peers:
        if cond is True:
            pl.semaphore_signal(barrier, inc=1, device_id={"dp": who})
            want = want + 1
        else:

            @pl.when(cond)
            def _(who=who):
                pl.semaphore_signal(barrier, inc=1, device_id={"dp": who})

            want = want + jnp.where(cond, 1, 0).astype(jnp.int32)

    W3 = 3 * G
    loads = Space()

    def load(src, dst, sem):
        copy = pltpu.make_async_copy(src, dst, R.in_sem.at[sem])
        copy.start()
        return copy

    loads.tok = load(R.tok, R.tokv, 0)
    loads.idx = load(R.idx, R.idxv, 1)
    loads.wq = load(R.wq, R.wqkv.at[:, pl.ds(0, G)], 2)
    loads.wk = load(R.wk, R.wqkv.at[:, pl.ds(G, G)], 3)
    loads.wv = load(R.wv, R.wqkv.at[:, pl.ds(2 * G, G)], 4)
    loads.ck = load(R.ck, R.kext.at[pl.ds(0, T)], 5)
    loads.cv = load(R.cv, R.vext.at[pl.ds(0, T)], 6)
    loads.mk = load(R.mk.at[0], R.mkv, 7)
    loads.mv = load(R.mv.at[0], R.mvv, 8)
    loads.wo = load(R.wo, R.wov, 9)
    loads.og = load(R.og, R.ogv, 10)
    loads.wu = load(R.wu, R.wuv, 11)
    loads.wi = load(R.wi, R.wiv, 12)


    def part_rows(hf, c):
        return pl.ds(pl.multiple_of(hf * HB + c * sub, sub), sub)

    def push_desc(p, hf):
        return pltpu.make_async_remote_copy(
            src_ref=R.part.at[p % 2, part_rows(hf, 1 - core)],
            dst_ref=R.cbuf.at[p % 2, pl.ds(hf * sub, sub)],
            send_sem=R.c_send.at[p, hf],
            recv_sem=R.c_recv.at[p, hf],
            device_id=mate,
            device_id_type=pl.DeviceIdType.MESH,
        )

    def cross_desc(p, hf):
        return pltpu.make_async_remote_copy(
            src_ref=R.part.at[p % 2, part_rows(hf, core)],
            dst_ref=R.ybuf.at[p % 2, pl.ds(hf * sub, sub)],
            send_sem=R.y_send.at[p, hf],
            recv_sem=R.y_recv.at[p, hf],
            device_id=across,
            device_id_type=pl.DeviceIdType.MESH,
        )

    def share_desc(p, hf, buf, c):
        rows = part_rows(hf, c)
        return pltpu.make_async_remote_copy(
            src_ref=buf.at[rows],
            dst_ref=buf.at[rows],
            send_sem=R.a_send.at[p, hf],
            recv_sem=R.a_recv.at[p, hf],
            device_id=mate,
            device_id_type=pl.DeviceIdType.MESH,
        )

    def push(p, hf):
        push_desc(p, hf).start()

    def mid(p, hf):
        push_desc(p, hf).wait_recv()
        for r in range(0, sub, CHUNK):
            rows = pl.ds(pl.multiple_of(hf * HB + core * sub + r, CHUNK), CHUNK)
            total = R.part[p % 2, rows, :].astype(F32) + R.cbuf[p % 2, pl.ds(hf * sub + r, CHUNK), :].astype(F32)
            R.part[p % 2, rows, :] = total.astype(BF)
        cross_desc(p, hf).start()

    def sent(p):
        for hf in range(HALVES):
            push_desc(p, hf).wait_send()
            cross_desc(p, hf).wait_send()

    def fin(p, hf, visit):
        cross_desc(p, hf).wait_recv()
        for r in range(0, sub, CHUNK):
            rows = pl.ds(pl.multiple_of(hf * HB + core * sub + r, CHUNK), CHUNK)
            mine = pl.ds(hf * sub + r, CHUNK)
            visit(rows, mine, R.part[p % 2, rows, :].astype(F32) + R.ybuf[p % 2, mine, :].astype(F32))

    RS_R, RS_S, AG_R, AG_S = R.rs_recv, R.rs_send, R.ag_recv, R.ag_send
    g, res, rbuf = R.g, R.res, R.rbuf
    SEG = cfg.seg

    plans = []
    for order in cfg.orders:
        base, size, off, live, plan = 0, SEG, 0, None, []
        for stride, r in order:
            d = lax.rem(me // stride, r)
            size = size // 2
            low_slot = off
            high_slot = off if r == 2 else off + size
            off = high_slot + size
            plan.append(
                Space(stride=stride, r=r, d=d, base=base, size=size, slots=(low_slot, high_slot), live=live)
            )
            base = base + size * (d // (r - 1))
            if r > 2:
                ends = (d == 0) | (d == r - 1)
                live = ends if live is None else live & ends
        plans.append(Space(stages=plan, own=base, own_size=size, live=live))

    def when(cond, live):
        return pl.when(cond if live is None else cond & live)

    def piece(st, hi, at=0, rows=None):
        first = st.base + hi * st.size + at
        return pl.ds(first if isinstance(first, int) else pl.multiple_of(first, 16), rows or st.size)

    def hop(st, right):
        return {"dp": me + st.stride if right else me - st.stride}

    def rs_desc(seg, t, st, hi):
        return pltpu.make_async_remote_copy(
            src_ref=g.at[seg, piece(st, hi)],
            dst_ref=rbuf.at[seg, pl.ds(st.slots[hi], st.size)],
            send_sem=RS_S.at[seg, t, hi],
            recv_sem=RS_R.at[seg, t, hi],
            device_id=hop(st, hi == 1),
            device_id_type=pl.DeviceIdType.MESH,
        )

    def ag_desc(seg, t, st, hi):
        return pltpu.make_async_remote_copy(
            src_ref=res.at[seg, piece(st, hi)],
            dst_ref=res.at[seg, piece(st, hi)],
            send_sem=AG_S.at[seg, t, hi],
            recv_sem=AG_R.at[seg, t, hi],
            device_id=hop(st, hi == 0),
            device_id_type=pl.DeviceIdType.MESH,
        )

    def add_in(seg, st, hi):
        step = min(64, st.size)
        for i in range(0, st.size, step):
            rows = piece(st, hi, i, step)
            total = g[seg, rows, :].astype(F32) + rbuf[seg, pl.ds(st.slots[hi] + i, step), :].astype(F32)
            g[seg, rows, :] = total.astype(BF)

    def each(segs, fn):
        lo, hi = segs
        if hi - lo == 1:
            fn(lo)
        elif hi > lo:
            lax.fori_loop(lo, hi, lambda s, c: (fn(s), c)[1], 0)

    def rs_first(plan, t, seg):
        st = plan.stages[t]

        @when(st.d == 0, st.live)
        def _():
            rs_desc(seg, t, st, 1).start()

        @when(st.d == st.r - 1, st.live)
        def _():
            rs_desc(seg, t, st, 0).start()

    def rs_phase(plan, t, h, seg):
        st = plan.stages[t]
        for hi, at in ((1, h), (0, st.r - 1 - h)):

            @when(st.d == at, st.live)
            def _(hi=hi):
                rs_desc(seg, t, st, hi).wait_recv()
                add_in(seg, st, hi)
                if h < st.r - 1:
                    rs_desc(seg, t, st, hi).start()

    def ag_first(plan, t, seg):
        st = plan.stages[t]

        @when(st.d == st.r - 1, st.live)
        def _():
            ag_desc(seg, t, st, 1).start()

        @when(st.d == 0, st.live)
        def _():
            ag_desc(seg, t, st, 0).start()

    def ag_phase(plan, t, h, seg):
        st = plan.stages[t]
        for hi, at in ((1, st.r - 1 - h), (0, h)):

            @when(st.d == at, st.live)
            def _(hi=hi):
                ag_desc(seg, t, st, hi).wait_recv()
                if h < st.r - 1:
                    ag_desc(seg, t, st, hi).start()

    def dp_start(segs, which):
        each(segs, lambda s: rs_first(plans[which], 0, s))

    def dp_phase(segs, which, k):
        plan = plans[which]
        hops = [st.r - 1 for st in plan.stages]
        S = len(hops)
        scatter = [(t, h + 1) for t in range(S) for h in range(hops[t])]
        gather = [(t, h + 1) for t in range(S - 1, -1, -1) for h in range(hops[t])]

        def one(seg):
            if k < len(scatter):
                t, h = scatter[k]
                rs_phase(plan, t, h, seg)
                if h == hops[t]:
                    if t + 1 < S:
                        rs_first(plan, t + 1, seg)
                    else:

                        @when(me >= 0, plan.live)
                        def _():
                            own = pl.ds(pl.multiple_of(plan.own, 16), plan.own_size)
                            res[seg, own, :] = g[seg, own, :]

                        ag_first(plan, S - 1, seg)
            else:
                t, h = gather[k - len(scatter)]
                ag_phase(plan, t, h, seg)
                if h == hops[t] and t > 0:
                    ag_first(plan, t - 1, seg)

        each(segs, one)

    PHASES = 2 * sum(r - 1 for _, r in cfg.stages)

    def advance(group, k):
        for i in range(PHASES * (k - 1) // 8, PHASES * k // 8):
            for which in (1, 0):
                dp_phase(group[which], which, i)

    def dp_begin(group):
        for which in (0, 1):
            dp_start(group[which], which)

    def dp_close(segs, which):
        plan = plans[which]

        def one(seg):
            for t, st in enumerate(plan.stages):

                @when(st.d < st.r - 1, st.live)
                def _():
                    rs_desc(seg, t, st, 1).wait_send()
                    ag_desc(seg, t, st, 0).wait_send()

                @when(st.d > 0, st.live)
                def _():
                    rs_desc(seg, t, st, 0).wait_send()
                    ag_desc(seg, t, st, 1).wait_send()

        each(segs, one)

    groups = cfg.groups
    outs = []

    def emit(src, dst):
        c = pltpu.make_async_copy(src, dst, R.out_sem.at[len(outs)])
        c.start()
        outs.append(c)

    def emit_seg(j):
        if j < D // TILE:
            emit(res.at[j], R.gwu.at[:, pl.ds(j * TILE, TILE)])
        elif j < cfg.late:
            emit(res.at[j], R.gwi.at[:, pl.ds((j - D // TILE) * TILE, TILE)])
        elif j == cfg.late:
            for i in range(D // TILE):
                emit(res.at[j, pl.ds(i * G, G)], R.gwo.at[:, pl.ds(i * TILE, TILE)])
        else:
            emit(res.at[j], (R.gwv, R.gwq, R.gwk)[j - cfg.late - 1])

    def emit_group(group):
        for j in range(group[0][0], group[1][1]):
            emit_seg(j)

    partners = [mate]
    for s in cfg.doubling:
        partners.append({"dp": me + s - 2 * s * lax.rem(me // s, 2)})
    smalls = R.small
    small_at = [0]

    def small_desc(i):
        return pltpu.make_async_remote_copy(
            src_ref=smalls.at[i],
            dst_ref=R.sbuf.at[i],
            send_sem=R.s_send.at[i],
            recv_sem=R.s_recv.at[i],
            device_id=partners[i],
            device_id_type=pl.DeviceIdType.MESH,
        )

    def small_step():
        i = small_at[0]
        if i == len(partners):
            return
        small_at[0] = i + 1
        small_desc(i).wait_recv()
        got = R.sbuf[i]
        if i == 0:
            got = jnp.where(lax.broadcasted_iota(jnp.int32, (8, D), 0) < 4, got, 0.0)
        smalls[i + 1] = smalls[i] + got
        if i + 1 < len(partners):
            small_desc(i + 1).start()
        else:
            emit(smalls.at[i + 1], R.gsmall)

    def at_point(i):
        for point, which, k in SCHEDULE:
            if point == i and which == SMALL:
                small_step()
            elif point == i:
                advance(groups[which], k)
                if k == 8:
                    emit_group(groups[which])

    fill = R.fill[0]
    topk = cfg.K
    accs = M // LANES // 4
    loads.idx.wait()
    for h in range(NH):
        at = R.idxv[h]
        hi = at // LANES
        lo = at - hi * LANES
        fld = lax.rem(hi, 4)
        one = jnp.where(fld == 0, 1, jnp.where(fld == 1, 1 << 8, jnp.where(fld == 2, 1 << 16, 1 << 24)))
        R.lo[...] = lo
        for a in range(accs):
            ok = (at < fill) & (hi >= 4 * a) & (hi < 4 * a + 4)
            R.inc[a] = jnp.where(ok, one, 0)

        def count_block(b, c):
            lane = lax.broadcasted_iota(jnp.int32, (16, T), 0) + b * 16
            got = [jnp.zeros((16, T), jnp.int32) for _ in range(accs)]
            for k in range(topk):
                hit = jnp.broadcast_to(R.lo[pl.ds(k, 1), :], (16, T)) == lane
                for a in range(accs):
                    got[a] = got[a] + jnp.where(hit, jnp.broadcast_to(R.inc[a, pl.ds(k, 1), :], (16, T)), 0)
            for a in range(accs):
                R.cntt[a, pl.ds(pl.multiple_of(b * 16, 16), 16), :] = got[a]
            return c

        lax.fori_loop(0, LANES // 16, count_block, 0)
        for a in range(accs):
            R.cnt[h, a] = R.cntt[a].T

    loads.tok.wait()

    def norm_one(i, c):
        for r in range(0, 128, CHUNK):
            rows = pl.ds(pl.multiple_of(i * 128 + r, CHUNK), CHUNK)
            cen, rstd = row_stats(R.tokv[rows, :].astype(F32))
            R.nrm[rows, :] = (cen * rstd * R.g1[...] + R.s1[...]).astype(BF)
        return c

    lax.fori_loop(0, T // 128, norm_one, 0)
    for copy in (loads.wq, loads.wk, loads.wv):
        copy.wait()
    for rb in range(2):
        rows = pl.ds(rb * HB, HB)
        low = R.nrm[rows, :]
        R.q[rows, :] = nn(low, R.wqkv[:, 0:G]).astype(BF)
        R.kext[pl.ds(T + rb * HB, HB), :] = nn(low, R.wqkv[:, G : 2 * G]).astype(BF)
        R.vext[pl.ds(T + rb * HB, HB), :] = nn(low, R.wqkv[:, 2 * G : W3]).astype(BF)

    band_row = lax.dot_general(
        R.table[...], R.oh[...], (((1,), (0,)), ((), ())), precision=EXACT, preferred_element_type=F32
    )
    u_at = lax.broadcasted_iota(jnp.int32, (NH, KW), 1)
    band_row = jnp.where((u_at >= 1) & (u_at <= T), band_row, NEGATIVE)
    for h in range(NH):
        wide = jnp.broadcast_to(band_row[h : h + 1, :], (HB, KW))
        R.band[h] = pltpu.roll(wide, 0, 1, stride=1, stride_axis=0)

    for j in range(U // LANES):
        R.ibv[:, j * LANES : (j + 1) * LANES] = R.ib[j : j + 1, :].astype(F32)
    mix = jax.nn.sigmoid(R.gate[...])
    pl.semaphore_wait(barrier, want)

    for copy in (loads.ck, loads.cv, loads.mk, loads.mv, loads.wo):
        copy.wait()

    def attend(rb, h):
        rows = pl.ds(rb * HB, HB)
        cols = slice(h * DH, (h + 1) * DH)
        wide = pl.ds(rb * HB, KW)
        q = R.q[rows, cols]
        raw = nt(q, R.kext[wide, cols])
        for r in range(0, HB, CHUNK):
            s = raw[r : r + CHUNK] * scale + R.band[h, r : r + CHUNK, :]
            e = jnp.exp(s - jnp.max(s, axis=-1, keepdims=True))
            p = e * (1.0 / jnp.sum(e, axis=-1, keepdims=True))
            R.pl[h, pl.ds(rb * HB + r, CHUNK), :] = p.astype(BF)
        near = nn(R.pl[h, rows, :], R.vext[wide, cols])
        raw = nt(q, R.mkv[:, cols])
        for r in range(0, HB, CHUNK):
            at = pl.ds(rb * HB + r, CHUNK)
            fields = []
            for f in range(M // LANES):
                fields.append(((R.cnt[h, f // 4, at, :] >> (8 * (f % 4))) & 255).astype(F32))
            c = jnp.concatenate(fields, axis=1)
            s = jnp.where(c > 0.0, raw[r : r + CHUNK] * scale, NEGATIVE)
            top = jnp.maximum(jnp.max(s, axis=-1, keepdims=True), 0.0)
            e = jnp.exp(s - top) * c
            total = jnp.exp(-top) + jnp.sum(e, axis=-1, keepdims=True)
            R.pm[h, at, :] = (e * (1.0 / total)).astype(BF)
        far = nn(R.pm[h, rows, :], R.mvv[:, cols])
        m = mix[:, h : h + 1]
        R.diff[rows, cols] = far - near
        R.joined[rows, cols] = (m * far + (1.0 - m) * near).astype(BF)

    def project(rb):
        rows = pl.ds(rb * HB, HB)
        for j in range(D // TILE):
            cols = slice(j * TILE, (j + 1) * TILE)
            R.part[0, rows, cols] = nn(R.joined[rows, :], R.wov[:, cols]).astype(BF)

    for h in range(NH):
        attend(0, h)
    project(0)
    push(0, 0)
    for h in range(NH):
        attend(1, h)
        if h == 0:
            mid(0, 0)
    project(1)
    push(0, 1)

    for copy in (loads.og, loads.wu, loads.wi):
        copy.wait()

    def tiles(count, fn):
        lax.fori_loop(0, count, lambda j, c: (fn(pl.ds(pl.multiple_of(j * TILE, TILE), TILE)), c)[1], 0)

    def feed_back(hf):
        rows = pl.ds(hf * HB, HB)

        def back_one(cols):
            R.ga[rows, cols] = nt(R.ogv[rows, :], R.wuv[cols, :])

        tiles(U // TILE, back_one)

    def second_norm(hf):
        def visit(rows, mine, total):
            x = R.tokv[rows, :].astype(F32) + total
            R.resid[mine, :] = x
            cen, rstd = row_stats(x)
            R.ntl[rows, :] = (cen * rstd * R.g2[...] + R.s2[...]).astype(BF)

        fin(0, hf, visit)
        share_desc(0, hf, R.ntl, core).start()

    def feed(hf):
        rows = pl.ds(hf * HB, HB)

        def unit(cols):
            pre = nn(R.ntl[rows, :], R.wiv[:, cols])
            bias = R.ibv[:, cols]
            sums = jnp.zeros((1, TILE), F32)
            for r in range(0, HB, CHUNK):
                at = pl.ds(hf * HB + r, CHUNK)
                x = pre[r : r + CHUNK] + bias
                x2 = x * x
                t = jnp.tanh(GELU_A * (x + GELU_B * x * x2))
                R.act[at, cols] = (0.5 * x * (1.0 + t)).astype(BF)
                slope = 0.5 * (1.0 + t) + 0.5 * x * (1.0 - t * t) * (GELU_A * (1.0 + 3.0 * GELU_B * x2))
                gi = (R.ga[at, cols] * slope).astype(BF)
                R.gi[at, cols] = gi
                sums = sums + jnp.sum(gi.astype(F32), axis=0, keepdims=True)
            R.gib[pl.ds(hf, 1), cols] = sums
            R.tr[cols, rows] = R.act[rows, cols].T

        tiles(U // TILE, unit)

        def back(cols):
            R.part[1, rows, cols] = nt(R.gi[rows, :], R.wiv[cols, :]).astype(BF)

        tiles(D // TILE, back)

    feed_back(0)
    mid(0, 1)
    feed_back(1)
    second_norm(0)
    share_desc(0, 0, R.ntl, 1 - core).wait_recv()
    feed(0)
    push(1, 0)
    second_norm(1)
    mid(1, 0)
    share_desc(0, 1, R.ntl, 1 - core).wait_recv()
    feed(1)
    push(1, 1)

    def start_one(j):
        group = groups[0] if j < D // TILE else groups[1]
        dp_start((j, j + 1), 0 if j < group[0][1] else 1)

    for j in range(D // TILE):
        g[j] = nn(R.tr[...], R.ogv[:, j * TILE : (j + 1) * TILE]).astype(BF)
        start_one(j)
        if j == 1:
            mid(1, 1)
    R.tr[...] = R.ntl[...].T
    for j in range(U // TILE):
        g[D // TILE + j] = nn(R.tr[...], R.gi[:, j * TILE : (j + 1) * TILE]).astype(BF)
        start_one(D // TILE + j)
    sent(0)
    for hf in range(HALVES):
        rows = pl.ds(hf * HB, HB)

        def fed(cols, rows=rows):
            R.part[0, rows, cols] = nn(R.act[rows, :], R.wuv[:, cols]).astype(BF)

        tiles(D // TILE, fed)
        push(2, hf)

    def norm_back(p, hf, source, gain, base, keep, out):
        gain_sum, shift_sum = [jnp.zeros((1, D), F32)], [jnp.zeros((1, D), F32)]

        def visit(rows, mine, dy):
            cen, rstd = row_stats(source(rows, mine))
            xh = cen * rstd
            gain_sum[0] = gain_sum[0] + jnp.sum(dy * xh, axis=0, keepdims=True)
            shift_sum[0] = shift_sum[0] + jnp.sum(dy, axis=0, keepdims=True)
            dx = dy * gain
            dx = rstd * (
                dx - jnp.mean(dx, axis=-1, keepdims=True) - xh * jnp.mean(dx * xh, axis=-1, keepdims=True)
            )
            got = base(rows, mine) + dx
            if keep is not None:
                keep[mine, :] = got
            out[rows, :] = got.astype(BF)

        fin(p, hf, visit)
        share_desc(p, hf, out, core).start()
        return gain_sum[0], shift_sum[0]

    sums = [
        norm_back(
            1, hf, lambda rows, mine: R.resid[mine, :], R.g2[...],
            lambda rows, mine: R.ogv[rows, :].astype(F32), R.gres, R.gat,
        )
        for hf in range(HALVES)
    ]
    R.small[0, 2:3, :] = sums[0][0] + sums[1][0]
    R.small[0, 3:4, :] = sums[0][1] + sums[1][1]
    for hf in range(HALVES):
        mid(2, hf)
    at_point(5)
    for hf in range(HALVES):
        share_desc(1, hf, R.gat, 1 - core).wait_recv()

    gate_sums = [jnp.zeros((1, 1), F32) for _ in range(NH)]
    for rb in range(2):
        rows = pl.ds(rb * HB, HB)
        gj = nt(R.gat[rows, :], R.wov[...])
        for h in range(NH):
            cols = slice(h * DH, (h + 1) * DH)
            m = mix[:, h : h + 1]
            gate_sums[h] = gate_sums[h] + jnp.sum(
                jnp.sum(gj[:, cols] * R.diff[rows, cols], axis=0, keepdims=True), axis=1, keepdims=True
            )
            R.gl[rows, cols] = ((1.0 - m) * gj[:, cols]).astype(BF)
            R.gm[rows, cols] = (m * gj[:, cols]).astype(BF)

    def own_keys(weights, other, out):
        for h in range(NH):
            cols = slice(h * DH, (h + 1) * DH)
            spot = slice(out * G + h * DH, out * G + (h + 1) * DH)
            top = tn(weights[h, 0:HB, T:KW], other[0:HB, cols]) + tn(weights[h, HB:T, HB:T], other[HB:T, cols])
            R.gqkv[0:HB, spot] = top.astype(BF)
            R.gqkv[HB:T, spot] = tn(weights[h, HB:T, T:KW], other[HB:T, cols]).astype(BF)

    def weight_seg(seg, out):
        g[seg] = nn(R.tr[...], R.gqkv[:, out * G : (out + 1) * G]).astype(BF)

    LATE = cfg.late
    for j in range(D // TILE):
        g[LATE, j * G : (j + 1) * G, :] = tn(R.joined[...], R.gat[:, j * TILE : (j + 1) * TILE]).astype(BF)
    dp_start((LATE, LATE + 1), 0)
    R.tr[...] = R.nrm[...].T
    own_keys(R.pl, R.gl, 2)
    weight_seg(LATE + 1, 2)
    dp_start((LATE + 1, LATE + 2), 1)
    at_point(7)
    for rb in range(2):
        rows = pl.ds(rb * HB, HB)
        wide = pl.ds(rb * HB, KW)
        for h in range(NH):
            cols = slice(h * DH, (h + 1) * DH)
            dp = nt(R.gl[rows, cols], R.vext[wide, cols])
            for r in range(0, HB, CHUNK):
                at = pl.ds(rb * HB + r, CHUNK)
                p, d = R.pl[h, at, :].astype(F32), dp[r : r + CHUNK]
                ds = p * (d - jnp.sum(p * d, axis=-1, keepdims=True))
                if rb == 0:
                    R.band[h, pl.ds(r, CHUNK), :] = ds
                else:
                    R.band[h, pl.ds(r, CHUNK), :] += ds
                R.pl[h, at, :] = (ds * scale).astype(BF)
            gq = nn(R.pl[h, rows, :], R.kext[wide, cols])
            dp = nt(R.gm[rows, cols], R.mvv[:, cols])
            for r in range(0, HB, CHUNK):
                at = pl.ds(rb * HB + r, CHUNK)
                p, d = R.pm[h, at, :].astype(F32), dp[r : r + CHUNK]
                ds = p * (d - jnp.sum(p * d, axis=-1, keepdims=True))
                R.pm[h, at, :] = (ds * scale).astype(BF)
            gq = gq + nn(R.pm[h, rows, :], R.mkv[:, cols])
            R.gqkv[rows, cols] = gq.astype(BF)
            at_point(8 + (rb * NH + h) * 4 // (2 * NH))

    weight_seg(LATE + 2, 0)
    dp_start((LATE + 2, LATE + 3), 0)
    own_keys(R.pl, R.q, 1)
    weight_seg(LATE + 3, 1)
    dp_start((LATE + 3, LATE + 4), 1)
    at_point(13)
    sent(1)
    for hf in range(HALVES):
        rows = pl.ds(hf * HB, HB)

        def back_in(cols, rows=rows):
            R.part[1, rows, cols] = nt(R.gqkv[rows, :], R.wqkv[cols, :]).astype(BF)

        tiles(D // TILE, back_in)
        push(3, hf)

    for hf in range(HALVES):

        def result(rows, mine, total):
            R.bo[rows, :] = (R.resid[mine, :] + total).astype(BF)

        fin(2, hf, result)
        share_desc(2, hf, R.bo, core).start()
    at_point(14)
    for hf in range(HALVES):
        mid(3, hf)
    at_point(15)

    at_row = lax.broadcasted_iota(jnp.int32, (8, KW), 0)
    table_grads = []
    for h in range(NH):
        half = HB
        cur = R.band[h]
        while half > 8:
            half //= 2
            cur = cur[:half] + pltpu.roll(cur[half:], KW - half, 1)
        for bit in (1, 2, 4):
            cur = jnp.where(lax.rem(at_row // bit, 2) == 1, pltpu.roll(cur, KW - bit, 1), cur)
        diag = jnp.sum(cur, axis=0, keepdims=True)
        table_grads.append(
            lax.dot_general(diag, R.oh[...], (((1,), (1,)), ((), ())), precision=EXACT, preferred_element_type=F32)
        )
    smalls[0, 4:5, :] = R.gib[0:1, :] + R.gib[1:2, :]
    smalls[0, 5:8, :] = jnp.zeros((3, D), F32)
    for h in range(NH):
        s = mix[:, h : h + 1]
        smalls[0, 5:6, h * LANES : h * LANES + NB] = table_grads[h]
        smalls[0, 6:7, h * LANES : (h + 1) * LANES] = jnp.broadcast_to(gate_sums[h] * s * (1.0 - s), (1, LANES))

    sums = [
        norm_back(
            3, hf, lambda rows, mine: R.tokv[rows, :].astype(F32), R.g1[...],
            lambda rows, mine: R.gres[mine, :], None, R.gt,
        )
        for hf in range(HALVES)
    ]
    smalls[0, 0:1, :] = sums[0][0] + sums[1][0]
    smalls[0, 1:2, :] = sums[0][1] + sums[1][1]
    small_desc(0).start()
    at_point(16)

    for hf in range(HALVES):
        share_desc(2, hf, R.bo, 1 - core).wait_recv()
        share_desc(3, hf, R.gt, 1 - core).wait_recv()
    emit(R.bo, R.block_out)
    emit(R.gt, R.gtok)
    at_point(17)
    for _ in partners:
        small_step()

    sent(2)
    sent(3)
    for p in range(4):
        for hf in range(HALVES):
            share_desc(p, hf, (R.ntl, R.gat, R.bo, R.gt)[p], core).wait_send()
    for i in range(len(partners)):
        small_desc(i).wait_send()
    for group in groups:
        for which in (0, 1):
            dp_close(group[which], which)
    for c in outs:
        c.wait()


def local(n, tokens, wq, wk, wv, wo, wi, ib, wu, g1, s1, g2, s2, table, gate, ck, cv, mk, mv, idx, fill, og):
    T, D = tokens.shape
    NH = table.shape[0]
    G = wq.shape[1]
    U = wi.shape[1]
    M = mk.shape[1]
    K = idx.shape[2]
    HB = T // 2
    KW = T + HB
    stages = stage_list(n)
    doubling = []
    s = 1
    while s < n:
        doubling.append(s)
        s *= 2
    ffn = (D + U) // TILE
    late = 1 + 3 * G // TILE
    nseg = ffn + late
    groups = []
    for lo, count in ((0, D // TILE), (D // TILE, U // TILE), (ffn, 2), (ffn + 2, 2)):
        half = lo + count // 2
        groups.append(((lo, half), (half, lo + count)))
    seg = D
    orders = (stages, stages[::-1])
    rows_needed = 0
    for order in orders:
        off, length = 0, seg
        for _, r in order:
            length //= 2
            off += (1 if r == 2 else 2) * length
        rows_needed = max(rows_needed, off)
    inputs = dict(
        tok=tokens, idx=idx.transpose(1, 2, 0), wq=wq, wk=wk, wv=wv, wo=wo, wi=wi, wu=wu, ck=ck, cv=cv, mk=mk, mv=mv, og=og
    )
    vectors = dict(
        ib=ib.reshape(U // LANES, LANES), g1=g1.reshape(1, D), s1=s1.reshape(1, D), g2=g2.reshape(1, D), s2=s2.reshape(1, D),
        table=table, gate=gate.reshape(1, NH), oh=jnp.asarray(bucket_rows(T)),
    )
    outputs = dict(
        block_out=((T, D), BF), gtok=((T, D), BF), gwq=((D, G), BF), gwk=((D, G), BF), gwv=((D, G), BF),
        gwo=((G, D), BF), gwi=((D, U), BF), gwu=((U, D), BF), gsmall=((8, D), F32),
    )
    S = len(stages)
    sem = pltpu.SemaphoreType.DMA
    scratch = dict(
        tokv=pltpu.VMEM((T, D), BF), ogv=pltpu.VMEM((T, D), BF), idxv=pltpu.VMEM((NH, K, T), jnp.int32),
        wqkv=pltpu.VMEM((D, 3 * G), BF), wov=pltpu.VMEM((G, D), BF), wiv=pltpu.VMEM((D, U), BF),
        wuv=pltpu.VMEM((U, D), BF), kext=pltpu.VMEM((2 * T, G), BF), vext=pltpu.VMEM((2 * T, G), BF),
        mkv=pltpu.VMEM((M, G), BF), mvv=pltpu.VMEM((M, G), BF),
        lo=pltpu.VMEM((K, T), jnp.int32), inc=pltpu.VMEM((M // LANES // 4, K, T), jnp.int32),
        cntt=pltpu.VMEM((M // LANES // 4, LANES, T), jnp.int32),
        cnt=pltpu.VMEM((NH, M // LANES // 4, T, LANES), jnp.int32),
        nrm=pltpu.VMEM((T, D), BF), q=pltpu.VMEM((T, G), BF), band=pltpu.VMEM((NH, HB, KW), F32),
        pl=pltpu.VMEM((NH, T, KW), BF), pm=pltpu.VMEM((NH, T, M), BF), diff=pltpu.VMEM((T, G), F32),
        joined=pltpu.VMEM((T, G), BF), ga=pltpu.VMEM((T, U), F32), ntl=pltpu.VMEM((T, D), BF),
        resid=pltpu.VMEM((HB, D), F32), act=pltpu.VMEM((T, U), BF), gi=pltpu.VMEM((T, U), BF),
        gib=pltpu.VMEM((8, U), F32), ibv=pltpu.VMEM((1, U), F32), tr=pltpu.VMEM((D, T), BF), gres=pltpu.VMEM((HB, D), F32),
        gat=pltpu.VMEM((T, D), BF), gl=pltpu.VMEM((T, G), BF), gm=pltpu.VMEM((T, G), BF),
        gqkv=pltpu.VMEM((T, 3 * G), BF), bo=pltpu.VMEM((T, D), BF), gt=pltpu.VMEM((T, D), BF),
        part=pltpu.VMEM((2, T, D), BF), cbuf=pltpu.VMEM((2, HB, D), BF), ybuf=pltpu.VMEM((2, HB, D), BF),
        small=pltpu.VMEM((len(doubling) + 2, 8, D), F32), sbuf=pltpu.VMEM((len(doubling) + 1, 8, D), F32),
        g=pltpu.VMEM((nseg, seg, TILE), BF), res=pltpu.VMEM((nseg, seg, TILE), BF),
        rbuf=pltpu.VMEM((nseg, rows_needed, TILE), BF),
        in_sem=sem((13,)), out_sem=sem((2 + 2 * (D // TILE) + U // TILE + 4,)),
        c_send=sem((4, HALVES)), c_recv=sem((4, HALVES)), y_send=sem((4, HALVES)), y_recv=sem((4, HALVES)),
        a_send=sem((4, HALVES)), a_recv=sem((4, HALVES)),
        s_send=sem((len(doubling) + 1,)), s_recv=sem((len(doubling) + 1,)),
        rs_send=sem((nseg, S, 2)), rs_recv=sem((nseg, S, 2)),
        ag_send=sem((nseg, S, 2)), ag_recv=sem((nseg, S, 2)),
    )
    cfg = Space(
        n=n, T=T, D=D, G=G, U=U, M=M, NH=NH, K=K, stages=stages, doubling=doubling, seg=seg, orders=orders,
        groups=groups, late=ffn,
        names=[*inputs, *vectors, "fill", *outputs, *scratch],
    )
    any_spec = pl.BlockSpec(memory_space=pl.ANY)
    vec_spec = pl.BlockSpec(memory_space=pltpu.VMEM)
    outs = pl.pallas_call(
        functools.partial(kernel, cfg),
        out_shape=[jax.ShapeDtypeStruct(*v) for v in outputs.values()],
        in_specs=[any_spec] * len(inputs) + [vec_spec] * len(vectors) + [pl.BlockSpec(memory_space=pltpu.SMEM)],
        out_specs=[any_spec] * len(outputs),
        scratch_shapes=list(scratch.values()),
        compiler_params=pltpu.CompilerParams(
            collective_id=0, has_side_effects=True, vmem_limit_bytes=63 * MIB
        ),
        cost_estimate=pl.CostEstimate(flops=12 * 10**9, bytes_accessed=20 * 10**6, transcendentals=3 * 10**6),
    )(
        *inputs.values(), *vectors.values(), fill,
    )
    return widen(outs, NH)


def widen_kernel(NH, cuts, *refs):
    ins, outs, scratch = refs[:9], refs[9:24], refs[24:]
    boxes = len(cuts)
    low, high, (in_sem, out_sem) = scratch[:boxes], scratch[boxes : 2 * boxes], scratch[2 * boxes :]
    loads, stores = [], []
    for n, (i, at, rows, cols) in enumerate(cuts):
        loads.append(pltpu.make_async_copy(ins[i].at[pl.ds(at, rows)], low[n], in_sem.at[n]))
        stores.append(pltpu.make_async_copy(high[n], outs[i].at[pl.ds(at, rows)], out_sem.at[n]))
        loads[n].start()
    copies = [pltpu.make_async_copy(ins[i], outs[i], out_sem.at[boxes + i]) for i in range(2)]
    for c in copies:
        c.start()
    small = ins[8]
    for i in range(5):
        outs[8 + i][...] = small[i : i + 1, :]
    for h in range(NH):
        outs[13][h : h + 1, :] = small[5:6, h * LANES : h * LANES + NB]
        outs[14][:, h : h + 1] = small[6:7, h * LANES : h * LANES + 1]
    for n, (i, at, rows, cols) in enumerate(cuts):
        loads[n].wait()
        high[n][...] = low[n][...].astype(F32)
        stores[n].start()
    for c in copies + stores:
        c.wait()


def widen(sums, NH):
    small = sums[8]
    D = small.shape[1]
    cuts = []
    for i in range(2, 8):
        rows, cols = sums[i].shape
        step = max(8, min(rows, TILE * D // cols))
        cuts += [(i, at, step, cols) for at in range(0, rows, step)]
    shapes = [jax.ShapeDtypeStruct(x.shape, BF if i < 2 else F32) for i, x in enumerate(sums[:8])]
    tiny = [(1, D)] * 5 + [(NH, NB), (1, NH)]
    hbm = pl.BlockSpec(memory_space=pl.ANY)
    vec = pl.BlockSpec(memory_space=pltpu.VMEM)
    got = pl.pallas_call(
        functools.partial(widen_kernel, NH, cuts),
        in_specs=[hbm] * 8 + [vec],
        out_specs=[hbm] * 8 + [vec] * len(tiny),
        out_shape=shapes + [jax.ShapeDtypeStruct(x, F32) for x in tiny],
        scratch_shapes=[pltpu.VMEM((rows, cols), BF) for _, _, rows, cols in cuts]
        + [pltpu.VMEM((rows, cols), F32) for _, _, rows, cols in cuts]
        + [pltpu.SemaphoreType.DMA((len(cuts),)), pltpu.SemaphoreType.DMA((len(cuts) + 2,))],
        compiler_params=pltpu.CompilerParams(vmem_limit_bytes=60 * MIB),
        cost_estimate=pl.CostEstimate(flops=0, bytes_accessed=22 * 10**6, transcendentals=0),
    )(*sums)
    block_out, gtok, gwq, gwk, gwv, gwo, gwi, gwu, g1, s1, g2, s2, ib, bias, gates = got
    return (
        block_out, gtok, gwq, gwk, gwv, gwo, gwi, ib.reshape(-1), gwu, g1.reshape(D), s1.reshape(D), g2.reshape(D),
        s2.reshape(D), bias, gates.reshape(NH),
    )


def solution(mesh):
    return jax.shard_map(
        functools.partial(local, mesh.shape["dp"]),
        mesh=mesh,
        in_specs=(
            P("dp", None), P(None, "head"), P(None, "head"), P(None, "head"), P("head", None), P(None, "head"),
            P("head"), P("head", None), P(), P(), P(), P(), P("head", None), P("head"), P("dp", "head"),
            P("dp", "head"), P("dp", None, "head"), P("dp", None, "head"), P("dp", "head", None), P("dp"),
            P("dp", None),
        ),
        out_specs=(
            P("dp", None), P("dp", None), P(None, "head"), P(None, "head"), P(None, "head"), P("head", None),
            P(None, "head"), P("head"), P("head", None), P(), P(), P(), P(), P("head", None), P("head"),
        ),
        check_vma=False,
    )
```

```python
import functools
import math
from types import SimpleNamespace as Space

import jax
import jax.numpy as jnp
import numpy as np
from jax import lax
from jax.experimental import pallas as pl
from jax.experimental.pallas import tpu as pltpu
from jax.sharding import PartitionSpec as P

NB = 32
MAXD = 128
EPSILON = 1e-05
NEGATIVE = -1e30
EXACT = lax.Precision.HIGHEST
BF = jnp.bfloat16
F32 = jnp.float32
LANES = 128
TILE = 256
HALVES = 2
CHUNK = 32
MIB = 1 << 20
SMALL = -1
SCHEDULE = (
    (5, 0, 1), (7, 0, 2), (7, 1, 1), (7, 0, 3), (9, 1, 2), (9, 0, 4), (9, 2, 1), (9, 1, 3), (9, 0, 5), (10, 2, 2),
    (10, 1, 4), (11, 2, 3), (13, 0, 6), (14, 0, 7), (14, 2, 4), (14, 1, 5), (15, 3, 1), (15, 3, 2), (15, 2, 5), (15, 1, 6),
    (16, 3, 3), (16, 0, 8), (16, 3, 4), (16, SMALL, 0), (16, 1, 7), (16, 2, 6), (16, SMALL, 0), (17, 2, 7), (17, 3, 5),
    (17, SMALL, 0), (17, 1, 8), (17, 2, 8), (17, SMALL, 0), (17, 3, 6), (17, 3, 7), (17, 3, 8),
)
GELU_A = math.sqrt(2.0 / math.pi)
GELU_B = 0.044715


def bucket_rows(length):
    span = np.arange(length)
    exact = NB // 2
    ratio = np.log(np.maximum(span, 1) / exact) / np.log(MAXD / exact)
    larger = np.minimum(exact + (ratio * (NB - exact)).astype(np.int32), NB - 1)
    bucket = np.where(span < exact, span, larger).astype(np.int32)
    table = np.zeros((NB, length + length // 2), np.float32)
    for u in range(1, length + 1):
        table[bucket[length - u], u] = 1.0
    return table


def nn(a, b):
    return lax.dot_general(a, b, (((1,), (0,)), ((), ())), preferred_element_type=F32)


def nt(a, b):
    return lax.dot_general(a, b, (((1,), (1,)), ((), ())), preferred_element_type=F32)


def tn(a, b):
    return lax.dot_general(a, b, (((0,), (0,)), ((), ())), preferred_element_type=F32)


def row_stats(x):
    mean = jnp.mean(x, axis=-1, keepdims=True)
    c = x - mean
    var = jnp.mean(c * c, axis=-1, keepdims=True)
    return c, lax.rsqrt(var + EPSILON)


def stage_list(n):
    stages, stride, left = [], 1, n
    if left >= 2:
        stages.append((1, 2))
        stride, left = 2, left // 2
    while left >= 4:
        stages.append((stride, 4))
        stride, left = stride * 4, left // 4
    if left == 2:
        stages.append((stride, 2))
    return stages


def kernel(cfg, *refs):
    n = cfg.n
    R = Space(**dict(zip(cfg.names, refs)))
    T, D, G, U, M, NH = cfg.T, cfg.D, cfg.G, cfg.U, cfg.M, cfg.NH
    DH = G // NH
    HB = T // 2
    KW = T + HB
    scale = 1.0 / math.sqrt(DH)
    me = lax.axis_index("dp")
    hid = lax.axis_index("head")
    core = lax.rem(hid, 2)
    mate = {"head": hid + 1 - 2 * core}
    across = {"head": lax.rem(hid + 2, 4)}
    sub = HB // 2

    open_scope = []

    def section(name):
        if open_scope:
            open_scope.pop().__exit__(None, None, None)
        if name:
            open_scope.append(jax.named_scope(name))
            open_scope[0].__enter__()

    peers = []
    for stride, r in cfg.stages:
        d = lax.rem(me // stride, r)
        peers.append((d > 0, me - stride))
        peers.append((d < r - 1, me + stride))
    for s in cfg.doubling:
        covered = False
        for stride, r in cfg.stages:
            if s == stride:
                covered = True
        if not covered:
            b = lax.rem(me // s, 2)
            peers.append((True, me + s - 2 * s * b))
    barrier = pltpu.get_barrier_semaphore()
    want = 2
    pl.semaphore_signal(barrier, inc=1, device_id=mate)
    pl.semaphore_signal(barrier, inc=1, device_id=across)
    for cond, who in peers:
        if cond is True:
            pl.semaphore_signal(barrier, inc=1, device_id={"dp": who})
            want = want + 1
        else:

            @pl.when(cond)
            def _(who=who):
                pl.semaphore_signal(barrier, inc=1, device_id={"dp": who})

            want = want + jnp.where(cond, 1, 0).astype(jnp.int32)

    W3 = 3 * G
    loads = Space()

    def load(src, dst, sem):
        copy = pltpu.make_async_copy(src, dst, R.in_sem.at[sem])
        copy.start()
        return copy

    loads.tok = load(R.tok, R.tokv, 0)
    loads.idx = load(R.idx, R.idxv, 1)
    loads.wq = load(R.wq, R.wqkv.at[:, pl.ds(0, G)], 2)
    loads.wk = load(R.wk, R.wqkv.at[:, pl.ds(G, G)], 3)
    loads.wv = load(R.wv, R.wqkv.at[:, pl.ds(2 * G, G)], 4)
    loads.ck = load(R.ck, R.kext.at[pl.ds(0, T)], 5)
    loads.cv = load(R.cv, R.vext.at[pl.ds(0, T)], 6)
    loads.mk = load(R.mk.at[0], R.mkv, 7)
    loads.mv = load(R.mv.at[0], R.mvv, 8)
    loads.wo = load(R.wo, R.wov, 9)
    loads.og = load(R.og, R.ogv, 10)
    loads.wu = load(R.wu, R.wuv, 11)
    loads.wi = load(R.wi, R.wiv, 12)


    def part_rows(hf, c):
        return pl.ds(pl.multiple_of(hf * HB + c * sub, sub), sub)

    def push_desc(p, hf):
        return pltpu.make_async_remote_copy(
            src_ref=R.part.at[p % 2, part_rows(hf, 1 - core)],
            dst_ref=R.cbuf.at[p % 2, pl.ds(hf * sub, sub)],
            send_sem=R.c_send.at[p, hf],
            recv_sem=R.c_recv.at[p, hf],
            device_id=mate,
            device_id_type=pl.DeviceIdType.MESH,
        )

    def cross_desc(p, hf):
        return pltpu.make_async_remote_copy(
            src_ref=R.part.at[p % 2, part_rows(hf, core)],
            dst_ref=R.ybuf.at[p % 2, pl.ds(hf * sub, sub)],
            send_sem=R.y_send.at[p, hf],
            recv_sem=R.y_recv.at[p, hf],
            device_id=across,
            device_id_type=pl.DeviceIdType.MESH,
        )

    def share_desc(p, hf, buf, c):
        rows = part_rows(hf, c)
        return pltpu.make_async_remote_copy(
            src_ref=buf.at[rows],
            dst_ref=buf.at[rows],
            send_sem=R.a_send.at[p, hf],
            recv_sem=R.a_recv.at[p, hf],
            device_id=mate,
            device_id_type=pl.DeviceIdType.MESH,
        )

    def push(p, hf):
        push_desc(p, hf).start()

    def mid(p, hf):
        push_desc(p, hf).wait_recv()
        for r in range(0, sub, CHUNK):
            rows = pl.ds(pl.multiple_of(hf * HB + core * sub + r, CHUNK), CHUNK)
            total = R.part[p % 2, rows, :].astype(F32) + R.cbuf[p % 2, pl.ds(hf * sub + r, CHUNK), :].astype(F32)
            R.part[p % 2, rows, :] = total.astype(BF)
        cross_desc(p, hf).start()

    def sent(p):
        for hf in range(HALVES):
            push_desc(p, hf).wait_send()
            cross_desc(p, hf).wait_send()

    def fin(p, hf, visit):
        cross_desc(p, hf).wait_recv()
        for r in range(0, sub, CHUNK):
            rows = pl.ds(pl.multiple_of(hf * HB + core * sub + r, CHUNK), CHUNK)
            mine = pl.ds(hf * sub + r, CHUNK)
            visit(rows, mine, R.part[p % 2, rows, :].astype(F32) + R.ybuf[p % 2, mine, :].astype(F32))

    RS_R, RS_S, AG_R, AG_S = R.rs_recv, R.rs_send, R.ag_recv, R.ag_send
    g, res, rbuf = R.g, R.res, R.rbuf
    SEG = cfg.seg

    plans = []
    for order in cfg.orders:
        base, size, off, live, plan = 0, SEG, 0, None, []
        for stride, r in order:
            d = lax.rem(me // stride, r)
            size = size // 2
            low_slot = off
            high_slot = off if r == 2 else off + size
            off = high_slot + size
            plan.append(
                Space(stride=stride, r=r, d=d, base=base, size=size, slots=(low_slot, high_slot), live=live)
            )
            base = base + size * (d // (r - 1))
            if r > 2:
                ends = (d == 0) | (d == r - 1)
                live = ends if live is None else live & ends
        plans.append(Space(stages=plan, own=base, own_size=size, live=live))

    def when(cond, live):
        return pl.when(cond if live is None else cond & live)

    def piece(st, hi, at=0, rows=None):
        first = st.base + hi * st.size + at
        return pl.ds(first if isinstance(first, int) else pl.multiple_of(first, 16), rows or st.size)

    def hop(st, right):
        return {"dp": me + st.stride if right else me - st.stride}

    def rs_desc(seg, t, st, hi):
        return pltpu.make_async_remote_copy(
            src_ref=g.at[seg, piece(st, hi)],
            dst_ref=rbuf.at[seg, pl.ds(st.slots[hi], st.size)],
            send_sem=RS_S.at[seg, t, hi],
            recv_sem=RS_R.at[seg, t, hi],
            device_id=hop(st, hi == 1),
            device_id_type=pl.DeviceIdType.MESH,
        )

    def ag_desc(seg, t, st, hi):
        return pltpu.make_async_remote_copy(
            src_ref=res.at[seg, piece(st, hi)],
            dst_ref=res.at[seg, piece(st, hi)],
            send_sem=AG_S.at[seg, t, hi],
            recv_sem=AG_R.at[seg, t, hi],
            device_id=hop(st, hi == 0),
            device_id_type=pl.DeviceIdType.MESH,
        )

    def add_in(seg, st, hi):
        step = min(64, st.size)
        for i in range(0, st.size, step):
            rows = piece(st, hi, i, step)
            total = g[seg, rows, :].astype(F32) + rbuf[seg, pl.ds(st.slots[hi] + i, step), :].astype(F32)
            g[seg, rows, :] = total.astype(BF)

    def each(segs, fn):
        lo, hi = segs
        if hi - lo == 1:
            fn(lo)
        elif hi > lo:
            lax.fori_loop(lo, hi, lambda s, c: (fn(s), c)[1], 0)

    def rs_first(plan, t, seg):
        st = plan.stages[t]

        @when(st.d == 0, st.live)
        def _():
            rs_desc(seg, t, st, 1).start()

        @when(st.d == st.r - 1, st.live)
        def _():
            rs_desc(seg, t, st, 0).start()

    def rs_phase(plan, t, h, seg):
        st = plan.stages[t]
        for hi, at in ((1, h), (0, st.r - 1 - h)):

            @when(st.d == at, st.live)
            def _(hi=hi):
                rs_desc(seg, t, st, hi).wait_recv()
                add_in(seg, st, hi)
                if h < st.r - 1:
                    rs_desc(seg, t, st, hi).start()

    def ag_first(plan, t, seg):
        st = plan.stages[t]

        @when(st.d == st.r - 1, st.live)
        def _():
            ag_desc(seg, t, st, 1).start()

        @when(st.d == 0, st.live)
        def _():
            ag_desc(seg, t, st, 0).start()

    def ag_phase(plan, t, h, seg):
        st = plan.stages[t]
        for hi, at in ((1, st.r - 1 - h), (0, h)):

            @when(st.d == at, st.live)
            def _(hi=hi):
                ag_desc(seg, t, st, hi).wait_recv()
                if h < st.r - 1:
                    ag_desc(seg, t, st, hi).start()

    def dp_start(segs, which):
        each(segs, lambda s: rs_first(plans[which], 0, s))

    def dp_phase(segs, which, k):
        plan = plans[which]
        hops = [st.r - 1 for st in plan.stages]
        S = len(hops)
        scatter = [(t, h + 1) for t in range(S) for h in range(hops[t])]
        gather = [(t, h + 1) for t in range(S - 1, -1, -1) for h in range(hops[t])]

        def one(seg):
            if k < len(scatter):
                t, h = scatter[k]
                rs_phase(plan, t, h, seg)
                if h == hops[t]:
                    if t + 1 < S:
                        rs_first(plan, t + 1, seg)
                    else:

                        @when(me >= 0, plan.live)
                        def _():
                            own = pl.ds(pl.multiple_of(plan.own, 16), plan.own_size)
                            res[seg, own, :] = g[seg, own, :]

                        ag_first(plan, S - 1, seg)
            else:
                t, h = gather[k - len(scatter)]
                ag_phase(plan, t, h, seg)
                if h == hops[t] and t > 0:
                    ag_first(plan, t - 1, seg)

        each(segs, one)

    PHASES = 2 * sum(r - 1 for _, r in cfg.stages)

    def advance(group, k):
        for i in range(PHASES * (k - 1) // 8, PHASES * k // 8):
            for which in (1, 0):
                dp_phase(group[which], which, i)

    def dp_begin(group):
        for which in (0, 1):
            dp_start(group[which], which)

    def dp_close(segs, which):
        plan = plans[which]

        def one(seg):
            for t, st in enumerate(plan.stages):

                @when(st.d < st.r - 1, st.live)
                def _():
                    rs_desc(seg, t, st, 1).wait_send()
                    ag_desc(seg, t, st, 0).wait_send()

                @when(st.d > 0, st.live)
                def _():
                    rs_desc(seg, t, st, 0).wait_send()
                    ag_desc(seg, t, st, 1).wait_send()

        each(segs, one)

    groups = cfg.groups
    outs = []

    def emit(src, dst):
        c = pltpu.make_async_copy(src, dst, R.out_sem.at[len(outs)])
        c.start()
        outs.append(c)

    def emit_seg(j):
        if j < D // TILE:
            emit(res.at[j], R.gwu.at[:, pl.ds(j * TILE, TILE)])
        elif j < cfg.late:
            emit(res.at[j], R.gwi.at[:, pl.ds((j - D // TILE) * TILE, TILE)])
        elif j == cfg.late:
            for i in range(D // TILE):
                emit(res.at[j, pl.ds(i * G, G)], R.gwo.at[:, pl.ds(i * TILE, TILE)])
        else:
            emit(res.at[j], (R.gwv, R.gwq, R.gwk)[j - cfg.late - 1])

    def emit_group(group):
        for j in range(group[0][0], group[1][1]):
            emit_seg(j)

    partners = [mate]
    for s in cfg.doubling:
        partners.append({"dp": me + s - 2 * s * lax.rem(me // s, 2)})
    smalls = R.small
    small_at = [0]

    def small_desc(i):
        return pltpu.make_async_remote_copy(
            src_ref=smalls.at[i],
            dst_ref=R.sbuf.at[i],
            send_sem=R.s_send.at[i],
            recv_sem=R.s_recv.at[i],
            device_id=partners[i],
            device_id_type=pl.DeviceIdType.MESH,
        )

    def small_step():
        i = small_at[0]
        if i == len(partners):
            return
        small_at[0] = i + 1
        small_desc(i).wait_recv()
        got = R.sbuf[i]
        if i == 0:
            got = jnp.where(lax.broadcasted_iota(jnp.int32, (8, D), 0) < 4, got, 0.0)
        smalls[i + 1] = smalls[i] + got
        if i + 1 < len(partners):
            small_desc(i + 1).start()
        else:
            emit(smalls.at[i + 1], R.gsmall)

    def at_point(i):
        for point, which, k in SCHEDULE:
            if point == i and which == SMALL:
                small_step()
            elif point == i:
                advance(groups[which], k)
                if k == 8:
                    emit_group(groups[which])

    section("slot_counts")
    fill = R.fill[0]
    topk = cfg.K
    rows_at_once = 32
    accs = M // LANES // 4
    loads.idx.wait()
    for h in range(NH):
        at = R.idxv[h]
        hi = at // LANES
        lo = at - hi * LANES
        fld = lax.rem(hi, 4)
        one = jnp.where(fld == 0, 1, jnp.where(fld == 1, 1 << 8, jnp.where(fld == 2, 1 << 16, 1 << 24)))
        R.lo[...] = lo
        for a in range(accs):
            ok = (at < fill) & (hi >= 4 * a) & (hi < 4 * a + 4)
            R.inc[a] = jnp.where(ok, one, 0)

        def count_block(b, c):
            lane = lax.broadcasted_iota(jnp.int32, (rows_at_once, T), 0) + b * rows_at_once
            got = [jnp.zeros((rows_at_once, T), jnp.int32) for _ in range(accs)]
            for k in range(topk):
                hit = jnp.broadcast_to(R.lo[pl.ds(k, 1), :], (rows_at_once, T)) == lane
                for a in range(accs):
                    got[a] = got[a] + jnp.where(hit, jnp.broadcast_to(R.inc[a, pl.ds(k, 1), :], (rows_at_once, T)), 0)
            for a in range(accs):
                R.cntt[a, pl.ds(pl.multiple_of(b * rows_at_once, 16), rows_at_once), :] = got[a]
            return c

        lax.fori_loop(0, LANES // rows_at_once, count_block, 0)
        for a in range(accs):
            R.cnt[h, a] = R.cntt[a].T

    section("first_norm")
    loads.tok.wait()

    def norm_one(i, c):
        for r in range(0, 128, CHUNK):
            rows = pl.ds(pl.multiple_of(i * 128 + r, CHUNK), CHUNK)
            cen, rstd = row_stats(R.tokv[rows, :].astype(F32))
            R.nrm[rows, :] = (cen * rstd * R.g1[...] + R.s1[...]).astype(BF)
        return c

    lax.fori_loop(0, T // 128, norm_one, 0)
    section("projections")
    for copy in (loads.wq, loads.wk, loads.wv):
        copy.wait()
    for rb in range(2):
        rows = pl.ds(rb * HB, HB)
        low = R.nrm[rows, :]
        R.q[rows, :] = nn(low, R.wqkv[:, 0:G]).astype(BF)
        R.kext[pl.ds(T + rb * HB, HB), :] = nn(low, R.wqkv[:, G : 2 * G]).astype(BF)
        R.vext[pl.ds(T + rb * HB, HB), :] = nn(low, R.wqkv[:, 2 * G : W3]).astype(BF)

    section("bias_band")
    band_row = lax.dot_general(
        R.table[...], R.oh[...], (((1,), (0,)), ((), ())), precision=EXACT, preferred_element_type=F32
    )
    u_at = lax.broadcasted_iota(jnp.int32, (NH, KW), 1)
    band_row = jnp.where((u_at >= 1) & (u_at <= T), band_row, NEGATIVE)
    for h in range(NH):
        wide = jnp.broadcast_to(band_row[h : h + 1, :], (HB, KW))
        R.band[h] = pltpu.roll(wide, 0, 1, stride=1, stride_axis=0)

    for j in range(U // LANES):
        R.ibv[:, j * LANES : (j + 1) * LANES] = R.ib[j : j + 1, :].astype(F32)
    mix = jax.nn.sigmoid(R.gate[...])
    section("entry")
    pl.semaphore_wait(barrier, want)

    section("attention_0")
    for copy in (loads.ck, loads.cv, loads.mk, loads.mv, loads.wo):
        copy.wait()

    def attend(rb, h):
        rows = pl.ds(rb * HB, HB)
        cols = slice(h * DH, (h + 1) * DH)
        wide = pl.ds(rb * HB, KW)
        q = R.q[rows, cols]
        raw = nt(q, R.kext[wide, cols])
        for r in range(0, HB, CHUNK):
            s = raw[r : r + CHUNK] * scale + R.band[h, r : r + CHUNK, :]
            e = jnp.exp(s - jnp.max(s, axis=-1, keepdims=True))
            p = e * (1.0 / jnp.sum(e, axis=-1, keepdims=True))
            R.pl[h, pl.ds(rb * HB + r, CHUNK), :] = p.astype(BF)
        near = nn(R.pl[h, rows, :], R.vext[wide, cols])
        raw = nt(q, R.mkv[:, cols])
        for r in range(0, HB, CHUNK):
            at = pl.ds(rb * HB + r, CHUNK)
            fields = []
            for f in range(M // LANES):
                fields.append(((R.cnt[h, f // 4, at, :] >> (8 * (f % 4))) & 255).astype(F32))
            c = jnp.concatenate(fields, axis=1)
            s = jnp.where(c > 0.0, raw[r : r + CHUNK] * scale, NEGATIVE)
            top = jnp.maximum(jnp.max(s, axis=-1, keepdims=True), 0.0)
            e = jnp.exp(s - top) * c
            total = jnp.exp(-top) + jnp.sum(e, axis=-1, keepdims=True)
            R.pm[h, at, :] = (e * (1.0 / total)).astype(BF)
        far = nn(R.pm[h, rows, :], R.mvv[:, cols])
        m = mix[:, h : h + 1]
        R.diff[rows, cols] = far - near
        R.joined[rows, cols] = (m * far + (1.0 - m) * near).astype(BF)

    def project(rb):
        rows = pl.ds(rb * HB, HB)
        for j in range(D // TILE):
            cols = slice(j * TILE, (j + 1) * TILE)
            R.part[0, rows, cols] = nn(R.joined[rows, :], R.wov[:, cols]).astype(BF)

    for h in range(NH):
        attend(0, h)
    project(0)
    push(0, 0)
    section("attention_1")
    for h in range(NH):
        attend(1, h)
        if h == 0:
            mid(0, 0)
    project(1)
    push(0, 1)

    for copy in (loads.og, loads.wu, loads.wi):
        copy.wait()

    def tiles(count, fn):
        lax.fori_loop(0, count, lambda j, c: (fn(pl.ds(pl.multiple_of(j * TILE, TILE), TILE)), c)[1], 0)

    def feed_back(hf):
        rows = pl.ds(hf * HB, HB)

        def back_one(cols):
            R.ga[rows, cols] = nt(R.ogv[rows, :], R.wuv[cols, :])

        tiles(U // TILE, back_one)

    def second_norm(hf):
        def visit(rows, mine, total):
            x = R.tokv[rows, :].astype(F32) + total
            R.resid[mine, :] = x
            cen, rstd = row_stats(x)
            R.ntl[rows, :] = (cen * rstd * R.g2[...] + R.s2[...]).astype(BF)

        fin(0, hf, visit)
        share_desc(0, hf, R.ntl, core).start()

    def feed(hf):
        rows = pl.ds(hf * HB, HB)

        def unit(cols):
            pre = nn(R.ntl[rows, :], R.wiv[:, cols])
            bias = R.ibv[:, cols]
            sums = jnp.zeros((1, TILE), F32)
            for r in range(0, HB, CHUNK):
                at = pl.ds(hf * HB + r, CHUNK)
                x = pre[r : r + CHUNK] + bias
                x2 = x * x
                t = jnp.tanh(GELU_A * (x + GELU_B * x * x2))
                R.act[at, cols] = (0.5 * x * (1.0 + t)).astype(BF)
                slope = 0.5 * (1.0 + t) + 0.5 * x * (1.0 - t * t) * (GELU_A * (1.0 + 3.0 * GELU_B * x2))
                gi = (R.ga[at, cols] * slope).astype(BF)
                R.gi[at, cols] = gi
                sums = sums + jnp.sum(gi.astype(F32), axis=0, keepdims=True)
            R.gib[pl.ds(hf, 1), cols] = sums
            R.tr[cols, rows] = R.act[rows, cols].T

        tiles(U // TILE, unit)

        def back(cols):
            R.part[1, rows, cols] = nt(R.gi[rows, :], R.wiv[cols, :]).astype(BF)

        tiles(D // TILE, back)

    section("feed_back")
    feed_back(0)
    mid(0, 1)
    feed_back(1)
    section("second_norm_0")
    second_norm(0)
    share_desc(0, 0, R.ntl, 1 - core).wait_recv()
    section("feed_0")
    feed(0)
    push(1, 0)
    section("second_norm_1")
    second_norm(1)
    mid(1, 0)
    share_desc(0, 1, R.ntl, 1 - core).wait_recv()
    section("feed_1")
    feed(1)
    push(1, 1)

    def start_one(j):
        group = groups[0] if j < D // TILE else groups[1]
        dp_start((j, j + 1), 0 if j < group[0][1] else 1)

    section("outer_grads")
    for j in range(D // TILE):
        g[j] = nn(R.tr[...], R.ogv[:, j * TILE : (j + 1) * TILE]).astype(BF)
        start_one(j)
        if j == 1:
            mid(1, 1)
    section("inner_grads")
    R.tr[...] = R.ntl[...].T
    for j in range(U // TILE):
        g[D // TILE + j] = nn(R.tr[...], R.gi[:, j * TILE : (j + 1) * TILE]).astype(BF)
        start_one(D // TILE + j)
    section("fed")
    sent(0)
    for hf in range(HALVES):
        rows = pl.ds(hf * HB, HB)

        def fed(cols, rows=rows):
            R.part[0, rows, cols] = nn(R.act[rows, :], R.wuv[:, cols]).astype(BF)

        tiles(D // TILE, fed)
        push(2, hf)

    def norm_back(p, hf, source, gain, base, keep, out):
        gain_sum, shift_sum = [jnp.zeros((1, D), F32)], [jnp.zeros((1, D), F32)]

        def visit(rows, mine, dy):
            cen, rstd = row_stats(source(rows, mine))
            xh = cen * rstd
            gain_sum[0] = gain_sum[0] + jnp.sum(dy * xh, axis=0, keepdims=True)
            shift_sum[0] = shift_sum[0] + jnp.sum(dy, axis=0, keepdims=True)
            dx = dy * gain
            dx = rstd * (
                dx - jnp.mean(dx, axis=-1, keepdims=True) - xh * jnp.mean(dx * xh, axis=-1, keepdims=True)
            )
            got = base(rows, mine) + dx
            if keep is not None:
                keep[mine, :] = got
            out[rows, :] = got.astype(BF)

        fin(p, hf, visit)
        share_desc(p, hf, out, core).start()
        return gain_sum[0], shift_sum[0]

    section("second_norm_back")
    sums = [
        norm_back(
            1, hf, lambda rows, mine: R.resid[mine, :], R.g2[...],
            lambda rows, mine: R.ogv[rows, :].astype(F32), R.gres, R.gat,
        )
        for hf in range(HALVES)
    ]
    R.small[0, 2:3, :] = sums[0][0] + sums[1][0]
    R.small[0, 3:4, :] = sums[0][1] + sums[1][1]
    for hf in range(HALVES):
        mid(2, hf)
    section("gather_rows")
    at_point(5)
    for hf in range(HALVES):
        share_desc(1, hf, R.gat, 1 - core).wait_recv()

    section("grad_joined")
    gate_sums = [jnp.zeros((1, 1), F32) for _ in range(NH)]
    for rb in range(2):
        rows = pl.ds(rb * HB, HB)
        gj = nt(R.gat[rows, :], R.wov[...])
        for h in range(NH):
            cols = slice(h * DH, (h + 1) * DH)
            m = mix[:, h : h + 1]
            gate_sums[h] = gate_sums[h] + jnp.sum(
                jnp.sum(gj[:, cols] * R.diff[rows, cols], axis=0, keepdims=True), axis=1, keepdims=True
            )
            R.gl[rows, cols] = ((1.0 - m) * gj[:, cols]).astype(BF)
            R.gm[rows, cols] = (m * gj[:, cols]).astype(BF)

    def own_keys(weights, other, out):
        for h in range(NH):
            cols = slice(h * DH, (h + 1) * DH)
            spot = slice(out * G + h * DH, out * G + (h + 1) * DH)
            top = tn(weights[h, 0:HB, T:KW], other[0:HB, cols]) + tn(weights[h, HB:T, HB:T], other[HB:T, cols])
            R.gqkv[0:HB, spot] = top.astype(BF)
            R.gqkv[HB:T, spot] = tn(weights[h, HB:T, T:KW], other[HB:T, cols]).astype(BF)

    def weight_seg(seg, out):
        g[seg] = nn(R.tr[...], R.gqkv[:, out * G : (out + 1) * G]).astype(BF)

    LATE = cfg.late
    for j in range(D // TILE):
        g[LATE, j * G : (j + 1) * G, :] = tn(R.joined[...], R.gat[:, j * TILE : (j + 1) * TILE]).astype(BF)
    dp_start((LATE, LATE + 1), 0)
    R.tr[...] = R.nrm[...].T
    own_keys(R.pl, R.gl, 2)
    weight_seg(LATE + 1, 2)
    dp_start((LATE + 1, LATE + 2), 1)
    section("point_7")
    at_point(7)
    for rb in range(2):
        rows = pl.ds(rb * HB, HB)
        wide = pl.ds(rb * HB, KW)
        for h in range(NH):
            section("attention_back")
            cols = slice(h * DH, (h + 1) * DH)
            dp = nt(R.gl[rows, cols], R.vext[wide, cols])
            for r in range(0, HB, CHUNK):
                at = pl.ds(rb * HB + r, CHUNK)
                p, d = R.pl[h, at, :].astype(F32), dp[r : r + CHUNK]
                ds = p * (d - jnp.sum(p * d, axis=-1, keepdims=True))
                if rb == 0:
                    R.band[h, pl.ds(r, CHUNK), :] = ds
                else:
                    R.band[h, pl.ds(r, CHUNK), :] += ds
                R.pl[h, at, :] = (ds * scale).astype(BF)
            gq = nn(R.pl[h, rows, :], R.kext[wide, cols])
            dp = nt(R.gm[rows, cols], R.mvv[:, cols])
            for r in range(0, HB, CHUNK):
                at = pl.ds(rb * HB + r, CHUNK)
                p, d = R.pm[h, at, :].astype(F32), dp[r : r + CHUNK]
                ds = p * (d - jnp.sum(p * d, axis=-1, keepdims=True))
                R.pm[h, at, :] = (ds * scale).astype(BF)
            gq = gq + nn(R.pm[h, rows, :], R.mkv[:, cols])
            R.gqkv[rows, cols] = gq.astype(BF)
            section("point_8")
            at_point(8 + (rb * NH + h) * 4 // (2 * NH))

    section("late_grads")
    weight_seg(LATE + 2, 0)
    dp_start((LATE + 2, LATE + 3), 0)
    own_keys(R.pl, R.q, 1)
    weight_seg(LATE + 3, 1)
    dp_start((LATE + 3, LATE + 4), 1)
    section("point_13")
    at_point(13)
    section("back_in")
    sent(1)
    for hf in range(HALVES):
        rows = pl.ds(hf * HB, HB)

        def back_in(cols, rows=rows):
            R.part[1, rows, cols] = nt(R.gqkv[rows, :], R.wqkv[cols, :]).astype(BF)

        tiles(D // TILE, back_in)
        push(3, hf)

    section("block_output")
    for hf in range(HALVES):

        def result(rows, mine, total):
            R.bo[rows, :] = (R.resid[mine, :] + total).astype(BF)

        fin(2, hf, result)
        share_desc(2, hf, R.bo, core).start()
    section("point_14")
    at_point(14)
    for hf in range(HALVES):
        mid(3, hf)
    section("point_15")
    at_point(15)

    section("bias_table")
    at_row = lax.broadcasted_iota(jnp.int32, (8, KW), 0)
    table_grads = []
    for h in range(NH):
        half = HB
        cur = R.band[h]
        while half > 8:
            half //= 2
            cur = cur[:half] + pltpu.roll(cur[half:], KW - half, 1)
        for bit in (1, 2, 4):
            cur = jnp.where(lax.rem(at_row // bit, 2) == 1, pltpu.roll(cur, KW - bit, 1), cur)
        diag = jnp.sum(cur, axis=0, keepdims=True)
        table_grads.append(
            lax.dot_general(diag, R.oh[...], (((1,), (1,)), ((), ())), precision=EXACT, preferred_element_type=F32)
        )
    smalls[0, 4:5, :] = R.gib[0:1, :] + R.gib[1:2, :]
    smalls[0, 5:8, :] = jnp.zeros((3, D), F32)
    for h in range(NH):
        s = mix[:, h : h + 1]
        smalls[0, 5:6, h * LANES : h * LANES + NB] = table_grads[h]
        smalls[0, 6:7, h * LANES : (h + 1) * LANES] = jnp.broadcast_to(gate_sums[h] * s * (1.0 - s), (1, LANES))

    section("first_norm_back")
    sums = [
        norm_back(
            3, hf, lambda rows, mine: R.tokv[rows, :].astype(F32), R.g1[...],
            lambda rows, mine: R.gres[mine, :], None, R.gt,
        )
        for hf in range(HALVES)
    ]
    smalls[0, 0:1, :] = sums[0][0] + sums[1][0]
    smalls[0, 1:2, :] = sums[0][1] + sums[1][1]
    small_desc(0).start()
    section("point_16")
    at_point(16)

    for hf in range(HALVES):
        share_desc(2, hf, R.bo, 1 - core).wait_recv()
        share_desc(3, hf, R.gt, 1 - core).wait_recv()
    emit(R.bo, R.block_out)
    emit(R.gt, R.gtok)
    section("point_17")
    at_point(17)
    for _ in partners:
        small_step()

    section("close")
    sent(2)
    sent(3)
    for p in range(4):
        for hf in range(HALVES):
            share_desc(p, hf, (R.ntl, R.gat, R.bo, R.gt)[p], core).wait_send()
    for i in range(len(partners)):
        small_desc(i).wait_send()
    for group in groups:
        for which in (0, 1):
            dp_close(group[which], which)
    for c in outs:
        c.wait()
    section(None)


def local(n, tokens, wq, wk, wv, wo, wi, ib, wu, g1, s1, g2, s2, table, gate, ck, cv, mk, mv, idx, fill, og):
    T, D = tokens.shape
    NH = table.shape[0]
    G = wq.shape[1]
    U = wi.shape[1]
    M = mk.shape[1]
    K = idx.shape[2]
    HB = T // 2
    KW = T + HB
    stages = stage_list(n)
    doubling = []
    s = 1
    while s < n:
        doubling.append(s)
        s *= 2
    ffn = (D + U) // TILE
    late = 1 + 3 * G // TILE
    nseg = ffn + late
    groups = []
    for lo, count in ((0, D // TILE), (D // TILE, U // TILE), (ffn, 2), (ffn + 2, 2)):
        half = lo + count // 2
        groups.append(((lo, half), (half, lo + count)))
    seg = D
    orders = (stages, stages[::-1])
    rows_needed = 0
    for order in orders:
        off, length = 0, seg
        for _, r in order:
            length //= 2
            off += (1 if r == 2 else 2) * length
        rows_needed = max(rows_needed, off)
    inputs = dict(
        tok=tokens, idx=idx.transpose(1, 2, 0), wq=wq, wk=wk, wv=wv, wo=wo, wi=wi, wu=wu, ck=ck, cv=cv, mk=mk, mv=mv, og=og
    )
    vectors = dict(
        ib=ib.reshape(U // LANES, LANES), g1=g1.reshape(1, D), s1=s1.reshape(1, D), g2=g2.reshape(1, D), s2=s2.reshape(1, D),
        table=table, gate=gate.reshape(1, NH), oh=jnp.asarray(bucket_rows(T)),
    )
    outputs = dict(
        block_out=((T, D), BF), gtok=((T, D), BF), gwq=((D, G), BF), gwk=((D, G), BF), gwv=((D, G), BF),
        gwo=((G, D), BF), gwi=((D, U), BF), gwu=((U, D), BF), gsmall=((8, D), F32),
    )
    S = len(stages)
    sem = pltpu.SemaphoreType.DMA
    scratch = dict(
        tokv=pltpu.VMEM((T, D), BF), ogv=pltpu.VMEM((T, D), BF), idxv=pltpu.VMEM((NH, K, T), jnp.int32),
        wqkv=pltpu.VMEM((D, 3 * G), BF), wov=pltpu.VMEM((G, D), BF), wiv=pltpu.VMEM((D, U), BF),
        wuv=pltpu.VMEM((U, D), BF), kext=pltpu.VMEM((2 * T, G), BF), vext=pltpu.VMEM((2 * T, G), BF),
        mkv=pltpu.VMEM((M, G), BF), mvv=pltpu.VMEM((M, G), BF),
        lo=pltpu.VMEM((K, T), jnp.int32), inc=pltpu.VMEM((M // LANES // 4, K, T), jnp.int32),
        cntt=pltpu.VMEM((M // LANES // 4, LANES, T), jnp.int32),
        cnt=pltpu.VMEM((NH, M // LANES // 4, T, LANES), jnp.int32),
        nrm=pltpu.VMEM((T, D), BF), q=pltpu.VMEM((T, G), BF), band=pltpu.VMEM((NH, HB, KW), F32),
        pl=pltpu.VMEM((NH, T, KW), BF), pm=pltpu.VMEM((NH, T, M), BF), diff=pltpu.VMEM((T, G), F32),
        joined=pltpu.VMEM((T, G), BF), ga=pltpu.VMEM((T, U), F32), ntl=pltpu.VMEM((T, D), BF),
        resid=pltpu.VMEM((HB, D), F32), act=pltpu.VMEM((T, U), BF), gi=pltpu.VMEM((T, U), BF),
        gib=pltpu.VMEM((8, U), F32), ibv=pltpu.VMEM((1, U), F32), tr=pltpu.VMEM((D, T), BF), gres=pltpu.VMEM((HB, D), F32),
        gat=pltpu.VMEM((T, D), BF), gl=pltpu.VMEM((T, G), BF), gm=pltpu.VMEM((T, G), BF),
        gqkv=pltpu.VMEM((T, 3 * G), BF), bo=pltpu.VMEM((T, D), BF), gt=pltpu.VMEM((T, D), BF),
        part=pltpu.VMEM((2, T, D), BF), cbuf=pltpu.VMEM((2, HB, D), BF), ybuf=pltpu.VMEM((2, HB, D), BF),
        small=pltpu.VMEM((len(doubling) + 2, 8, D), F32), sbuf=pltpu.VMEM((len(doubling) + 1, 8, D), F32),
        g=pltpu.VMEM((nseg, seg, TILE), BF), res=pltpu.VMEM((nseg, seg, TILE), BF),
        rbuf=pltpu.VMEM((nseg, rows_needed, TILE), BF),
        in_sem=sem((13,)), out_sem=sem((2 + 2 * (D // TILE) + U // TILE + 4,)),
        c_send=sem((4, HALVES)), c_recv=sem((4, HALVES)), y_send=sem((4, HALVES)), y_recv=sem((4, HALVES)),
        a_send=sem((4, HALVES)), a_recv=sem((4, HALVES)),
        s_send=sem((len(doubling) + 1,)), s_recv=sem((len(doubling) + 1,)),
        rs_send=sem((nseg, S, 2)), rs_recv=sem((nseg, S, 2)),
        ag_send=sem((nseg, S, 2)), ag_recv=sem((nseg, S, 2)),
    )
    cfg = Space(
        n=n, T=T, D=D, G=G, U=U, M=M, NH=NH, K=K, stages=stages, doubling=doubling, seg=seg, orders=orders,
        groups=groups, late=ffn,
        names=[*inputs, *vectors, "fill", *outputs, *scratch],
    )
    any_spec = pl.BlockSpec(memory_space=pl.ANY)
    vec_spec = pl.BlockSpec(memory_space=pltpu.VMEM)
    outs = pl.pallas_call(
        functools.partial(kernel, cfg),
        out_shape=[jax.ShapeDtypeStruct(*v) for v in outputs.values()],
        in_specs=[any_spec] * len(inputs) + [vec_spec] * len(vectors) + [pl.BlockSpec(memory_space=pltpu.SMEM)],
        out_specs=[any_spec] * len(outputs),
        scratch_shapes=list(scratch.values()),
        compiler_params=pltpu.CompilerParams(
            collective_id=0, has_side_effects=True, vmem_limit_bytes=63 * MIB
        ),
        cost_estimate=pl.CostEstimate(flops=12 * 10**9, bytes_accessed=20 * 10**6, transcendentals=3 * 10**6),
    )(
        *inputs.values(), *vectors.values(), fill,
    )
    return widen(outs, NH)


def widen_kernel(NH, cuts, *refs):
    ins, outs, scratch = refs[:9], refs[9:24], refs[24:]
    boxes = len(cuts)
    low, (in_sem, out_sem), high = scratch[:boxes], scratch[boxes : boxes + 2], list(scratch[boxes + 2 :])
    high = [low[n] if cut[0] < 2 else high.pop(0) for n, cut in enumerate(cuts)]
    loads, stores = [], []
    for n, (i, at, rows, cols) in enumerate(cuts):
        loads.append(pltpu.make_async_copy(ins[i].at[pl.ds(at, rows)], low[n], in_sem.at[n]))
        stores.append(pltpu.make_async_copy(high[n], outs[i].at[pl.ds(at, rows)], out_sem.at[n]))
        loads[n].start()
    small = ins[8]
    for i in range(5):
        outs[8 + i][...] = small[i : i + 1, :]
    for h in range(NH):
        outs[13][h : h + 1, :] = small[5:6, h * LANES : h * LANES + NB]
        outs[14][:, h : h + 1] = small[6:7, h * LANES : h * LANES + 1]
    for n, (i, at, rows, cols) in enumerate(cuts):
        loads[n].wait()
        if high[n] is not low[n]:
            high[n][...] = low[n][...].astype(F32)
        stores[n].start()
    for c in stores:
        c.wait()


def widen(sums, NH):
    small = sums[8]
    D = small.shape[1]
    cuts = []
    for i in (2, 3, 4, 5, 6, 7, 0, 1):
        rows, cols = sums[i].shape
        step = max(8, min(rows, TILE * D // cols))
        cuts += [(i, at, step, cols) for at in range(0, rows, step)]
    shapes = [jax.ShapeDtypeStruct(x.shape, BF if i < 2 else F32) for i, x in enumerate(sums[:8])]
    tiny = [(1, D)] * 5 + [(NH, NB), (1, NH)]
    hbm = pl.BlockSpec(memory_space=pl.ANY)
    vec = pl.BlockSpec(memory_space=pltpu.VMEM)
    got = pl.pallas_call(
        functools.partial(widen_kernel, NH, cuts),
        in_specs=[hbm] * 8 + [vec],
        out_specs=[hbm] * 8 + [vec] * len(tiny),
        out_shape=shapes + [jax.ShapeDtypeStruct(x, F32) for x in tiny],
        scratch_shapes=[pltpu.VMEM((rows, cols), BF) for _, _, rows, cols in cuts]
        + [pltpu.SemaphoreType.DMA((len(cuts),))] * 2
        + [pltpu.VMEM((rows, cols), F32) for i, _, rows, cols in cuts if i >= 2],
        compiler_params=pltpu.CompilerParams(vmem_limit_bytes=60 * MIB),
        cost_estimate=pl.CostEstimate(flops=0, bytes_accessed=22 * 10**6, transcendentals=0),
    )(*sums)
    block_out, gtok, gwq, gwk, gwv, gwo, gwi, gwu, g1, s1, g2, s2, ib, bias, gates = got
    return (
        block_out, gtok, gwq, gwk, gwv, gwo, gwi, ib.reshape(-1), gwu, g1.reshape(D), s1.reshape(D), g2.reshape(D),
        s2.reshape(D), bias, gates.reshape(NH),
    )


def solution(mesh):
    return jax.shard_map(
        functools.partial(local, mesh.shape["dp"]),
        mesh=mesh,
        in_specs=(
            P("dp", None), P(None, "head"), P(None, "head"), P(None, "head"), P("head", None), P(None, "head"),
            P("head"), P("head", None), P(), P(), P(), P(), P("head", None), P("head"), P("dp", "head"),
            P("dp", "head"), P("dp", None, "head"), P("dp", None, "head"), P("dp", "head", None), P("dp"),
            P("dp", None),
        ),
        out_specs=(
            P("dp", None), P("dp", None), P(None, "head"), P(None, "head"), P(None, "head"), P("head", None),
            P(None, "head"), P("head"), P("head", None), P(), P(), P(), P(), P("head", None), P("head"),
        ),
        check_vma=False,
    )
```

```python
import functools
import math
from types import SimpleNamespace as Space

import jax
import jax.numpy as jnp
import numpy as np
from jax import lax
from jax.experimental import pallas as pl
from jax.experimental.pallas import tpu as pltpu
from jax.sharding import PartitionSpec as P

NB = 32
MAXD = 128
EPSILON = 1e-05
NEGATIVE = -1e30
EXACT = lax.Precision.HIGHEST
BF = jnp.bfloat16
F32 = jnp.float32
LANES = 128
TILE = 256
HALVES = 2
CHUNK = 32
MIB = 1 << 20
ORDERS = (0, 0, 0, 1, 0, 0, 0, 1, 1, 0, 0, 1)
LAST_POINT = 30
SCHEDULE = (
    (2, 0, 1), (3, 3, 1), (4, 7, 1), (4, 1, 1), (6, 3, 2), (6, 2, 1), (6, 1, 2), (6, 0, 2), (8, 7, 2),
    (8, 4, 1), (8, 2, 2), (8, 1, 3), (9, 3, 3), (10, 8, 1), (10, 5, 1), (10, 0, 3), (11, 4, 2), (11, 7, 3),
    (11, 2, 3), (12, 6, 1), (12, 5, 2), (12, 1, 4), (13, 8, 2), (14, 6, 2), (14, 4, 3), (14, 9, 1), (14, 0, 4),
    (15, 5, 3), (15, 3, 4), (15, 2, 4), (15, 1, 5), (16, 9, 2), (16, 6, 3), (17, 8, 3), (17, 7, 4), (17, 1, 6),
    (17, 0, 5), (18, 3, 5), (19, 4, 4), (19, 9, 3), (19, 2, 5), (20, 8, 4), (21, 5, 4), (21, 0, 6), (22, 7, 5),
    (22, 6, 4), (22, 3, 6), (23, 2, 6), (24, 4, 5), (24, 1, 7), (25, 10, 1), (25, 9, 4), (26, 8, 5), (26, 3, 7),
    (26, 0, 7), (26, 11, 1), (27, 4, 6), (27, 2, 7), (27, 5, 5), (28, 1, 8), (29, 11, 2), (30, 7, 6), (30, 3, 8),
    (30, 5, 6), (30, 0, 8), (30, 6, 5), (30, 4, 7), (30, 10, 2), (30, 7, 7), (30, 2, 8), (30, 11, 3), (30, 9, 5),
    (30, 6, 6), (30, 5, 7), (30, 10, 3), (30, 4, 8), (30, 8, 6), (30, 9, 6), (30, 11, 4), (30, 7, 8), (30, 6, 7),
    (30, 8, 7), (30, 5, 8), (30, 10, 4), (30, 11, 5), (30, 9, 7), (30, 10, 5), (30, 10, 6), (30, 6, 8), (30, 8, 8),
    (30, 11, 6), (30, 10, 7), (30, 11, 7), (30, 9, 8), (30, 11, 8), (30, 10, 8),
)
GELU_A = math.sqrt(2.0 / math.pi)
GELU_B = 0.044715


def bucket_rows(length):
    span = np.arange(length)
    exact = NB // 2
    ratio = np.log(np.maximum(span, 1) / exact) / np.log(MAXD / exact)
    larger = np.minimum(exact + (ratio * (NB - exact)).astype(np.int32), NB - 1)
    bucket = np.where(span < exact, span, larger).astype(np.int32)
    table = np.zeros((NB, length + length // 2), np.float32)
    for u in range(1, length + 1):
        table[bucket[length - u], u] = 1.0
    return table


def nn(a, b):
    return lax.dot_general(a, b, (((1,), (0,)), ((), ())), preferred_element_type=F32)


def nt(a, b):
    return lax.dot_general(a, b, (((1,), (1,)), ((), ())), preferred_element_type=F32)


def tn(a, b):
    return lax.dot_general(a, b, (((0,), (0,)), ((), ())), preferred_element_type=F32)


def row_stats(x):
    mean = jnp.mean(x, axis=-1, keepdims=True)
    c = x - mean
    var = jnp.mean(c * c, axis=-1, keepdims=True)
    return c, lax.rsqrt(var + EPSILON)


def stage_list(n):
    stages, stride, left = [], 1, n
    if left >= 2:
        stages.append((1, 2))
        stride, left = 2, left // 2
    while left >= 4:
        stages.append((stride, 4))
        stride, left = stride * 4, left // 4
    if left == 2:
        stages.append((stride, 2))
    return stages


def kernel(cfg, *refs):
    n = cfg.n
    R = Space(**dict(zip(cfg.names, refs)))
    T, D, G, U, M, NH = cfg.T, cfg.D, cfg.G, cfg.U, cfg.M, cfg.NH
    DH = G // NH
    HB = T // 2
    KW = T + HB
    scale = 1.0 / math.sqrt(DH)
    me = lax.axis_index("dp")
    hid = lax.axis_index("head")
    core = lax.rem(hid, 2)
    mate = {"head": hid + 1 - 2 * core}
    across = {"head": lax.rem(hid + 2, 4)}
    sub = HB // 2

    peers = []
    for stride, r in cfg.stages:
        d = lax.rem(me // stride, r)
        peers.append((d > 0, me - stride))
        peers.append((d < r - 1, me + stride))
    for s in cfg.doubling:
        covered = False
        for stride, r in cfg.stages:
            if s == stride:
                covered = True
        if not covered:
            b = lax.rem(me // s, 2)
            peers.append((True, me + s - 2 * s * b))
    barrier = pltpu.get_barrier_semaphore()
    want = 2
    pl.semaphore_signal(barrier, inc=1, device_id=mate)
    pl.semaphore_signal(barrier, inc=1, device_id=across)
    for cond, who in peers:
        if cond is True:
            pl.semaphore_signal(barrier, inc=1, device_id={"dp": who})
            want = want + 1
        else:

            @pl.when(cond)
            def _(who=who):
                pl.semaphore_signal(barrier, inc=1, device_id={"dp": who})

            want = want + jnp.where(cond, 1, 0).astype(jnp.int32)

    W3 = 3 * G
    loads = Space()

    def load(src, dst, sem):
        copy = pltpu.make_async_copy(src, dst, R.in_sem.at[sem])
        copy.start()
        return copy

    loads.tok = load(R.tok, R.tokv, 0)
    loads.idx = load(R.idx, R.idxv, 1)
    loads.wq = load(R.wq, R.wqkv.at[:, pl.ds(0, G)], 2)
    loads.wk = load(R.wk, R.wqkv.at[:, pl.ds(G, G)], 3)
    loads.wv = load(R.wv, R.wqkv.at[:, pl.ds(2 * G, G)], 4)
    loads.ck = load(R.ck, R.kext.at[pl.ds(0, T)], 5)
    loads.cv = load(R.cv, R.vext.at[pl.ds(0, T)], 6)
    loads.mk = load(R.mk.at[0], R.mkv, 7)
    loads.mv = load(R.mv.at[0], R.mvv, 8)
    loads.wo = load(R.wo, R.wov, 9)
    loads.og = load(R.og, R.ogv, 10)
    loads.wu = load(R.wu, R.wuv, 11)
    loads.wi = load(R.wi, R.wiv, 12)


    def part_rows(hf, c):
        return pl.ds(pl.multiple_of(hf * HB + c * sub, sub), sub)

    def push_desc(p, hf):
        return pltpu.make_async_remote_copy(
            src_ref=R.part.at[p % 2, part_rows(hf, 1 - core)],
            dst_ref=R.cbuf.at[p % 2, pl.ds(hf * sub, sub)],
            send_sem=R.c_send.at[p, hf],
            recv_sem=R.c_recv.at[p, hf],
            device_id=mate,
            device_id_type=pl.DeviceIdType.MESH,
        )

    def cross_desc(p, hf):
        return pltpu.make_async_remote_copy(
            src_ref=R.part.at[p % 2, part_rows(hf, core)],
            dst_ref=R.ybuf.at[p % 2, pl.ds(hf * sub, sub)],
            send_sem=R.y_send.at[p, hf],
            recv_sem=R.y_recv.at[p, hf],
            device_id=across,
            device_id_type=pl.DeviceIdType.MESH,
        )

    def share_desc(p, hf, buf, c):
        rows = part_rows(hf, c)
        return pltpu.make_async_remote_copy(
            src_ref=buf.at[rows],
            dst_ref=buf.at[rows],
            send_sem=R.a_send.at[p, hf],
            recv_sem=R.a_recv.at[p, hf],
            device_id=mate,
            device_id_type=pl.DeviceIdType.MESH,
        )

    def push(p, hf):
        push_desc(p, hf).start()

    def mid(p, hf):
        push_desc(p, hf).wait_recv()
        for r in range(0, sub, CHUNK):
            rows = pl.ds(pl.multiple_of(hf * HB + core * sub + r, CHUNK), CHUNK)
            total = R.part[p % 2, rows, :].astype(F32) + R.cbuf[p % 2, pl.ds(hf * sub + r, CHUNK), :].astype(F32)
            R.part[p % 2, rows, :] = total.astype(BF)
        cross_desc(p, hf).start()

    def sent(p):
        for hf in range(HALVES):
            push_desc(p, hf).wait_send()
            cross_desc(p, hf).wait_send()

    def fin(p, hf, visit):
        cross_desc(p, hf).wait_recv()
        for r in range(0, sub, CHUNK):
            rows = pl.ds(pl.multiple_of(hf * HB + core * sub + r, CHUNK), CHUNK)
            mine = pl.ds(hf * sub + r, CHUNK)
            visit(rows, mine, R.part[p % 2, rows, :].astype(F32) + R.ybuf[p % 2, mine, :].astype(F32))

    RS_R, RS_S, AG_R, AG_S = R.rs_recv, R.rs_send, R.ag_recv, R.ag_send
    g, res, rbuf = R.g, R.res, R.rbuf
    SEG = cfg.seg

    plans = []
    for order in cfg.orders:
        base, size, off, live, plan = 0, SEG, 0, None, []
        for stride, r in order:
            d = lax.rem(me // stride, r)
            size = size // 2
            low_slot = off
            high_slot = off if r == 2 else off + size
            off = high_slot + size
            plan.append(
                Space(stride=stride, r=r, d=d, base=base, size=size, slots=(low_slot, high_slot), live=live)
            )
            base = base + size * (d // (r - 1))
            if r > 2:
                ends = (d == 0) | (d == r - 1)
                live = ends if live is None else live & ends
        plans.append(Space(stages=plan, own=base, own_size=size, live=live))

    def when(cond, live):
        return pl.when(cond if live is None else cond & live)

    def piece(st, hi, at=0, rows=None):
        first = st.base + hi * st.size + at
        return pl.ds(first if isinstance(first, int) else pl.multiple_of(first, 16), rows or st.size)

    def hop(st, right):
        return {"dp": me + st.stride if right else me - st.stride}

    def rs_desc(seg, t, st, hi):
        return pltpu.make_async_remote_copy(
            src_ref=g.at[seg, piece(st, hi)],
            dst_ref=rbuf.at[seg, pl.ds(st.slots[hi], st.size)],
            send_sem=RS_S.at[seg, t, hi],
            recv_sem=RS_R.at[seg, t, hi],
            device_id=hop(st, hi == 1),
            device_id_type=pl.DeviceIdType.MESH,
        )

    def ag_desc(seg, t, st, hi):
        return pltpu.make_async_remote_copy(
            src_ref=res.at[seg, piece(st, hi)],
            dst_ref=res.at[seg, piece(st, hi)],
            send_sem=AG_S.at[seg, t, hi],
            recv_sem=AG_R.at[seg, t, hi],
            device_id=hop(st, hi == 0),
            device_id_type=pl.DeviceIdType.MESH,
        )

    def add_in(seg, st, hi):
        step = min(64, st.size)
        for i in range(0, st.size, step):
            rows = piece(st, hi, i, step)
            total = g[seg, rows, :].astype(F32) + rbuf[seg, pl.ds(st.slots[hi] + i, step), :].astype(F32)
            g[seg, rows, :] = total.astype(BF)

    def rs_first(plan, t, seg):
        st = plan.stages[t]

        @when(st.d == 0, st.live)
        def _():
            rs_desc(seg, t, st, 1).start()

        @when(st.d == st.r - 1, st.live)
        def _():
            rs_desc(seg, t, st, 0).start()

    def rs_phase(plan, t, h, seg):
        st = plan.stages[t]
        for hi, at in ((1, h), (0, st.r - 1 - h)):

            @when(st.d == at, st.live)
            def _(hi=hi):
                rs_desc(seg, t, st, hi).wait_recv()
                add_in(seg, st, hi)
                if h < st.r - 1:
                    rs_desc(seg, t, st, hi).start()

    def ag_first(plan, t, seg):
        st = plan.stages[t]

        @when(st.d == st.r - 1, st.live)
        def _():
            ag_desc(seg, t, st, 1).start()

        @when(st.d == 0, st.live)
        def _():
            ag_desc(seg, t, st, 0).start()

    def ag_phase(plan, t, h, seg):
        st = plan.stages[t]
        for hi, at in ((1, st.r - 1 - h), (0, h)):

            @when(st.d == at, st.live)
            def _(hi=hi):
                ag_desc(seg, t, st, hi).wait_recv()
                if h < st.r - 1:
                    ag_desc(seg, t, st, hi).start()

    def dp_phase(seg, which, k):
        plan = plans[which]
        hops = [st.r - 1 for st in plan.stages]
        S = len(hops)
        scatter = [(t, h + 1) for t in range(S) for h in range(hops[t])]
        gather = [(t, h + 1) for t in range(S - 1, -1, -1) for h in range(hops[t])]
        if k < len(scatter):
            t, h = scatter[k]
            rs_phase(plan, t, h, seg)
            if h == hops[t] and t + 1 < S:
                rs_first(plan, t + 1, seg)
            elif h == hops[t]:

                @when(me >= 0, plan.live)
                def _():
                    own = pl.ds(pl.multiple_of(plan.own, 16), plan.own_size)
                    res[seg, own, :] = g[seg, own, :]

                ag_first(plan, S - 1, seg)
        else:
            t, h = gather[k - len(scatter)]
            ag_phase(plan, t, h, seg)
            if h == hops[t] and t > 0:
                ag_first(plan, t - 1, seg)

    PHASES = 2 * sum(r - 1 for _, r in cfg.stages)

    def advance(seg, k):
        for i in range(PHASES * (k - 1) // 8, PHASES * k // 8):
            dp_phase(seg, ORDERS[seg], i)

    def dp_begin(seg):
        rs_first(plans[ORDERS[seg]], 0, seg)

    def dp_close(seg):
        for t, st in enumerate(plans[ORDERS[seg]].stages):

            @when(st.d < st.r - 1, st.live)
            def _():
                rs_desc(seg, t, st, 1).wait_send()
                ag_desc(seg, t, st, 0).wait_send()

            @when(st.d > 0, st.live)
            def _():
                rs_desc(seg, t, st, 0).wait_send()
                ag_desc(seg, t, st, 1).wait_send()

    outs = []

    def emit(src, dst):
        c = pltpu.make_async_copy(src, dst, R.out_sem.at[len(outs)])
        c.start()
        outs.append(c)

    def emit_seg(j):
        if j < D // TILE:
            emit(res.at[j], R.gwu.at[:, pl.ds(j * TILE, TILE)])
        elif j < cfg.late:
            emit(res.at[j], R.gwi.at[:, pl.ds((j - D // TILE) * TILE, TILE)])
        elif j == cfg.late:
            for i in range(D // TILE):
                emit(res.at[j, pl.ds(i * G, G)], R.gwo.at[:, pl.ds(i * TILE, TILE)])
        else:
            emit(res.at[j], (R.gwv, R.gwq, R.gwk)[j - cfg.late - 1])

    partners = [mate]
    for s in cfg.doubling:
        partners.append({"dp": me + s - 2 * s * lax.rem(me // s, 2)})
    smalls = R.small
    small_at = [0]

    def small_desc(i):
        return pltpu.make_async_remote_copy(
            src_ref=smalls.at[i],
            dst_ref=R.sbuf.at[i],
            send_sem=R.s_send.at[i],
            recv_sem=R.s_recv.at[i],
            device_id=partners[i],
            device_id_type=pl.DeviceIdType.MESH,
        )

    def small_step():
        i = small_at[0]
        if i == len(partners):
            return
        small_at[0] = i + 1
        small_desc(i).wait_recv()
        got = R.sbuf[i]
        if i == 0:
            got = jnp.where(lax.broadcasted_iota(jnp.int32, (8, D), 0) < 4, got, 0.0)
        smalls[i + 1] = smalls[i] + got
        if i + 1 < len(partners):
            small_desc(i + 1).start()
        else:
            emit(smalls.at[i + 1], R.gsmall)

    def at_point(i):
        for n, (_, seg, k) in enumerate([entry for entry in SCHEDULE if entry[0] == i]):
            advance(seg, k)
            if k == 8:
                emit_seg(seg)
            if i == LAST_POINT and n % 3 == 2:
                small_step()

    fill = R.fill[0]
    accs = M // LANES // 4
    many = LANES * LANES // T
    loads.idx.wait()
    for h in range(NH):
        at = R.idxv[h]
        hi = at // LANES
        lo = at - hi * LANES
        fld = lax.rem(hi, 4)
        one = jnp.where(fld == 0, 1, jnp.where(fld == 1, 1 << 8, jnp.where(fld == 2, 1 << 16, 1 << 24)))
        R.lo[h] = lo
        for a in range(accs):
            ok = (at < fill) & (hi >= 4 * a) & (hi < 4 * a + 4)
            R.inc[h, a] = jnp.where(ok, one, 0)
    for copy in (loads.tok, loads.wq, loads.wk, loads.wv):
        copy.wait()

    def begin_block(i, c):
        for r in range(0, LANES, CHUNK):
            rows = pl.ds(pl.multiple_of(i * LANES + r, CHUNK), CHUNK)
            cen, rstd = row_stats(R.tokv[rows, :].astype(F32))
            R.nrm[rows, :] = (cen * rstd * R.g1[...] + R.s1[...]).astype(BF)
        rows = pl.ds(pl.multiple_of(i * LANES, LANES), LANES)
        own = pl.ds(pl.multiple_of(T + i * LANES, LANES), LANES)
        low = R.nrm[rows, :]
        R.q[rows, :] = nn(low, R.wqkv[:, 0:G]).astype(BF)
        R.kext[own, :] = nn(low, R.wqkv[:, G : 2 * G]).astype(BF)
        R.vext[own, :] = nn(low, R.wqkv[:, 2 * G : W3]).astype(BF)
        lane = lax.broadcasted_iota(jnp.int32, (many, T), 0) + i * many
        for h in range(NH):
            got = [jnp.zeros((many, T), jnp.int32) for _ in range(accs)]
            for k in range(cfg.K):
                hit = jnp.broadcast_to(R.lo[h, pl.ds(k, 1), :], (many, T)) == lane
                for a in range(accs):
                    got[a] = got[a] + jnp.where(hit, jnp.broadcast_to(R.inc[h, a, pl.ds(k, 1), :], (many, T)), 0)
            for a in range(accs):
                R.cntt[h, a, pl.ds(pl.multiple_of(i * many, many), many), :] = got[a]
        return c

    lax.fori_loop(0, T // LANES, begin_block, 0)
    for h in range(NH):
        for a in range(accs):
            R.cnt[h, a] = R.cntt[h, a].T

    band_row = lax.dot_general(
        R.table[...], R.oh[...], (((1,), (0,)), ((), ())), precision=EXACT, preferred_element_type=F32
    )
    u_at = lax.broadcasted_iota(jnp.int32, (NH, KW), 1)
    band_row = jnp.where((u_at >= 1) & (u_at <= T), band_row, NEGATIVE)
    for h in range(NH):
        wide = jnp.broadcast_to(band_row[h : h + 1, :], (HB, KW))
        R.band[h] = pltpu.roll(wide, 0, 1, stride=1, stride_axis=0)

    for j in range(U // LANES):
        R.ibv[:, j * LANES : (j + 1) * LANES] = R.ib[j : j + 1, :].astype(F32)
    mix = jax.nn.sigmoid(R.gate[...])
    pl.semaphore_wait(barrier, want)

    for copy in (loads.ck, loads.cv, loads.mk, loads.mv, loads.wo, loads.og, loads.wu):
        copy.wait()

    def near_probs(rb, h, raw):
        for r in range(0, HB, CHUNK):
            s = raw[r : r + CHUNK] * scale + R.band[h, r : r + CHUNK, :]
            e = jnp.exp(s - jnp.max(s, axis=-1, keepdims=True))
            p = e * (1.0 / jnp.sum(e, axis=-1, keepdims=True))
            R.pl[h, pl.ds(rb * HB + r, CHUNK), :] = p.astype(BF)

    def far_probs(rb, h, raw):
        for r in range(0, HB, CHUNK):
            at = pl.ds(rb * HB + r, CHUNK)
            fields = []
            for f in range(M // LANES):
                fields.append(((R.cnt[h, f // 4, at, :] >> (8 * (f % 4))) & 255).astype(F32))
            c = jnp.concatenate(fields, axis=1)
            s = jnp.where(c > 0.0, raw[r : r + CHUNK] * scale, NEGATIVE)
            top = jnp.maximum(jnp.max(s, axis=-1, keepdims=True), 0.0)
            e = jnp.exp(s - top) * c
            total = jnp.exp(-top) + jnp.sum(e, axis=-1, keepdims=True)
            R.pm[h, at, :] = (e * (1.0 / total)).astype(BF)

    def attend(rb, hook):
        rows = pl.ds(rb * HB, HB)
        wide = pl.ds(rb * HB, KW)
        heads = [slice(h * DH, (h + 1) * DH) for h in range(NH)]
        ahead = list(range(U // TILE))

        def side():
            if ahead:
                cols = slice(ahead[0] * TILE, (ahead.pop(0) + 1) * TILE)
                R.ga[rows, cols] = nt(R.ogv[rows, :], R.wuv[cols, :])

        near_raw = nt(R.q[rows, heads[0]], R.kext[wide, heads[0]])
        for h in range(NH):
            cols = heads[h]
            q = R.q[rows, cols]
            far_raw = nt(q, R.mkv[:, cols])
            side()
            near_probs(rb, h, near_raw)
            if h + 1 < NH:
                near_raw = nt(R.q[rows, heads[h + 1]], R.kext[wide, heads[h + 1]])
            near = nn(R.pl[h, rows, :], R.vext[wide, cols])
            if h == 0:
                hook()
            side()
            far_probs(rb, h, far_raw)
            far = nn(R.pm[h, rows, :], R.mvv[:, cols])
            m = mix[:, h : h + 1]
            R.diff[rows, cols] = far - near
            R.joined[rows, cols] = (m * far + (1.0 - m) * near).astype(BF)
        while ahead:
            side()

    def project(rb):
        rows = pl.ds(rb * HB, HB)
        for j in range(D // TILE):
            cols = slice(j * TILE, (j + 1) * TILE)
            R.part[0, rows, cols] = nn(R.joined[rows, :], R.wov[:, cols]).astype(BF)

    attend(0, lambda: None)
    project(0)
    push(0, 0)
    attend(1, lambda: mid(0, 0))
    project(1)
    push(0, 1)

    loads.wi.wait()

    def tiles(count, fn):
        lax.fori_loop(0, count, lambda j, c: (fn(pl.ds(pl.multiple_of(j * TILE, TILE), TILE)), c)[1], 0)

    def second_norm(hf):
        def visit(rows, mine, total):
            x = R.tokv[rows, :].astype(F32) + total
            R.resid[mine, :] = x
            cen, rstd = row_stats(x)
            R.ntl[rows, :] = (cen * rstd * R.g2[...] + R.s2[...]).astype(BF)

        fin(0, hf, visit)
        share_desc(0, hf, R.ntl, core).start()

    def feed(hf):
        rows = pl.ds(hf * HB, HB)
        blocks = [slice(j * TILE, (j + 1) * TILE) for j in range(U // TILE)]

        def unit(cols, pre):
            bias = R.ibv[:, cols]
            sums = jnp.zeros((1, TILE), F32)
            for r in range(0, HB, CHUNK):
                at = pl.ds(hf * HB + r, CHUNK)
                x = pre[r : r + CHUNK] + bias
                x2 = x * x
                t = jnp.tanh(GELU_A * (x + GELU_B * x * x2))
                R.act[at, cols] = (0.5 * x * (1.0 + t)).astype(BF)
                slope = 0.5 * (1.0 + t) + 0.5 * x * (1.0 - t * t) * (GELU_A * (1.0 + 3.0 * GELU_B * x2))
                gi = (R.ga[at, cols] * slope).astype(BF)
                R.gi[at, cols] = gi
                sums = sums + jnp.sum(gi.astype(F32), axis=0, keepdims=True)
            R.gib[pl.ds(hf, 1), cols] = sums

        pre = nn(R.ntl[rows, :], R.wiv[:, blocks[0]])
        for j, cols in enumerate(blocks):
            later = nn(R.ntl[rows, :], R.wiv[:, blocks[j + 1]]) if j + 1 < len(blocks) else None
            unit(cols, pre)
            R.tr[cols, rows] = R.act[rows, cols].T
            pre = later

        def back(cols):
            R.part[1, rows, cols] = nt(R.gi[rows, :], R.wiv[cols, :]).astype(BF)

        tiles(D // TILE, back)

    second_norm(0)
    mid(0, 1)
    share_desc(0, 0, R.ntl, 1 - core).wait_recv()
    feed(0)
    push(1, 0)
    second_norm(1)
    mid(1, 0)
    share_desc(0, 1, R.ntl, 1 - core).wait_recv()
    feed(1)
    push(1, 1)

    for j in range(D // TILE):
        g[j] = nn(R.tr[...], R.ogv[:, j * TILE : (j + 1) * TILE]).astype(BF)
        dp_begin(j)
        if j == 1:
            mid(1, 1)
    R.tr[...] = R.ntl[...].T
    for j in range(U // TILE):
        g[D // TILE + j] = nn(R.tr[...], R.gi[:, j * TILE : (j + 1) * TILE]).astype(BF)
        dp_begin(D // TILE + j)
    sent(0)
    at_point(1)
    for hf in range(HALVES):
        rows = pl.ds(hf * HB, HB)

        def fed(cols, rows=rows):
            R.part[0, rows, cols] = nn(R.act[rows, :], R.wuv[:, cols]).astype(BF)

        tiles(D // TILE, fed)
        push(2, hf)
        at_point(2 + hf)

    def norm_back(p, hf, source, gain, base, keep, out):
        gain_sum, shift_sum = [jnp.zeros((1, D), F32)], [jnp.zeros((1, D), F32)]

        def visit(rows, mine, dy):
            cen, rstd = row_stats(source(rows, mine))
            xh = cen * rstd
            gain_sum[0] = gain_sum[0] + jnp.sum(dy * xh, axis=0, keepdims=True)
            shift_sum[0] = shift_sum[0] + jnp.sum(dy, axis=0, keepdims=True)
            dx = dy * gain
            dx = rstd * (
                dx - jnp.mean(dx, axis=-1, keepdims=True) - xh * jnp.mean(dx * xh, axis=-1, keepdims=True)
            )
            got = base(rows, mine) + dx
            if keep is not None:
                keep[mine, :] = got
            out[rows, :] = got.astype(BF)

        fin(p, hf, visit)
        share_desc(p, hf, out, core).start()
        return gain_sum[0], shift_sum[0]

    sums = []
    for hf in range(HALVES):
        sums.append(
            norm_back(
                1, hf, lambda rows, mine: R.resid[mine, :], R.g2[...],
                lambda rows, mine: R.ogv[rows, :].astype(F32), R.gres, R.gat,
            )
        )
        at_point(4 + hf)
    R.small[0, 2:3, :] = sums[0][0] + sums[1][0]
    R.small[0, 3:4, :] = sums[0][1] + sums[1][1]
    for hf in range(HALVES):
        mid(2, hf)
    for hf in range(HALVES):
        share_desc(1, hf, R.gat, 1 - core).wait_recv()

    gate_sums = [jnp.zeros((1, 1), F32) for _ in range(NH)]
    for rb in range(2):
        rows = pl.ds(rb * HB, HB)
        gj = nt(R.gat[rows, :], R.wov[...])
        for h in range(NH):
            cols = slice(h * DH, (h + 1) * DH)
            m = mix[:, h : h + 1]
            gate_sums[h] = gate_sums[h] + jnp.sum(
                jnp.sum(gj[:, cols] * R.diff[rows, cols], axis=0, keepdims=True), axis=1, keepdims=True
            )
            R.gl[rows, cols] = ((1.0 - m) * gj[:, cols]).astype(BF)
            R.gm[rows, cols] = (m * gj[:, cols]).astype(BF)

    at_point(6)

    def own_keys(weights, other, out, point):
        for h in range(NH):
            cols = slice(h * DH, (h + 1) * DH)
            spot = slice(out * G + h * DH, out * G + (h + 1) * DH)
            top = tn(weights[h, 0:HB, T:KW], other[0:HB, cols]) + tn(weights[h, HB:T, HB:T], other[HB:T, cols])
            R.gqkv[0:HB, spot] = top.astype(BF)
            R.gqkv[HB:T, spot] = tn(weights[h, HB:T, T:KW], other[HB:T, cols]).astype(BF)
            if h == 0:
                at_point(point)

    def weight_seg(seg, out):
        g[seg] = nn(R.tr[...], R.gqkv[:, out * G : (out + 1) * G]).astype(BF)

    LATE = cfg.late
    for j in range(D // TILE):
        g[LATE, j * G : (j + 1) * G, :] = tn(R.joined[...], R.gat[:, j * TILE : (j + 1) * TILE]).astype(BF)
    dp_begin(LATE)
    at_point(7)
    R.tr[...] = R.nrm[...].T
    own_keys(R.pl, R.gl, 2, 8)
    weight_seg(LATE + 1, 2)
    dp_begin(LATE + 1)
    at_point(9)
    for rb in range(2):
        rows = pl.ds(rb * HB, HB)
        wide = pl.ds(rb * HB, KW)
        for h in range(NH):
            cols = slice(h * DH, (h + 1) * DH)
            dp = nt(R.gl[rows, cols], R.vext[wide, cols])
            for r in range(0, HB, CHUNK):
                at = pl.ds(rb * HB + r, CHUNK)
                p, d = R.pl[h, at, :].astype(F32), dp[r : r + CHUNK]
                ds = p * (d - jnp.sum(p * d, axis=-1, keepdims=True))
                if rb == 0:
                    R.band[h, pl.ds(r, CHUNK), :] = ds
                else:
                    R.band[h, pl.ds(r, CHUNK), :] += ds
                R.pl[h, at, :] = (ds * scale).astype(BF)
            gq = nn(R.pl[h, rows, :], R.kext[wide, cols])
            at_point(10 + 2 * (rb * NH + h))
            dp = nt(R.gm[rows, cols], R.mvv[:, cols])
            for r in range(0, HB, CHUNK):
                at = pl.ds(rb * HB + r, CHUNK)
                p, d = R.pm[h, at, :].astype(F32), dp[r : r + CHUNK]
                ds = p * (d - jnp.sum(p * d, axis=-1, keepdims=True))
                R.pm[h, at, :] = (ds * scale).astype(BF)
            gq = gq + nn(R.pm[h, rows, :], R.mkv[:, cols])
            R.gqkv[rows, cols] = gq.astype(BF)
            at_point(11 + 2 * (rb * NH + h))

    weight_seg(LATE + 2, 0)
    dp_begin(LATE + 2)
    at_point(18)
    own_keys(R.pl, R.q, 1, 19)
    weight_seg(LATE + 3, 1)
    dp_begin(LATE + 3)
    at_point(20)
    sent(1)
    for hf in range(HALVES):
        rows = pl.ds(hf * HB, HB)

        def back_in(cols, rows=rows):
            R.part[1, rows, cols] = nt(R.gqkv[rows, :], R.wqkv[cols, :]).astype(BF)

        tiles(D // TILE, back_in)
        push(3, hf)
        at_point(21 + hf)

    for hf in range(HALVES):

        def result(rows, mine, total):
            R.bo[rows, :] = (R.resid[mine, :] + total).astype(BF)

        fin(2, hf, result)
        share_desc(2, hf, R.bo, core).start()
    at_point(23)
    for hf in range(HALVES):
        mid(3, hf)
    at_point(24)

    at_row = lax.broadcasted_iota(jnp.int32, (8, KW), 0)
    table_grads = []
    for h in range(NH):
        half = HB
        cur = R.band[h]
        while half > 8:
            half //= 2
            cur = cur[:half] + pltpu.roll(cur[half:], KW - half, 1)
        for bit in (1, 2, 4):
            cur = jnp.where(lax.rem(at_row // bit, 2) == 1, pltpu.roll(cur, KW - bit, 1), cur)
        diag = jnp.sum(cur, axis=0, keepdims=True)
        table_grads.append(
            lax.dot_general(diag, R.oh[...], (((1,), (1,)), ((), ())), precision=EXACT, preferred_element_type=F32)
        )
        if h == 0:
            at_point(25)
    at_point(26)
    smalls[0, 4:5, :] = R.gib[0:1, :] + R.gib[1:2, :]
    smalls[0, 5:8, :] = jnp.zeros((3, D), F32)
    for h in range(NH):
        s = mix[:, h : h + 1]
        smalls[0, 5:6, h * LANES : h * LANES + NB] = table_grads[h]
        smalls[0, 6:7, h * LANES : (h + 1) * LANES] = jnp.broadcast_to(gate_sums[h] * s * (1.0 - s), (1, LANES))

    at_point(27)
    sums = []
    for hf in range(HALVES):
        sums.append(
            norm_back(
                3, hf, lambda rows, mine: R.tokv[rows, :].astype(F32), R.g1[...],
                lambda rows, mine: R.gres[mine, :], None, R.gt,
            )
        )
        at_point(28 + hf)
    smalls[0, 0:1, :] = sums[0][0] + sums[1][0]
    smalls[0, 1:2, :] = sums[0][1] + sums[1][1]
    small_desc(0).start()

    for hf in range(HALVES):
        share_desc(2, hf, R.bo, 1 - core).wait_recv()
        share_desc(3, hf, R.gt, 1 - core).wait_recv()
    emit(R.bo, R.block_out)
    emit(R.gt, R.gtok)
    at_point(LAST_POINT)
    for _ in partners:
        small_step()

    sent(2)
    sent(3)
    for p in range(4):
        for hf in range(HALVES):
            share_desc(p, hf, (R.ntl, R.gat, R.bo, R.gt)[p], core).wait_send()
    for i in range(len(partners)):
        small_desc(i).wait_send()
    for seg in range(len(ORDERS)):
        dp_close(seg)
    for c in outs:
        c.wait()


def local(n, tokens, wq, wk, wv, wo, wi, ib, wu, g1, s1, g2, s2, table, gate, ck, cv, mk, mv, idx, fill, og):
    T, D = tokens.shape
    NH = table.shape[0]
    G = wq.shape[1]
    U = wi.shape[1]
    M = mk.shape[1]
    K = idx.shape[2]
    HB = T // 2
    KW = T + HB
    stages = stage_list(n)
    doubling = []
    s = 1
    while s < n:
        doubling.append(s)
        s *= 2
    ffn = (D + U) // TILE
    late = 1 + 3 * G // TILE
    nseg = ffn + late
    seg = D
    orders = (stages, stages[::-1])
    rows_needed = 0
    for order in orders:
        off, length = 0, seg
        for _, r in order:
            length //= 2
            off += (1 if r == 2 else 2) * length
        rows_needed = max(rows_needed, off)
    inputs = dict(
        tok=tokens, idx=idx.transpose(1, 2, 0), wq=wq, wk=wk, wv=wv, wo=wo, wi=wi, wu=wu, ck=ck, cv=cv, mk=mk, mv=mv, og=og
    )
    vectors = dict(
        ib=ib.reshape(U // LANES, LANES), g1=g1.reshape(1, D), s1=s1.reshape(1, D), g2=g2.reshape(1, D), s2=s2.reshape(1, D),
        table=table, gate=gate.reshape(1, NH), oh=jnp.asarray(bucket_rows(T)),
    )
    outputs = dict(
        block_out=((T, D), BF), gtok=((T, D), BF), gwq=((D, G), BF), gwk=((D, G), BF), gwv=((D, G), BF),
        gwo=((G, D), BF), gwi=((D, U), BF), gwu=((U, D), BF), gsmall=((8, D), F32),
    )
    S = len(stages)
    sem = pltpu.SemaphoreType.DMA
    scratch = dict(
        tokv=pltpu.VMEM((T, D), BF), ogv=pltpu.VMEM((T, D), BF), idxv=pltpu.VMEM((NH, K, T), jnp.int32),
        wqkv=pltpu.VMEM((D, 3 * G), BF), wov=pltpu.VMEM((G, D), BF), wiv=pltpu.VMEM((D, U), BF),
        wuv=pltpu.VMEM((U, D), BF), kext=pltpu.VMEM((2 * T, G), BF), vext=pltpu.VMEM((2 * T, G), BF),
        mkv=pltpu.VMEM((M, G), BF), mvv=pltpu.VMEM((M, G), BF),
        lo=pltpu.VMEM((NH, K, T), jnp.int32), inc=pltpu.VMEM((NH, M // LANES // 4, K, T), jnp.int32),
        cntt=pltpu.VMEM((NH, M // LANES // 4, LANES, T), jnp.int32),
        cnt=pltpu.VMEM((NH, M // LANES // 4, T, LANES), jnp.int32),
        nrm=pltpu.VMEM((T, D), BF), q=pltpu.VMEM((T, G), BF), band=pltpu.VMEM((NH, HB, KW), F32),
        pl=pltpu.VMEM((NH, T, KW), BF), pm=pltpu.VMEM((NH, T, M), BF), diff=pltpu.VMEM((T, G), F32),
        joined=pltpu.VMEM((T, G), BF), ga=pltpu.VMEM((T, U), F32), ntl=pltpu.VMEM((T, D), BF),
        resid=pltpu.VMEM((HB, D), F32), act=pltpu.VMEM((T, U), BF), gi=pltpu.VMEM((T, U), BF),
        gib=pltpu.VMEM((8, U), F32), ibv=pltpu.VMEM((1, U), F32), tr=pltpu.VMEM((D, T), BF), gres=pltpu.VMEM((HB, D), F32),
        gat=pltpu.VMEM((T, D), BF), gl=pltpu.VMEM((T, G), BF), gm=pltpu.VMEM((T, G), BF),
        gqkv=pltpu.VMEM((T, 3 * G), BF), bo=pltpu.VMEM((T, D), BF), gt=pltpu.VMEM((T, D), BF),
        part=pltpu.VMEM((2, T, D), BF), cbuf=pltpu.VMEM((2, HB, D), BF), ybuf=pltpu.VMEM((2, HB, D), BF),
        small=pltpu.VMEM((len(doubling) + 2, 8, D), F32), sbuf=pltpu.VMEM((len(doubling) + 1, 8, D), F32),
        g=pltpu.VMEM((nseg, seg, TILE), BF), res=pltpu.VMEM((nseg, seg, TILE), BF),
        rbuf=pltpu.VMEM((nseg, rows_needed, TILE), BF),
        in_sem=sem((13,)), out_sem=sem((2 + 2 * (D // TILE) + U // TILE + 4,)),
        c_send=sem((4, HALVES)), c_recv=sem((4, HALVES)), y_send=sem((4, HALVES)), y_recv=sem((4, HALVES)),
        a_send=sem((4, HALVES)), a_recv=sem((4, HALVES)),
        s_send=sem((len(doubling) + 1,)), s_recv=sem((len(doubling) + 1,)),
        rs_send=sem((nseg, S, 2)), rs_recv=sem((nseg, S, 2)),
        ag_send=sem((nseg, S, 2)), ag_recv=sem((nseg, S, 2)),
    )
    cfg = Space(
        n=n, T=T, D=D, G=G, U=U, M=M, NH=NH, K=K, stages=stages, doubling=doubling, seg=seg, orders=orders,
        late=ffn,
        names=[*inputs, *vectors, "fill", *outputs, *scratch],
    )
    any_spec = pl.BlockSpec(memory_space=pl.ANY)
    vec_spec = pl.BlockSpec(memory_space=pltpu.VMEM)
    outs = pl.pallas_call(
        functools.partial(kernel, cfg),
        out_shape=[jax.ShapeDtypeStruct(*v) for v in outputs.values()],
        in_specs=[any_spec] * len(inputs) + [vec_spec] * len(vectors) + [pl.BlockSpec(memory_space=pltpu.SMEM)],
        out_specs=[any_spec] * len(outputs),
        scratch_shapes=list(scratch.values()),
        compiler_params=pltpu.CompilerParams(
            collective_id=0, has_side_effects=True, vmem_limit_bytes=63 * MIB
        ),
        cost_estimate=pl.CostEstimate(flops=12 * 10**9, bytes_accessed=20 * 10**6, transcendentals=3 * 10**6),
    )(
        *inputs.values(), *vectors.values(), fill,
    )
    return widen(outs, NH)


def widen_kernel(NH, cuts, *refs):
    ins, outs, scratch = refs[:9], refs[9:24], refs[24:]
    boxes = len(cuts)
    low, (in_sem, out_sem), high = scratch[:boxes], scratch[boxes : boxes + 2], list(scratch[boxes + 2 :])
    high = [low[n] if cut[0] < 2 else high.pop(0) for n, cut in enumerate(cuts)]
    loads, stores = [], []
    for n, (i, at, rows, cols) in enumerate(cuts):
        loads.append(pltpu.make_async_copy(ins[i].at[pl.ds(at, rows)], low[n], in_sem.at[n]))
        stores.append(pltpu.make_async_copy(high[n], outs[i].at[pl.ds(at, rows)], out_sem.at[n]))
        loads[n].start()
    small = ins[8]
    for i in range(5):
        outs[8 + i][...] = small[i : i + 1, :]
    for h in range(NH):
        outs[13][h : h + 1, :] = small[5:6, h * LANES : h * LANES + NB]
        outs[14][:, h : h + 1] = small[6:7, h * LANES : h * LANES + 1]
    for n, (i, at, rows, cols) in enumerate(cuts):
        loads[n].wait()
        if high[n] is not low[n]:
            high[n][...] = low[n][...].astype(F32)
        stores[n].start()
    for c in stores:
        c.wait()


def widen(sums, NH):
    small = sums[8]
    D = small.shape[1]
    cuts = []
    for i in (2, 3, 4, 5, 6, 7, 0, 1):
        rows, cols = sums[i].shape
        step = max(8, min(rows, TILE * D // cols))
        cuts += [(i, at, step, cols) for at in range(0, rows, step)]
    shapes = [jax.ShapeDtypeStruct(x.shape, BF if i < 2 else F32) for i, x in enumerate(sums[:8])]
    tiny = [(1, D)] * 5 + [(NH, NB), (1, NH)]
    hbm = pl.BlockSpec(memory_space=pl.ANY)
    vec = pl.BlockSpec(memory_space=pltpu.VMEM)
    got = pl.pallas_call(
        functools.partial(widen_kernel, NH, cuts),
        in_specs=[hbm] * 8 + [vec],
        out_specs=[hbm] * 8 + [vec] * len(tiny),
        out_shape=shapes + [jax.ShapeDtypeStruct(x, F32) for x in tiny],
        scratch_shapes=[pltpu.VMEM((rows, cols), BF) for _, _, rows, cols in cuts]
        + [pltpu.SemaphoreType.DMA((len(cuts),))] * 2
        + [pltpu.VMEM((rows, cols), F32) for i, _, rows, cols in cuts if i >= 2],
        compiler_params=pltpu.CompilerParams(vmem_limit_bytes=60 * MIB),
        cost_estimate=pl.CostEstimate(flops=0, bytes_accessed=22 * 10**6, transcendentals=0),
    )(*sums)
    block_out, gtok, gwq, gwk, gwv, gwo, gwi, gwu, g1, s1, g2, s2, ib, bias, gates = got
    return (
        block_out, gtok, gwq, gwk, gwv, gwo, gwi, ib.reshape(-1), gwu, g1.reshape(D), s1.reshape(D), g2.reshape(D),
        s2.reshape(D), bias, gates.reshape(NH),
    )


def solution(mesh):
    return jax.shard_map(
        functools.partial(local, mesh.shape["dp"]),
        mesh=mesh,
        in_specs=(
            P("dp", None), P(None, "head"), P(None, "head"), P(None, "head"), P("head", None), P(None, "head"),
            P("head"), P("head", None), P(), P(), P(), P(), P("head", None), P("head"), P("dp", "head"),
            P("dp", "head"), P("dp", None, "head"), P("dp", None, "head"), P("dp", "head", None), P("dp"),
            P("dp", None),
        ),
        out_specs=(
            P("dp", None), P("dp", None), P(None, "head"), P(None, "head"), P(None, "head"), P("head", None),
            P(None, "head"), P("head"), P("head", None), P(), P(), P(), P(), P("head", None), P("head"),
        ),
        check_vma=False,
    )
```

```python
import functools
import math
from types import SimpleNamespace as Space

import jax
import jax.numpy as jnp
import numpy as np
from jax import lax
from jax.experimental import pallas as pl
from jax.experimental.pallas import tpu as pltpu
from jax.sharding import PartitionSpec as P

NB = 32
MAXD = 128
EPSILON = 1e-05
NEGATIVE = -1e30
EXACT = lax.Precision.HIGHEST
BF = jnp.bfloat16
F32 = jnp.float32
LANES = 128
TILE = 256
HALVES = 2
CHUNK = 32
MIB = 1 << 20
KINDS = dict(
    A=(False, False, False), a=(False, True, False), B=(True, False, False), C=(True, True, False),
    F=(False, False, True), f=(False, True, True),
)
SEGMENTS = "ffffBaaaAaCa"
LAST_POINT = 30
SCHEDULE = (
    (1, 4, 0), (4, 0, 0), (4, 4, 1), (4, 5, 0), (5, 0, 1), (6, 2, 0), (6, 4, 2), (6, 0, 2), (6, 4, 3),
    (7, 6, 0), (7, 0, 3), (7, 1, 0), (7, 3, 0), (7, 2, 1), (9, 3, 1), (9, 5, 1), (10, 2, 2), (11, 3, 2),
    (11, 7, 0), (11, 3, 3), (11, 5, 2), (11, 8, 0), (11, 2, 3), (12, 1, 1), (12, 6, 1), (14, 9, 0), (14, 5, 3),
    (14, 4, 4), (14, 5, 4), (14, 7, 1), (14, 3, 4), (14, 6, 2), (14, 8, 1), (14, 1, 2), (16, 1, 3), (16, 9, 1),
    (17, 7, 2), (17, 8, 2), (20, 9, 2), (20, 4, 5), (20, 6, 3), (20, 8, 3), (20, 7, 3), (21, 11, 0), (21, 7, 4),
    (21, 6, 4), (22, 10, 0), (23, 9, 3), (24, 4, 6), (24, 10, 1), (24, 8, 4), (24, 11, 1), (24, 8, 5), (24, 9, 4),
    (25, 0, 4), (25, 10, 2), (25, 2, 4), (25, 11, 2), (25, 7, 5), (26, 8, 6), (26, 11, 3), (26, 5, 5), (27, 10, 3),
    (28, 4, 7), (28, 1, 4), (28, 11, 4), (28, 10, 4), (29, 6, 5), (29, 9, 5), (29, 8, 7), (29, 11, 5), (29, 10, 5),
)
GELU_A = math.sqrt(2.0 / math.pi)
GELU_B = 0.044715


def bucket_rows(length):
    span = np.arange(length)
    exact = NB // 2
    ratio = np.log(np.maximum(span, 1) / exact) / np.log(MAXD / exact)
    larger = np.minimum(exact + (ratio * (NB - exact)).astype(np.int32), NB - 1)
    bucket = np.where(span < exact, span, larger).astype(np.int32)
    table = np.zeros((NB, length + length // 2), np.float32)
    for u in range(1, length + 1):
        table[bucket[length - u], u] = 1.0
    return table


def nn(a, b):
    return lax.dot_general(a, b, (((1,), (0,)), ((), ())), preferred_element_type=F32)


def nt(a, b):
    return lax.dot_general(a, b, (((1,), (1,)), ((), ())), preferred_element_type=F32)


def tn(a, b):
    return lax.dot_general(a, b, (((0,), (0,)), ((), ())), preferred_element_type=F32)


def row_stats(x):
    mean = jnp.mean(x, axis=-1, keepdims=True)
    c = x - mean
    var = jnp.mean(c * c, axis=-1, keepdims=True)
    return c, lax.rsqrt(var + EPSILON)


def stage_list(n):
    stages, stride, left = [], 1, n
    if left >= 2:
        stages.append((1, 2))
        stride, left = 2, left // 2
    while left >= 4:
        stages.append((stride, 4))
        stride, left = stride * 4, left // 4
    if left == 2:
        stages.append((stride, 2))
    return stages


def line_hops(r, middle):
    if r == 2 or not middle:
        scatter = [[(h, h + 1, 1), (r - 1 - h, r - 2 - h, 0)] for h in range(r - 1)]
        gather = [[(r - 1 - h, r - 2 - h, 1), (h, h + 1, 0)] for h in range(r - 1)]
        return scatter, gather, [(0, 0 if r == 2 else 1)] * (r - 1), 1 if r == 2 else 2, (0, r - 1)
    scatter = [[(0, 1, 1), (0, 1, 0), (3, 2, 0), (3, 2, 1)], [(1, 2, 1), (2, 1, 0)]]
    gather = [[(1, 2, 0), (1, 0, 0), (2, 1, 1), (2, 3, 1)], [(1, 0, 1), (2, 3, 0)]]
    return scatter, gather, [(0, 1), (2, 2)], 3, (1, 2)


def plan_of(kind, stages, seg):
    back, middle, factors = KINDS[kind]
    plan, off, size = [], 0, seg
    for t, (stride, r) in enumerate(stages[::-1] if back else stages):
        size //= 2
        scatter, gather, slots, count, owners = line_hops(r, middle)
        skip = factors and t == 0
        plan.append(
            Space(
                stride=stride, r=r, size=size, off=off, scatter=scatter, gather=gather, slots=slots, owners=owners, skip=skip
            )
        )
        off += 0 if skip else count * size
    return plan, off


def kernel(cfg, *refs):
    n = cfg.n
    R = Space(**dict(zip(cfg.names, refs)))
    T, D, G, U, M, NH = cfg.T, cfg.D, cfg.G, cfg.U, cfg.M, cfg.NH
    DH = G // NH
    HB = T // 2
    KW = T + HB
    scale = 1.0 / math.sqrt(DH)
    me = lax.axis_index("dp")
    hid = lax.axis_index("head")
    core = lax.rem(hid, 2)
    mate = {"head": hid + 1 - 2 * core}
    across = {"head": lax.rem(hid + 2, 4)}
    sub = HB // 2

    peers = []
    for stride, r in cfg.stages:
        d = lax.rem(me // stride, r)
        peers.append((d > 0, me - stride))
        peers.append((d < r - 1, me + stride))
    for s in cfg.doubling:
        covered = False
        for stride, r in cfg.stages:
            if s == stride:
                covered = True
        if not covered:
            b = lax.rem(me // s, 2)
            peers.append((True, me + s - 2 * s * b))
    barrier = pltpu.get_barrier_semaphore()
    want = 2
    pl.semaphore_signal(barrier, inc=1, device_id=mate)
    pl.semaphore_signal(barrier, inc=1, device_id=across)
    for cond, who in peers:
        if cond is True:
            pl.semaphore_signal(barrier, inc=1, device_id={"dp": who})
            want = want + 1
        else:

            @pl.when(cond)
            def _(who=who):
                pl.semaphore_signal(barrier, inc=1, device_id={"dp": who})

            want = want + jnp.where(cond, 1, 0).astype(jnp.int32)

    W3 = 3 * G
    loads = Space()

    def load(src, dst, sem):
        copy = pltpu.make_async_copy(src, dst, R.in_sem.at[sem])
        copy.start()
        return copy

    loads.tok = load(R.tok, R.tokv, 0)
    loads.idx = load(R.idx, R.idxv, 1)
    loads.wq = load(R.wq, R.wqkv.at[:, pl.ds(0, G)], 2)
    loads.wk = load(R.wk, R.wqkv.at[:, pl.ds(G, G)], 3)
    loads.wv = load(R.wv, R.wqkv.at[:, pl.ds(2 * G, G)], 4)
    loads.ck = load(R.ck, R.kext.at[pl.ds(0, T)], 5)
    loads.cv = load(R.cv, R.vext.at[pl.ds(0, T)], 6)
    loads.mk = load(R.mk.at[0], R.mkv, 7)
    loads.mv = load(R.mv.at[0], R.mvv, 8)
    loads.wo = load(R.wo, R.wov, 9)
    loads.og = load(R.og, R.ogv.at[pl.ds(0, T)], 10)
    loads.wu = load(R.wu, R.wuv, 11)
    loads.wi = load(R.wi, R.wiv, 12)


    def part_rows(hf, c):
        return pl.ds(pl.multiple_of(hf * HB + c * sub, sub), sub)

    def push_desc(p, hf):
        return pltpu.make_async_remote_copy(
            src_ref=R.part.at[p % 2, part_rows(hf, 1 - core)],
            dst_ref=R.cbuf.at[p % 2, pl.ds(hf * sub, sub)],
            send_sem=R.c_send.at[p, hf],
            recv_sem=R.c_recv.at[p, hf],
            device_id=mate,
            device_id_type=pl.DeviceIdType.MESH,
        )

    def cross_desc(p, hf):
        return pltpu.make_async_remote_copy(
            src_ref=R.part.at[p % 2, part_rows(hf, core)],
            dst_ref=R.ybuf.at[p % 2, pl.ds(hf * sub, sub)],
            send_sem=R.y_send.at[p, hf],
            recv_sem=R.y_recv.at[p, hf],
            device_id=across,
            device_id_type=pl.DeviceIdType.MESH,
        )

    def share_desc(p, hf, buf, c):
        rows = part_rows(hf, c)
        return pltpu.make_async_remote_copy(
            src_ref=buf.at[rows],
            dst_ref=buf.at[rows],
            send_sem=R.a_send.at[p, hf],
            recv_sem=R.a_recv.at[p, hf],
            device_id=mate,
            device_id_type=pl.DeviceIdType.MESH,
        )

    def push(p, hf):
        push_desc(p, hf).start()

    def mid(p, hf):
        push_desc(p, hf).wait_recv()
        for r in range(0, sub, CHUNK):
            rows = pl.ds(pl.multiple_of(hf * HB + core * sub + r, CHUNK), CHUNK)
            total = R.part[p % 2, rows, :].astype(F32) + R.cbuf[p % 2, pl.ds(hf * sub + r, CHUNK), :].astype(F32)
            R.part[p % 2, rows, :] = total.astype(BF)
        cross_desc(p, hf).start()

    def sent(p):
        for hf in range(HALVES):
            push_desc(p, hf).wait_send()
            cross_desc(p, hf).wait_send()

    def fin(p, hf, visit, side=()):
        cross_desc(p, hf).wait_recv()
        side = list(side)
        for r in range(0, sub, CHUNK):
            rows = pl.ds(pl.multiple_of(hf * HB + core * sub + r, CHUNK), CHUNK)
            mine = pl.ds(hf * sub + r, CHUNK)
            if side:
                side.pop(0)()
            visit(rows, mine, R.part[p % 2, rows, :].astype(F32) + R.ybuf[p % 2, mine, :].astype(F32))
        for work in side:
            work()

    g, res, rbuf = R.g, R.res, R.rbuf
    SEG = cfg.seg

    plans = {}
    for kind in sorted(set(SEGMENTS)):
        base, live = 0, None
        plan, _ = plan_of(kind, cfg.stages, SEG)
        for st in plan:
            st.d = lax.rem(me // st.stride, st.r)
            st.base, st.live = base, live
            base = base + st.size * (st.d // st.owners[1])
            if st.r > 2:
                owner = (st.d == st.owners[0]) | (st.d == st.owners[1])
                live = owner if live is None else live & owner
        phases = [(0, t, h) for t, st in enumerate(plan) if not st.skip for h in range(len(st.scatter))]
        phases += [(1, t, h) for t, st in reversed(list(enumerate(plan))) for h in range(len(st.gather))]
        plans[kind] = Space(stages=plan, own=base, own_size=plan[-1].size, live=live, phases=phases)

    def when(cond, live):
        return pl.when(cond if live is None else cond & live)

    def piece(st, hi):
        first = st.base + hi * st.size
        return pl.ds(first if isinstance(first, int) else pl.multiple_of(first, 16), st.size)

    def slot(seg, st, h, hi):
        return pl.ds(cfg.offsets[seg] + st.off + st.slots[h][hi] * st.size, st.size)

    def hop_desc(seg, phase, move):
        gather, t, h = phase
        st = plans[SEGMENTS[seg]].stages[t]
        a, b, hi = move
        return pltpu.make_async_remote_copy(
            src_ref=(res if gather else g).at[seg, piece(st, hi)],
            dst_ref=res.at[seg, piece(st, hi)] if gather else rbuf.at[slot(seg, st, h, hi)],
            send_sem=R.dp_send.at[seg, t, gather, h, 2 * hi + int(b > a)],
            recv_sem=R.dp_recv.at[seg, t, gather, h, hi],
            device_id={"dp": me + st.stride if b > a else me - st.stride},
            device_id_type=pl.DeviceIdType.MESH,
        )

    def moves_of(seg, phase):
        st = plans[SEGMENTS[seg]].stages[phase[1]]
        return (st.gather if phase[0] else st.scatter)[phase[2]]

    def add_in(seg, phase, hi):
        _, t, h = phase
        st = plans[SEGMENTS[seg]].stages[t]
        step = min(64, st.size)
        to, come = st.base + hi * st.size, cfg.offsets[seg] + st.off + st.slots[h][hi] * st.size

        def some(i, c):
            rows = pl.ds(pl.multiple_of(to + i * step, 16), step)
            total = g[seg, rows, :].astype(F32) + rbuf[pl.ds(pl.multiple_of(come + i * step, 16), step), :].astype(F32)
            g[seg, rows, :] = total.astype(BF)
            return c

        lax.fori_loop(0, st.size // step, some, 0)

    def dp_open(seg, k):
        plan = plans[SEGMENTS[seg]]
        phase = plan.phases[k]
        if phase[0] and (k == 0 or not plan.phases[k - 1][0]):

            @when(me >= 0, plan.live)
            def _():
                own = pl.ds(pl.multiple_of(plan.own, 16), plan.own_size)
                res[seg, own, :] = g[seg, own, :]

        st = plan.stages[phase[1]]
        for at in range(st.r):
            mine = [move for move in moves_of(seg, phase) if move[0] == at]
            if mine:

                @when(st.d == at, st.live)
                def _(mine=mine):
                    for move in mine:
                        hop_desc(seg, phase, move).start()

    def dp_phase(seg, k):
        plan = plans[SEGMENTS[seg]]
        phase = plan.phases[k]
        st = plan.stages[phase[1]]
        later = plan.phases[k + 1] if k + 1 < len(plan.phases) else None
        follows = later is not None and later[:2] == phase[:2]
        for at in range(st.r):
            mine = [move for move in moves_of(seg, phase) if move[1] == at]
            if mine:

                @when(st.d == at, st.live)
                def _(mine=mine, at=at):
                    for move in mine:
                        hop_desc(seg, phase, move).wait_recv()
                        if not phase[0]:
                            add_in(seg, phase, move[2])
                        for onward in moves_of(seg, later) if follows else ():
                            if onward[0] == at and onward[2] == move[2]:
                                hop_desc(seg, later, onward).start()

        if later is not None and not follows:
            dp_open(seg, k + 1)

    def advance(seg, k):
        parts = len([entry for entry in SCHEDULE if entry[1] == seg])
        total = len(plans[SEGMENTS[seg]].phases)
        for i in range(total * k // parts, total * (k + 1) // parts):
            dp_phase(seg, i)
        return k + 1 == parts

    def dp_begin(seg):
        dp_open(seg, 0)

    def dp_close(seg):
        plan = plans[SEGMENTS[seg]]
        for t, st in enumerate(plan.stages):
            for at in range(st.r):
                mine = [(ph, mv) for ph in plan.phases if ph[1] == t for mv in moves_of(seg, ph) if mv[0] == at]

                @when(st.d == at, st.live)
                def _(mine=mine):
                    for phase, move in mine:
                        hop_desc(seg, phase, move).wait_send()

    half = lax.rem(me, 2)
    pair = {"dp": me + 1 - 2 * half}
    UH = U // 2

    def grad_desc(forward):
        rows = pl.ds(pl.multiple_of(core * HB, HB), HB)
        away = pl.ds(pl.multiple_of(T + core * HB, HB), HB)
        return pltpu.make_async_remote_copy(
            src_ref=R.ogv.at[away if forward else rows],
            dst_ref=R.ogv.at[away],
            send_sem=R.x_send.at[HALVES + forward],
            recv_sem=R.x_recv.at[HALVES + forward],
            device_id=mate if forward else pair,
            device_id_type=pl.DeviceIdType.MESH,
        )

    def active_desc(hf):
        rows = pl.ds(hf * HB, HB)
        return pltpu.make_async_remote_copy(
            src_ref=R.act.at[rows, pl.ds(pl.multiple_of((1 - half) * UH, TILE), UH)],
            dst_ref=R.gt.at[rows, pl.ds(0, UH)],
            send_sem=R.x_send.at[hf],
            recv_sem=R.x_recv.at[hf],
            device_id=pair,
            device_id_type=pl.DeviceIdType.MESH,
        )

    outs = []

    def emit(src, dst):
        c = pltpu.make_async_copy(src, dst, R.out_sem.at[len(outs)])
        c.start()
        outs.append(c)

    def emit_seg(j):
        if j < D // TILE:
            emit(res.at[j], R.gwu.at[:, pl.ds(j * TILE, TILE)])
        elif j < cfg.late:
            emit(res.at[j], R.gwi.at[:, pl.ds((j - D // TILE) * TILE, TILE)])
        elif j == cfg.late:
            for i in range(D // TILE):
                emit(res.at[j, pl.ds(i * G, G)], R.gwo.at[:, pl.ds(i * TILE, TILE)])
        else:
            emit(res.at[j], (R.gwv, R.gwq, R.gwk)[j - cfg.late - 1])

    partners = [mate]
    for s in cfg.doubling:
        partners.append({"dp": me + s - 2 * s * lax.rem(me // s, 2)})
    smalls = R.small
    small_at = [0]

    def small_desc(i):
        return pltpu.make_async_remote_copy(
            src_ref=smalls.at[i],
            dst_ref=R.sbuf.at[i],
            send_sem=R.s_send.at[i],
            recv_sem=R.s_recv.at[i],
            device_id=partners[i],
            device_id_type=pl.DeviceIdType.MESH,
        )

    def small_step():
        i = small_at[0]
        if i == len(partners):
            return
        small_at[0] = i + 1
        small_desc(i).wait_recv()
        got = R.sbuf[i]
        if i == 0:
            got = jnp.where(lax.broadcasted_iota(jnp.int32, (8, D), 0) < 4, got, 0.0)
        smalls[i + 1] = smalls[i] + got
        if i + 1 < len(partners):
            small_desc(i + 1).start()
        else:
            emit(smalls.at[i + 1], R.gsmall)

    def at_point(i):
        for n, (_, seg, k) in enumerate([entry for entry in SCHEDULE if entry[0] == i]):
            if advance(seg, k):
                emit_seg(seg)
            if i == LAST_POINT and n % 3 == 2:
                small_step()

    fill = R.fill[0]
    words = M // LANES // 8
    many = LANES * LANES // T
    loads.idx.wait()
    for h in range(NH):
        at = R.idxv[h]
        hi = at // LANES
        R.lo[h] = at - hi * LANES
        one = jnp.left_shift(1, 4 * lax.rem(hi, 8))
        for w in range(words):
            ok = (at < fill) & (hi >= 8 * w) & (hi < 8 * w + 8)
            R.inc[h, w] = jnp.where(ok, one, 0)
    for copy in (loads.tok, loads.wq, loads.wk, loads.wv):
        copy.wait()

    def begin_block(i, c):
        for r in range(0, LANES, CHUNK):
            rows = pl.ds(pl.multiple_of(i * LANES + r, CHUNK), CHUNK)
            cen, rstd = row_stats(R.tokv[rows, :].astype(F32))
            R.nrm[rows, :] = (cen * rstd * R.g1[...] + R.s1[...]).astype(BF)
        rows = pl.ds(pl.multiple_of(i * LANES, LANES), LANES)
        own = pl.ds(pl.multiple_of(T + i * LANES, LANES), LANES)
        low = R.nrm[rows, :]
        R.q[rows, :] = nn(low, R.wqkv[:, 0:G]).astype(BF)
        R.kext[own, :] = nn(low, R.wqkv[:, G : 2 * G]).astype(BF)
        R.vext[own, :] = nn(low, R.wqkv[:, 2 * G : W3]).astype(BF)
        lane = lax.broadcasted_iota(jnp.int32, (many, T), 0) + i * many
        for h in range(NH):
            for w in range(words):
                even = odd = jnp.zeros((many, T), jnp.int32)
                for first in range(0, cfg.K, 15):
                    got = jnp.zeros((many, T), jnp.int32)
                    for k in range(first, min(first + 15, cfg.K)):
                        hit = jnp.broadcast_to(R.lo[h, pl.ds(k, 1), :], (many, T)) == lane
                        got = got + jnp.where(hit, jnp.broadcast_to(R.inc[h, w, pl.ds(k, 1), :], (many, T)), 0)
                    even = even + (got & 0x0F0F0F0F)
                    odd = odd + ((got >> 4) & 0x0F0F0F0F)
                at = pl.ds(pl.multiple_of(i * many, many), many)
                R.cntt[h, 2 * w, at, :] = even
                R.cntt[h, 2 * w + 1, at, :] = odd
        return c

    lax.fori_loop(0, T // LANES, begin_block, 0)
    for h in range(NH):
        for a in range(2 * words):
            R.cnt[h, a] = R.cntt[h, a].T

    band_row = lax.dot_general(
        R.table[...], R.oh[...], (((1,), (0,)), ((), ())), precision=EXACT, preferred_element_type=F32
    )
    u_at = lax.broadcasted_iota(jnp.int32, (NH, KW), 1)
    band_row = jnp.where((u_at >= 1) & (u_at <= T), band_row, NEGATIVE)
    for h in range(NH):
        wide = jnp.broadcast_to(band_row[h : h + 1, :], (HB, KW))
        R.band[h] = pltpu.roll(wide, 0, 1, stride=1, stride_axis=0)

    for j in range(U // LANES):
        R.ibv[:, j * LANES : (j + 1) * LANES] = R.ib[j : j + 1, :].astype(F32)
    mix = jax.nn.sigmoid(R.gate[...])
    pl.semaphore_wait(barrier, want)
    loads.og.wait()
    grad_desc(0).start()

    for copy in (loads.ck, loads.cv, loads.mk, loads.mv, loads.wo, loads.wu):
        copy.wait()

    def near_probs(rb, h, raw):
        for r in range(0, HB, CHUNK):
            s = raw[r : r + CHUNK] * scale + R.band[h, r : r + CHUNK, :]
            e = jnp.exp(s - jnp.max(s, axis=-1, keepdims=True))
            p = e * (1.0 / jnp.sum(e, axis=-1, keepdims=True))
            R.pl[h, pl.ds(rb * HB + r, CHUNK), :] = p.astype(BF)

    def far_probs(rb, h, raw):
        for r in range(0, HB, CHUNK):
            at = pl.ds(rb * HB + r, CHUNK)
            fields = []
            for f in range(M // LANES):
                word = R.cnt[h, f // 8 * 2 + f % 2, at, :]
                fields.append(((word >> (8 * (f % 8 // 2))) & 255).astype(F32))
            c = jnp.concatenate(fields, axis=1)
            s = jnp.where(c > 0.0, raw[r : r + CHUNK] * scale, NEGATIVE)
            top = jnp.maximum(jnp.max(s, axis=-1, keepdims=True), 0.0)
            e = jnp.exp(s - top) * c
            total = jnp.exp(-top) + jnp.sum(e, axis=-1, keepdims=True)
            R.pm[h, at, :] = (e * (1.0 / total)).astype(BF)

    def attend(rb, hook):
        rows = pl.ds(rb * HB, HB)
        wide = pl.ds(rb * HB, KW)
        heads = [slice(h * DH, (h + 1) * DH) for h in range(NH)]
        ahead = list(range(U // TILE))

        def side():
            if ahead:
                cols = slice(ahead[0] * TILE, (ahead.pop(0) + 1) * TILE)
                R.ga[rows, cols] = nt(R.ogv[rows, :], R.wuv[cols, :])

        near_raw = nt(R.q[rows, heads[0]], R.kext[wide, heads[0]])
        for h in range(NH):
            cols = heads[h]
            q = R.q[rows, cols]
            far_raw = nt(q, R.mkv[:, cols])
            side()
            near_probs(rb, h, near_raw)
            if h + 1 < NH:
                near_raw = nt(R.q[rows, heads[h + 1]], R.kext[wide, heads[h + 1]])
            near = nn(R.pl[h, rows, :], R.vext[wide, cols])
            if h == 0:
                hook()
            side()
            far_probs(rb, h, far_raw)
            far = nn(R.pm[h, rows, :], R.mvv[:, cols])
            m = mix[:, h : h + 1]
            R.diff[rows, cols] = far - near
            R.joined[rows, cols] = (m * far + (1.0 - m) * near).astype(BF)
        while ahead:
            side()

    def project(rb):
        rows = pl.ds(rb * HB, HB)
        for j in range(D // TILE):
            cols = slice(j * TILE, (j + 1) * TILE)
            R.part[0, rows, cols] = nn(R.joined[rows, :], R.wov[:, cols]).astype(BF)

    attend(0, lambda: None)
    project(0)
    push(0, 0)
    attend(1, lambda: mid(0, 0))
    project(1)
    push(0, 1)

    loads.wi.wait()

    def tiles(count, fn):
        lax.fori_loop(0, count, lambda j, c: (fn(pl.ds(pl.multiple_of(j * TILE, TILE), TILE)), c)[1], 0)

    def second_norm(hf):
        def visit(rows, mine, total):
            x = R.tokv[rows, :].astype(F32) + total
            R.resid[mine, :] = x
            cen, rstd = row_stats(x)
            R.ntl[rows, :] = (cen * rstd * R.g2[...] + R.s2[...]).astype(BF)

        fin(0, hf, visit)
        share_desc(0, hf, R.ntl, core).start()

    def feed(hf):
        rows = pl.ds(hf * HB, HB)
        count = U // TILE
        places = [lax.rem(j + count // 2 * (1 - half), count) * TILE for j in range(count)]
        blocks = [pl.ds(pl.multiple_of(at, TILE), TILE) for at in places]

        def unit(cols, pre):
            bias = R.ibv[:, cols]
            sums = jnp.zeros((1, TILE), F32)
            for r in range(0, HB, CHUNK):
                at = pl.ds(hf * HB + r, CHUNK)
                x = pre[r : r + CHUNK] + bias
                x2 = x * x
                t = jnp.tanh(GELU_A * (x + GELU_B * x * x2))
                R.act[at, cols] = (0.5 * x * (1.0 + t)).astype(BF)
                slope = 0.5 * (1.0 + t) + 0.5 * x * (1.0 - t * t) * (GELU_A * (1.0 + 3.0 * GELU_B * x2))
                gi = (R.ga[at, cols] * slope).astype(BF)
                R.gi[at, cols] = gi
                sums = sums + jnp.sum(gi.astype(F32), axis=0, keepdims=True)
            R.gib[pl.ds(hf, 1), cols] = sums

        pre = nn(R.ntl[rows, :], R.wiv[:, blocks[0]])
        for j, cols in enumerate(blocks):
            later = nn(R.ntl[rows, :], R.wiv[:, blocks[j + 1]]) if j + 1 < count else None
            unit(cols, pre)
            pre = later
            if 2 * (j + 1) == count:
                active_desc(hf).start()
            elif 2 * j >= count:
                R.tr[pl.ds(j * TILE - UH, TILE), rows] = R.act[rows, cols].T
        R.trn[:, rows] = R.ntl[rows, :].T

        def back(cols):
            R.part[1, rows, cols] = nt(R.gi[rows, :], R.wiv[cols, :]).astype(BF)

        tiles(D // TILE, back)

    second_norm(0)
    mid(0, 1)
    share_desc(0, 0, R.ntl, 1 - core).wait_recv()
    feed(0)
    push(1, 0)
    grad_desc(0).wait_recv()
    grad_desc(1).start()
    second_norm(1)
    mid(1, 0)
    share_desc(0, 1, R.ntl, 1 - core).wait_recv()
    feed(1)
    push(1, 1)

    for j in range(U // TILE):
        g[D // TILE + j] = nn(R.trn[...], R.gi[:, j * TILE : (j + 1) * TILE]).astype(BF)
        dp_begin(D // TILE + j)
        if j == 1:
            mid(1, 1)
    for hf in range(HALVES):
        active_desc(hf).wait_recv()
        R.tr[UH:U, hf * HB : (hf + 1) * HB] = R.gt[hf * HB : (hf + 1) * HB, 0:UH].T
    grad_desc(1).wait_recv()
    mine = pl.ds(pl.multiple_of(half * UH, TILE), UH)
    for j in range(D // TILE):
        cols = slice(j * TILE, (j + 1) * TILE)
        g[j, mine, :] = (nn(R.tr[0:UH, :], R.ogv[0:T, cols]) + nn(R.tr[UH:U, :], R.ogv[T : 2 * T, cols])).astype(BF)
        dp_begin(j)
    sent(0)
    at_point(1)

    def fed(hf, j):
        rows = pl.ds(hf * HB, HB)
        cols = slice(j * TILE, (j + 1) * TILE)
        R.part[0, rows, cols] = nn(R.act[rows, :], R.wuv[:, cols]).astype(BF)

    for j in range(D // TILE):
        fed(0, j)
    push(2, 0)
    at_point(2)
    R.trn[...] = R.nrm[...].T
    at_point(3)

    def norm_back(p, hf, source, gain, base, keep, out, side=()):
        gain_sum, shift_sum = [jnp.zeros((1, D), F32)], [jnp.zeros((1, D), F32)]

        def visit(rows, mine, dy):
            cen, rstd = row_stats(source(rows, mine))
            xh = cen * rstd
            gain_sum[0] = gain_sum[0] + jnp.sum(dy * xh, axis=0, keepdims=True)
            shift_sum[0] = shift_sum[0] + jnp.sum(dy, axis=0, keepdims=True)
            dx = dy * gain
            dx = rstd * (
                dx - jnp.mean(dx, axis=-1, keepdims=True) - xh * jnp.mean(dx * xh, axis=-1, keepdims=True)
            )
            got = base(rows, mine) + dx
            if keep is not None:
                keep[mine, :] = got
            out[rows, :] = got.astype(BF)

        fin(p, hf, visit, side)
        share_desc(p, hf, out, core).start()
        return gain_sum[0], shift_sum[0]

    sums = []
    for hf in range(HALVES):
        sums.append(
            norm_back(
                1, hf, lambda rows, mine: R.resid[mine, :], R.g2[...],
                lambda rows, mine: R.ogv[rows, :].astype(F32), R.gres, R.gat,
                [functools.partial(fed, 1, j) for j in range(D // TILE)] if hf == 0 else (),
            )
        )
        if hf == 0:
            push(2, 1)
        at_point(4 + hf)
    R.small[0, 2:3, :] = sums[0][0] + sums[1][0]
    R.small[0, 3:4, :] = sums[0][1] + sums[1][1]
    for hf in range(HALVES):
        mid(2, hf)
    for hf in range(HALVES):
        share_desc(1, hf, R.gat, 1 - core).wait_recv()

    gate_sums = [jnp.zeros((1, 1), F32) for _ in range(NH)]
    for rb in range(2):
        rows = pl.ds(rb * HB, HB)
        gj = nt(R.gat[rows, :], R.wov[...])
        for h in range(NH):
            cols = slice(h * DH, (h + 1) * DH)
            m = mix[:, h : h + 1]
            gate_sums[h] = gate_sums[h] + jnp.sum(
                jnp.sum(gj[:, cols] * R.diff[rows, cols], axis=0, keepdims=True), axis=1, keepdims=True
            )
            R.gl[rows, cols] = ((1.0 - m) * gj[:, cols]).astype(BF)
            R.gm[rows, cols] = (m * gj[:, cols]).astype(BF)

    at_point(6)

    def own_keys(weights, other, out, point):
        for h in range(NH):
            cols = slice(h * DH, (h + 1) * DH)
            spot = slice(out * G + h * DH, out * G + (h + 1) * DH)
            top = tn(weights[h, 0:HB, T:KW], other[0:HB, cols]) + tn(weights[h, HB:T, HB:T], other[HB:T, cols])
            R.gqkv[0:HB, spot] = top.astype(BF)
            R.gqkv[HB:T, spot] = tn(weights[h, HB:T, T:KW], other[HB:T, cols]).astype(BF)
            if h == 0:
                at_point(point)

    def weight_seg(seg, out):
        g[seg] = nn(R.trn[...], R.gqkv[:, out * G : (out + 1) * G]).astype(BF)

    LATE = cfg.late
    for j in range(D // TILE):
        g[LATE, j * G : (j + 1) * G, :] = tn(R.joined[...], R.gat[:, j * TILE : (j + 1) * TILE]).astype(BF)
    dp_begin(LATE)
    at_point(7)
    own_keys(R.pl, R.gl, 2, 8)
    weight_seg(LATE + 1, 2)
    dp_begin(LATE + 1)
    at_point(9)
    parts = [(rb, h, far) for rb in range(2) for h in range(NH) for far in range(2)]
    near_grads = [None]

    def span(part):
        rb, h, _ = part
        return pl.ds(rb * HB, HB), pl.ds(rb * HB, KW), slice(h * DH, (h + 1) * DH)

    def first_product(part):
        rows, wide, cols = span(part)
        if part[2]:
            return nt(R.gm[rows, cols], R.mvv[:, cols])
        return nt(R.gl[rows, cols], R.vext[wide, cols])

    def last_product(part):
        rows, wide, cols = span(part)
        if part[2]:
            R.gqkv[rows, cols] = (near_grads[0] + nn(R.pm[part[1], rows, :], R.mkv[:, cols])).astype(BF)
        else:
            near_grads[0] = nn(R.pl[part[1], rows, :], R.kext[wide, cols])

    def score_grads(part, dp):
        rb, h, far = part
        probs = R.pm if far else R.pl
        for r in range(0, HB, CHUNK):
            at = pl.ds(rb * HB + r, CHUNK)
            p, d = probs[h, at, :].astype(F32), dp[r : r + CHUNK]
            ds = p * (d - jnp.sum(p * d, axis=-1, keepdims=True))
            if not far and rb == 0:
                R.band[h, pl.ds(r, CHUNK), :] = ds
            elif not far:
                R.band[h, pl.ds(r, CHUNK), :] += ds
            probs[h, at, :] = (ds * scale).astype(BF)

    dp = first_product(parts[0])
    for i, part in enumerate(parts):
        later = first_product(parts[i + 1]) if i + 1 < len(parts) else None
        if i > 0:
            last_product(parts[i - 1])
        score_grads(part, dp)
        dp = later
        at_point(10 + i)
    last_product(parts[-1])

    weight_seg(LATE + 2, 0)
    dp_begin(LATE + 2)
    at_point(18)
    own_keys(R.pl, R.q, 1, 19)
    weight_seg(LATE + 3, 1)
    dp_begin(LATE + 3)
    at_point(20)
    sent(1)
    at_row = lax.broadcasted_iota(jnp.int32, (8, KW), 0)
    table_grads = []

    def table_grad(h):
        half_rows = HB
        cur = R.band[h]
        while half_rows > 8:
            half_rows //= 2
            cur = cur[:half_rows] + pltpu.roll(cur[half_rows:], KW - half_rows, 1)
        for bit in (1, 2, 4):
            cur = jnp.where(lax.rem(at_row // bit, 2) == 1, pltpu.roll(cur, KW - bit, 1), cur)
        diag = jnp.sum(cur, axis=0, keepdims=True)
        table_grads.append(
            lax.dot_general(diag, R.oh[...], (((1,), (1,)), ((), ())), precision=EXACT, preferred_element_type=F32)
        )

    for hf in range(HALVES):
        rows = pl.ds(hf * HB, HB)

        for j in range(D // TILE):
            cols = slice(j * TILE, (j + 1) * TILE)
            R.part[1, rows, cols] = nt(R.gqkv[rows, :], R.wqkv[cols, :]).astype(BF)
        if hf < NH:
            table_grad(hf)
        push(3, hf)
        at_point(21 + hf)

    for hf in range(HALVES):

        def result(rows, mine, total):
            R.bo[rows, :] = (R.resid[mine, :] + total).astype(BF)

        fin(2, hf, result)
        share_desc(2, hf, R.bo, core).start()
    at_point(23)
    for hf in range(HALVES):
        mid(3, hf)
    at_point(24)

    at_point(25)
    at_point(26)
    for h in range(HALVES, NH):
        table_grad(h)
    smalls[0, 4:5, :] = R.gib[0:1, :] + R.gib[1:2, :]
    smalls[0, 5:8, :] = jnp.zeros((3, D), F32)
    for h in range(NH):
        s = mix[:, h : h + 1]
        smalls[0, 5:6, h * LANES : h * LANES + NB] = table_grads[h]
        smalls[0, 6:7, h * LANES : (h + 1) * LANES] = jnp.broadcast_to(gate_sums[h] * s * (1.0 - s), (1, LANES))

    at_point(27)
    sums = []
    for hf in range(HALVES):
        sums.append(
            norm_back(
                3, hf, lambda rows, mine: R.tokv[rows, :].astype(F32), R.g1[...],
                lambda rows, mine: R.gres[mine, :], None, R.gt,
            )
        )
        at_point(28 + hf)
    smalls[0, 0:1, :] = sums[0][0] + sums[1][0]
    smalls[0, 1:2, :] = sums[0][1] + sums[1][1]
    small_desc(0).start()

    for hf in range(HALVES):
        share_desc(2, hf, R.bo, 1 - core).wait_recv()
        share_desc(3, hf, R.gt, 1 - core).wait_recv()
    emit(R.bo, R.block_out)
    emit(R.gt, R.gtok)
    at_point(LAST_POINT)
    for _ in partners:
        small_step()

    sent(2)
    sent(3)
    grad_desc(0).wait_send()
    grad_desc(1).wait_send()
    for hf in range(HALVES):
        active_desc(hf).wait_send()
    for p in range(4):
        for hf in range(HALVES):
            share_desc(p, hf, (R.ntl, R.gat, R.bo, R.gt)[p], core).wait_send()
    for i in range(len(partners)):
        small_desc(i).wait_send()
    for seg in range(len(SEGMENTS)):
        dp_close(seg)
    for c in outs:
        c.wait()


def local(n, tokens, wq, wk, wv, wo, wi, ib, wu, g1, s1, g2, s2, table, gate, ck, cv, mk, mv, idx, fill, og):
    T, D = tokens.shape
    NH = table.shape[0]
    G = wq.shape[1]
    U = wi.shape[1]
    M = mk.shape[1]
    K = idx.shape[2]
    HB = T // 2
    KW = T + HB
    stages = stage_list(n)
    doubling = []
    s = 1
    while s < n:
        doubling.append(s)
        s *= 2
    ffn = (D + U) // TILE
    late = 1 + 3 * G // TILE
    nseg = ffn + late
    seg = D
    offsets, rows_needed = [], 0
    for kind in SEGMENTS:
        offsets.append(rows_needed)
        rows_needed += plan_of(kind, stages, seg)[1]
    inputs = dict(
        tok=tokens, idx=idx.transpose(1, 2, 0), wq=wq, wk=wk, wv=wv, wo=wo, wi=wi, wu=wu, ck=ck, cv=cv, mk=mk, mv=mv, og=og
    )
    vectors = dict(
        ib=ib.reshape(U // LANES, LANES), g1=g1.reshape(1, D), s1=s1.reshape(1, D), g2=g2.reshape(1, D), s2=s2.reshape(1, D),
        table=table, gate=gate.reshape(1, NH), oh=jnp.asarray(bucket_rows(T)),
    )
    outputs = dict(
        block_out=((T, D), BF), gtok=((T, D), BF), gwq=((D, G), BF), gwk=((D, G), BF), gwv=((D, G), BF),
        gwo=((G, D), BF), gwi=((D, U), BF), gwu=((U, D), BF), gsmall=((8, D), F32),
    )
    S = len(stages)
    sem = pltpu.SemaphoreType.DMA
    scratch = dict(
        tokv=pltpu.VMEM((T, D), BF), ogv=pltpu.VMEM((2 * T, D), BF), idxv=pltpu.VMEM((NH, K, T), jnp.int32),
        wqkv=pltpu.VMEM((D, 3 * G), BF), wov=pltpu.VMEM((G, D), BF), wiv=pltpu.VMEM((D, U), BF),
        wuv=pltpu.VMEM((U, D), BF), kext=pltpu.VMEM((2 * T, G), BF), vext=pltpu.VMEM((2 * T, G), BF),
        mkv=pltpu.VMEM((M, G), BF), mvv=pltpu.VMEM((M, G), BF),
        lo=pltpu.VMEM((NH, K, T), jnp.int32), inc=pltpu.VMEM((NH, M // LANES // 8, K, T), jnp.int32),
        cntt=pltpu.VMEM((NH, M // LANES // 4, LANES, T), jnp.int32),
        cnt=pltpu.VMEM((NH, M // LANES // 4, T, LANES), jnp.int32),
        nrm=pltpu.VMEM((T, D), BF), q=pltpu.VMEM((T, G), BF), band=pltpu.VMEM((NH, HB, KW), F32),
        pl=pltpu.VMEM((NH, T, KW), BF), pm=pltpu.VMEM((NH, T, M), BF), diff=pltpu.VMEM((T, G), F32),
        joined=pltpu.VMEM((T, G), BF), ga=pltpu.VMEM((T, U), F32), ntl=pltpu.VMEM((T, D), BF),
        resid=pltpu.VMEM((HB, D), F32), act=pltpu.VMEM((T, U), BF), gi=pltpu.VMEM((T, U), BF),
        gib=pltpu.VMEM((8, U), F32), ibv=pltpu.VMEM((1, U), F32), tr=pltpu.VMEM((U, T), BF), trn=pltpu.VMEM((D, T), BF), gres=pltpu.VMEM((HB, D), F32),
        gat=pltpu.VMEM((T, D), BF), gl=pltpu.VMEM((T, G), BF), gm=pltpu.VMEM((T, G), BF),
        gqkv=pltpu.VMEM((T, 3 * G), BF), bo=pltpu.VMEM((T, D), BF), gt=pltpu.VMEM((T, D), BF),
        part=pltpu.VMEM((2, T, D), BF), cbuf=pltpu.VMEM((2, HB, D), BF), ybuf=pltpu.VMEM((2, HB, D), BF),
        small=pltpu.VMEM((len(doubling) + 2, 8, D), F32), sbuf=pltpu.VMEM((len(doubling) + 1, 8, D), F32),
        g=pltpu.VMEM((nseg, seg, TILE), BF), res=pltpu.VMEM((nseg, seg, TILE), BF),
        rbuf=pltpu.VMEM((rows_needed, TILE), BF),
        in_sem=sem((13,)), out_sem=sem((2 + 2 * (D // TILE) + U // TILE + 4,)),
        c_send=sem((4, HALVES)), c_recv=sem((4, HALVES)), y_send=sem((4, HALVES)), y_recv=sem((4, HALVES)),
        a_send=sem((4, HALVES)), a_recv=sem((4, HALVES)),
        s_send=sem((len(doubling) + 1,)), s_recv=sem((len(doubling) + 1,)),
        dp_send=sem((nseg, S, 2, 3, 4)), dp_recv=sem((nseg, S, 2, 3, 2)),
        x_send=sem((HALVES + 2,)), x_recv=sem((HALVES + 2,)),
    )
    cfg = Space(
        n=n, T=T, D=D, G=G, U=U, M=M, NH=NH, K=K, stages=stages, doubling=doubling, seg=seg, offsets=offsets,
        late=ffn,
        names=[*inputs, *vectors, "fill", *outputs, *scratch],
    )
    any_spec = pl.BlockSpec(memory_space=pl.ANY)
    vec_spec = pl.BlockSpec(memory_space=pltpu.VMEM)
    outs = pl.pallas_call(
        functools.partial(kernel, cfg),
        out_shape=[jax.ShapeDtypeStruct(*v) for v in outputs.values()],
        in_specs=[any_spec] * len(inputs) + [vec_spec] * len(vectors) + [pl.BlockSpec(memory_space=pltpu.SMEM)],
        out_specs=[any_spec] * len(outputs),
        scratch_shapes=list(scratch.values()),
        compiler_params=pltpu.CompilerParams(
            collective_id=0, has_side_effects=True, vmem_limit_bytes=63 * MIB
        ),
        cost_estimate=pl.CostEstimate(flops=12 * 10**9, bytes_accessed=20 * 10**6, transcendentals=3 * 10**6),
    )(
        *inputs.values(), *vectors.values(), fill,
    )
    return widen(outs, NH)


def widen_kernel(NH, cuts, *refs):
    ins, outs, scratch = refs[:9], refs[9:24], refs[24:]
    boxes = len(cuts)
    low, (in_sem, out_sem), high = scratch[:boxes], scratch[boxes : boxes + 2], list(scratch[boxes + 2 :])
    high = [low[n] if cut[0] < 2 else high.pop(0) for n, cut in enumerate(cuts)]
    loads, stores = [], []
    for n, (i, at, rows, cols) in enumerate(cuts):
        loads.append(pltpu.make_async_copy(ins[i].at[pl.ds(at, rows)], low[n], in_sem.at[n]))
        stores.append(pltpu.make_async_copy(high[n], outs[i].at[pl.ds(at, rows)], out_sem.at[n]))
        loads[n].start()
    small = ins[8]
    for i in range(5):
        outs[8 + i][...] = small[i : i + 1, :]
    for h in range(NH):
        outs[13][h : h + 1, :] = small[5:6, h * LANES : h * LANES + NB]
        outs[14][:, h : h + 1] = small[6:7, h * LANES : h * LANES + 1]
    for n, (i, at, rows, cols) in enumerate(cuts):
        loads[n].wait()
        if high[n] is not low[n]:
            high[n][...] = low[n][...].astype(F32)
        stores[n].start()
    for c in stores:
        c.wait()


def widen(sums, NH):
    small = sums[8]
    D = small.shape[1]
    cuts = []
    for i in (2, 3, 4, 5, 6, 7, 0, 1):
        rows, cols = sums[i].shape
        step = max(16, min(rows, 2 * TILE * D // cols))
        cuts += [(i, at, step, cols) for at in range(0, rows, step)]
    shapes = [jax.ShapeDtypeStruct(x.shape, BF if i < 2 else F32) for i, x in enumerate(sums[:8])]
    tiny = [(1, D)] * 5 + [(NH, NB), (1, NH)]
    hbm = pl.BlockSpec(memory_space=pl.ANY)
    vec = pl.BlockSpec(memory_space=pltpu.VMEM)
    got = pl.pallas_call(
        functools.partial(widen_kernel, NH, cuts),
        in_specs=[hbm] * 8 + [vec],
        out_specs=[hbm] * 8 + [vec] * len(tiny),
        out_shape=shapes + [jax.ShapeDtypeStruct(x, F32) for x in tiny],
        scratch_shapes=[pltpu.VMEM((rows, cols), BF) for _, _, rows, cols in cuts]
        + [pltpu.SemaphoreType.DMA((len(cuts),))] * 2
        + [pltpu.VMEM((rows, cols), F32) for i, _, rows, cols in cuts if i >= 2],
        compiler_params=pltpu.CompilerParams(vmem_limit_bytes=60 * MIB),
        cost_estimate=pl.CostEstimate(flops=0, bytes_accessed=22 * 10**6, transcendentals=0),
    )(*sums)
    block_out, gtok, gwq, gwk, gwv, gwo, gwi, gwu, g1, s1, g2, s2, ib, bias, gates = got
    return (
        block_out, gtok, gwq, gwk, gwv, gwo, gwi, ib.reshape(-1), gwu, g1.reshape(D), s1.reshape(D), g2.reshape(D),
        s2.reshape(D), bias, gates.reshape(NH),
    )


def solution(mesh):
    return jax.shard_map(
        functools.partial(local, mesh.shape["dp"]),
        mesh=mesh,
        in_specs=(
            P("dp", None), P(None, "head"), P(None, "head"), P(None, "head"), P("head", None), P(None, "head"),
            P("head"), P("head", None), P(), P(), P(), P(), P("head", None), P("head"), P("dp", "head"),
            P("dp", "head"), P("dp", None, "head"), P("dp", None, "head"), P("dp", "head", None), P("dp"),
            P("dp", None),
        ),
        out_specs=(
            P("dp", None), P("dp", None), P(None, "head"), P(None, "head"), P(None, "head"), P("head", None),
            P(None, "head"), P("head"), P("head", None), P(), P(), P(), P(), P("head", None), P("head"),
        ),
        check_vma=False,
    )
```

```python
import functools
import math
from types import SimpleNamespace as Space

import jax
import jax.numpy as jnp
import numpy as np
from jax import lax
from jax.experimental import pallas as pl
from jax.experimental.pallas import tpu as pltpu
from jax.sharding import PartitionSpec as P

NB = 32
MAXD = 128
EPSILON = 1e-05
NEGATIVE = -1e30
EXACT = lax.Precision.HIGHEST
BF = jnp.bfloat16
F32 = jnp.float32
LANES = 128
TILE = 256
HALVES = 2
CHUNK = 32
MIB = 1 << 20
KINDS = dict(
    A=(False, False, False), a=(False, True, False), B=(True, False, False), C=(True, True, False),
    F=(False, False, True), f=(False, True, True),
)
SEGMENTS = "FfffBaaAAaCa"
LAST_POINT = 30
SCHEDULE = (
    (3, 4, 0), (4, 0, 0), (5, 5, 0), (7, 1, 0), (7, 4, 1), (7, 0, 1), (7, 2, 0), (10, 1, 1), (10, 6, 0),
    (10, 8, 0), (10, 2, 1), (10, 3, 0), (11, 4, 2), (11, 0, 2), (12, 1, 2), (12, 4, 3), (13, 5, 1), (13, 9, 0),
    (13, 1, 3), (13, 6, 1), (13, 2, 2), (14, 3, 1), (14, 8, 1), (15, 7, 0), (15, 2, 3), (15, 0, 3), (16, 4, 4),
    (16, 6, 2), (18, 3, 2), (20, 5, 2), (20, 3, 3), (20, 7, 1), (21, 0, 4), (21, 9, 1), (22, 6, 3), (23, 11, 0),
    (23, 5, 3), (23, 4, 5), (23, 5, 4), (23, 7, 2), (24, 8, 2), (24, 6, 4), (24, 9, 2), (24, 7, 3), (24, 0, 5),
    (24, 8, 3), (25, 10, 0), (27, 5, 5), (27, 4, 6), (27, 11, 1), (28, 9, 3), (28, 7, 4), (28, 10, 1), (30, 3, 4),
    (30, 9, 4), (30, 11, 2), (30, 8, 4), (30, 10, 2), (30, 7, 5), (30, 2, 4), (30, 4, 7), (30, 11, 3), (30, 0, 6),
    (30, 6, 5), (30, 7, 6), (30, 8, 5), (30, 9, 5), (30, 10, 3), (30, 8, 6), (30, 11, 4), (30, 7, 7), (30, 1, 4),
    (30, 10, 4), (30, 10, 5), (30, 8, 7), (30, 11, 5),
)
GELU_A = math.sqrt(2.0 / math.pi)
GELU_B = 0.044715


def bucket_rows(length):
    span = np.arange(length)
    exact = NB // 2
    ratio = np.log(np.maximum(span, 1) / exact) / np.log(MAXD / exact)
    larger = np.minimum(exact + (ratio * (NB - exact)).astype(np.int32), NB - 1)
    bucket = np.where(span < exact, span, larger).astype(np.int32)
    table = np.zeros((NB, length + length // 2), np.float32)
    for u in range(1, length + 1):
        table[bucket[length - u], u] = 1.0
    return table


def nn(a, b):
    return lax.dot_general(a, b, (((1,), (0,)), ((), ())), preferred_element_type=F32)


def nt(a, b):
    return lax.dot_general(a, b, (((1,), (1,)), ((), ())), preferred_element_type=F32)


def tn(a, b):
    return lax.dot_general(a, b, (((0,), (0,)), ((), ())), preferred_element_type=F32)


def row_stats(x):
    mean = jnp.mean(x, axis=-1, keepdims=True)
    c = x - mean
    var = jnp.mean(c * c, axis=-1, keepdims=True)
    return c, lax.rsqrt(var + EPSILON)


def stage_list(n):
    stages, stride, left = [], 1, n
    if left >= 2:
        stages.append((1, 2))
        stride, left = 2, left // 2
    while left >= 4:
        stages.append((stride, 4))
        stride, left = stride * 4, left // 4
    if left == 2:
        stages.append((stride, 2))
    return stages


def line_hops(r, middle):
    if r == 2 or not middle:
        scatter = [[(h, h + 1, 1), (r - 1 - h, r - 2 - h, 0)] for h in range(r - 1)]
        gather = [[(r - 1 - h, r - 2 - h, 1), (h, h + 1, 0)] for h in range(r - 1)]
        return scatter, gather, [(0, 0 if r == 2 else 1)] * (r - 1), 1 if r == 2 else 2, (0, r - 1)
    scatter = [[(0, 1, 1), (0, 1, 0), (3, 2, 0), (3, 2, 1)], [(1, 2, 1), (2, 1, 0)]]
    gather = [[(1, 2, 0), (1, 0, 0), (2, 1, 1), (2, 3, 1)], [(1, 0, 1), (2, 3, 0)]]
    return scatter, gather, [(0, 1), (2, 2)], 3, (1, 2)


def plan_of(kind, stages, seg):
    back, middle, factors = KINDS[kind]
    plan, off, size = [], 0, seg
    for t, (stride, r) in enumerate(stages[::-1] if back else stages):
        size //= 2
        scatter, gather, slots, count, owners = line_hops(r, middle)
        skip = factors and t == 0
        plan.append(
            Space(
                stride=stride, r=r, size=size, off=off, scatter=scatter, gather=gather, slots=slots, owners=owners, skip=skip
            )
        )
        off += 0 if skip else count * size
    return plan, off


def kernel(cfg, *refs):
    n = cfg.n
    R = Space(**dict(zip(cfg.names, refs)))
    T, D, G, U, M, NH = cfg.T, cfg.D, cfg.G, cfg.U, cfg.M, cfg.NH
    DH = G // NH
    HB = T // 2
    KW = T + HB
    scale = 1.0 / math.sqrt(DH)
    me = lax.axis_index("dp")
    hid = lax.axis_index("head")
    core = lax.rem(hid, 2)
    mate = {"head": hid + 1 - 2 * core}
    across = {"head": lax.rem(hid + 2, 4)}
    sub = HB // 2

    peers = []
    for stride, r in cfg.stages:
        d = lax.rem(me // stride, r)
        peers.append((d > 0, me - stride))
        peers.append((d < r - 1, me + stride))
    for s in cfg.doubling:
        covered = False
        for stride, r in cfg.stages:
            if s == stride:
                covered = True
        if not covered:
            b = lax.rem(me // s, 2)
            peers.append((True, me + s - 2 * s * b))
    barrier = pltpu.get_barrier_semaphore()
    want = 2
    pl.semaphore_signal(barrier, inc=1, device_id=mate)
    pl.semaphore_signal(barrier, inc=1, device_id=across)
    for cond, who in peers:
        if cond is True:
            pl.semaphore_signal(barrier, inc=1, device_id={"dp": who})
            want = want + 1
        else:

            @pl.when(cond)
            def _(who=who):
                pl.semaphore_signal(barrier, inc=1, device_id={"dp": who})

            want = want + jnp.where(cond, 1, 0).astype(jnp.int32)

    W3 = 3 * G
    loads = Space()

    def load(src, dst, sem):
        copy = pltpu.make_async_copy(src, dst, R.in_sem.at[sem])
        copy.start()
        return copy

    loads.tok = load(R.tok, R.tokv, 0)
    loads.idx = load(R.idx, R.idxv, 1)
    loads.wq = load(R.wq, R.wqkv.at[:, pl.ds(0, G)], 2)
    loads.wk = load(R.wk, R.wqkv.at[:, pl.ds(G, G)], 3)
    loads.wv = load(R.wv, R.wqkv.at[:, pl.ds(2 * G, G)], 4)
    loads.ck = load(R.ck, R.kext.at[pl.ds(0, T)], 5)
    loads.cv = load(R.cv, R.vext.at[pl.ds(0, T)], 6)
    loads.mk = load(R.mk.at[0], R.mkv, 7)
    loads.mv = load(R.mv.at[0], R.mvv, 8)
    loads.wo = load(R.wo, R.wov, 9)
    loads.og = load(R.og, R.ogv.at[pl.ds(0, T)], 10)
    loads.wu = load(R.wu, R.wuv, 11)
    loads.wi = load(R.wi, R.wiv, 12)


    def part_rows(hf, c):
        return pl.ds(pl.multiple_of(hf * HB + c * sub, sub), sub)

    def push_desc(p, hf):
        return pltpu.make_async_remote_copy(
            src_ref=R.part.at[p % 2, part_rows(hf, 1 - core)],
            dst_ref=R.cbuf.at[p % 2, pl.ds(hf * sub, sub)],
            send_sem=R.c_send.at[p, hf],
            recv_sem=R.c_recv.at[p, hf],
            device_id=mate,
            device_id_type=pl.DeviceIdType.MESH,
        )

    def cross_desc(p, hf):
        return pltpu.make_async_remote_copy(
            src_ref=R.part.at[p % 2, part_rows(hf, core)],
            dst_ref=R.ybuf.at[p % 2, pl.ds(hf * sub, sub)],
            send_sem=R.y_send.at[p, hf],
            recv_sem=R.y_recv.at[p, hf],
            device_id=across,
            device_id_type=pl.DeviceIdType.MESH,
        )

    def share_desc(p, hf, buf, c):
        rows = part_rows(hf, c)
        return pltpu.make_async_remote_copy(
            src_ref=buf.at[rows],
            dst_ref=buf.at[rows],
            send_sem=R.a_send.at[p, hf],
            recv_sem=R.a_recv.at[p, hf],
            device_id=mate,
            device_id_type=pl.DeviceIdType.MESH,
        )

    def push(p, hf):
        push_desc(p, hf).start()

    def mid(p, hf):
        push_desc(p, hf).wait_recv()
        for r in range(0, sub, CHUNK):
            rows = pl.ds(pl.multiple_of(hf * HB + core * sub + r, CHUNK), CHUNK)
            total = R.part[p % 2, rows, :].astype(F32) + R.cbuf[p % 2, pl.ds(hf * sub + r, CHUNK), :].astype(F32)
            R.part[p % 2, rows, :] = total.astype(BF)
        cross_desc(p, hf).start()

    def sent(p):
        for hf in range(HALVES):
            push_desc(p, hf).wait_send()
            cross_desc(p, hf).wait_send()

    def fin(p, hf, visit, side=()):
        cross_desc(p, hf).wait_recv()
        side = list(side)
        for r in range(0, sub, CHUNK):
            rows = pl.ds(pl.multiple_of(hf * HB + core * sub + r, CHUNK), CHUNK)
            mine = pl.ds(hf * sub + r, CHUNK)
            if side:
                side.pop(0)()
            visit(rows, mine, R.part[p % 2, rows, :].astype(F32) + R.ybuf[p % 2, mine, :].astype(F32))
        for work in side:
            work()

    g, res, rbuf = R.g, R.res, R.rbuf
    SEG = cfg.seg

    plans = {}
    for kind in sorted(set(SEGMENTS)):
        base, live = 0, None
        plan, _ = plan_of(kind, cfg.stages, SEG)
        for st in plan:
            st.d = lax.rem(me // st.stride, st.r)
            st.base, st.live = base, live
            base = base + st.size * (st.d // st.owners[1])
            if st.r > 2:
                owner = (st.d == st.owners[0]) | (st.d == st.owners[1])
                live = owner if live is None else live & owner
        phases = [(0, t, h) for t, st in enumerate(plan) if not st.skip for h in range(len(st.scatter))]
        phases += [(1, t, h) for t, st in reversed(list(enumerate(plan))) for h in range(len(st.gather))]
        plans[kind] = Space(stages=plan, own=base, own_size=plan[-1].size, live=live, phases=phases)

    def when(cond, live):
        return pl.when(cond if live is None else cond & live)

    def piece(st, hi):
        first = st.base + hi * st.size
        return pl.ds(first if isinstance(first, int) else pl.multiple_of(first, 16), st.size)

    def slot(seg, st, h, hi):
        return pl.ds(cfg.offsets[seg] + st.off + st.slots[h][hi] * st.size, st.size)

    def hop_desc(seg, phase, move):
        gather, t, h = phase
        st = plans[SEGMENTS[seg]].stages[t]
        a, b, hi = move
        return pltpu.make_async_remote_copy(
            src_ref=(res if gather else g).at[seg, piece(st, hi)],
            dst_ref=res.at[seg, piece(st, hi)] if gather else rbuf.at[slot(seg, st, h, hi)],
            send_sem=R.dp_send.at[seg, t, gather, h, 2 * hi + int(b > a)],
            recv_sem=R.dp_recv.at[seg, t, gather, h, hi],
            device_id={"dp": me + st.stride if b > a else me - st.stride},
            device_id_type=pl.DeviceIdType.MESH,
        )

    def moves_of(seg, phase):
        st = plans[SEGMENTS[seg]].stages[phase[1]]
        return (st.gather if phase[0] else st.scatter)[phase[2]]

    def add_in(seg, phase, hi):
        _, t, h = phase
        st = plans[SEGMENTS[seg]].stages[t]
        step = min(64, st.size)
        to, come = st.base + hi * st.size, cfg.offsets[seg] + st.off + st.slots[h][hi] * st.size

        def some(i, c):
            rows = pl.ds(pl.multiple_of(to + i * step, 16), step)
            total = g[seg, rows, :].astype(F32) + rbuf[pl.ds(pl.multiple_of(come + i * step, 16), step), :].astype(F32)
            g[seg, rows, :] = total.astype(BF)
            return c

        lax.fori_loop(0, st.size // step, some, 0)

    def dp_open(seg, k):
        plan = plans[SEGMENTS[seg]]
        phase = plan.phases[k]
        if phase[0] and (k == 0 or not plan.phases[k - 1][0]):

            @when(me >= 0, plan.live)
            def _():
                own = pl.ds(pl.multiple_of(plan.own, 16), plan.own_size)
                res[seg, own, :] = g[seg, own, :]

        st = plan.stages[phase[1]]
        for at in range(st.r):
            mine = [move for move in moves_of(seg, phase) if move[0] == at]
            if mine:

                @when(st.d == at, st.live)
                def _(mine=mine):
                    for move in mine:
                        hop_desc(seg, phase, move).start()

    def dp_phase(seg, k):
        plan = plans[SEGMENTS[seg]]
        phase = plan.phases[k]
        st = plan.stages[phase[1]]
        later = plan.phases[k + 1] if k + 1 < len(plan.phases) else None
        follows = later is not None and later[:2] == phase[:2]
        for at in range(st.r):
            mine = [move for move in moves_of(seg, phase) if move[1] == at]
            if mine:

                @when(st.d == at, st.live)
                def _(mine=mine, at=at):
                    for move in mine:
                        hop_desc(seg, phase, move).wait_recv()
                        if not phase[0]:
                            add_in(seg, phase, move[2])
                        for onward in moves_of(seg, later) if follows else ():
                            if onward[0] == at and onward[2] == move[2]:
                                hop_desc(seg, later, onward).start()

        if later is not None and not follows:
            dp_open(seg, k + 1)

    def advance(seg, k):
        parts = len([entry for entry in SCHEDULE if entry[1] == seg])
        total = len(plans[SEGMENTS[seg]].phases)
        for i in range(total * k // parts, total * (k + 1) // parts):
            dp_phase(seg, i)
        return k + 1 == parts

    def dp_begin(seg):
        dp_open(seg, 0)

    def dp_close(seg):
        plan = plans[SEGMENTS[seg]]
        for t, st in enumerate(plan.stages):
            for at in range(st.r):
                mine = [(ph, mv) for ph in plan.phases if ph[1] == t for mv in moves_of(seg, ph) if mv[0] == at]

                @when(st.d == at, st.live)
                def _(mine=mine):
                    for phase, move in mine:
                        hop_desc(seg, phase, move).wait_send()

    half = lax.rem(me, 2)
    pair = {"dp": me + 1 - 2 * half}
    UH = U // 2

    def grad_desc(forward):
        rows = pl.ds(pl.multiple_of(core * HB, HB), HB)
        away = pl.ds(pl.multiple_of(T + core * HB, HB), HB)
        return pltpu.make_async_remote_copy(
            src_ref=R.ogv.at[away if forward else rows],
            dst_ref=R.ogv.at[away],
            send_sem=R.x_send.at[HALVES + forward],
            recv_sem=R.x_recv.at[HALVES + forward],
            device_id=mate if forward else pair,
            device_id_type=pl.DeviceIdType.MESH,
        )

    def active_desc(hf):
        rows = pl.ds(hf * HB, HB)
        return pltpu.make_async_remote_copy(
            src_ref=R.act.at[rows, pl.ds(pl.multiple_of((1 - half) * UH, TILE), UH)],
            dst_ref=R.gt.at[rows, pl.ds(0, UH)],
            send_sem=R.x_send.at[hf],
            recv_sem=R.x_recv.at[hf],
            device_id=pair,
            device_id_type=pl.DeviceIdType.MESH,
        )

    outs = []

    def emit(src, dst):
        c = pltpu.make_async_copy(src, dst, R.out_sem.at[len(outs)])
        c.start()
        outs.append(c)

    def emit_seg(j):
        if j < D // TILE:
            emit(res.at[j], R.gwu.at[:, pl.ds(j * TILE, TILE)])
        elif j < cfg.late:
            emit(res.at[j], R.gwi.at[:, pl.ds((j - D // TILE) * TILE, TILE)])
        elif j == cfg.late:
            for i in range(D // TILE):
                emit(res.at[j, pl.ds(i * G, G)], R.gwo.at[:, pl.ds(i * TILE, TILE)])
        else:
            emit(res.at[j], (R.gwv, R.gwq, R.gwk)[j - cfg.late - 1])

    partners = [mate]
    for s in cfg.doubling:
        partners.append({"dp": me + s - 2 * s * lax.rem(me // s, 2)})
    smalls = R.small
    small_at = [0]

    def small_desc(i):
        return pltpu.make_async_remote_copy(
            src_ref=smalls.at[i],
            dst_ref=R.sbuf.at[i],
            send_sem=R.s_send.at[i],
            recv_sem=R.s_recv.at[i],
            device_id=partners[i],
            device_id_type=pl.DeviceIdType.MESH,
        )

    def small_step():
        i = small_at[0]
        if i == len(partners):
            return
        small_at[0] = i + 1
        small_desc(i).wait_recv()
        got = R.sbuf[i]
        if i == 0:
            got = jnp.where(lax.broadcasted_iota(jnp.int32, (8, D), 0) < 4, got, 0.0)
        smalls[i + 1] = smalls[i] + got
        if i + 1 < len(partners):
            small_desc(i + 1).start()
        else:
            emit(smalls.at[i + 1], R.gsmall)

    def at_point(i):
        for n, (_, seg, k) in enumerate([entry for entry in SCHEDULE if entry[0] == i]):
            if advance(seg, k):
                emit_seg(seg)
            if i == LAST_POINT and n % 3 == 2:
                small_step()

    fill = R.fill[0]
    words = M // LANES // 8
    many = LANES * LANES // T
    loads.idx.wait()
    for h in range(NH):
        at = R.idxv[h]
        hi = at // LANES
        R.lo[h] = at - hi * LANES
        one = jnp.left_shift(1, 4 * lax.rem(hi, 8))
        for w in range(words):
            ok = (at < fill) & (hi >= 8 * w) & (hi < 8 * w + 8)
            R.inc[h, w] = jnp.where(ok, one, 0)
    for copy in (loads.tok, loads.wq, loads.wk, loads.wv):
        copy.wait()

    def begin_block(i, c):
        for r in range(0, LANES, CHUNK):
            rows = pl.ds(pl.multiple_of(i * LANES + r, CHUNK), CHUNK)
            cen, rstd = row_stats(R.tokv[rows, :].astype(F32))
            R.nrm[rows, :] = (cen * rstd * R.g1[...] + R.s1[...]).astype(BF)
        rows = pl.ds(pl.multiple_of(i * LANES, LANES), LANES)
        own = pl.ds(pl.multiple_of(T + i * LANES, LANES), LANES)
        low = R.nrm[rows, :]
        R.q[rows, :] = nn(low, R.wqkv[:, 0:G]).astype(BF)
        R.kext[own, :] = nn(low, R.wqkv[:, G : 2 * G]).astype(BF)
        R.vext[own, :] = nn(low, R.wqkv[:, 2 * G : W3]).astype(BF)
        lane = lax.broadcasted_iota(jnp.int32, (many, T), 0) + i * many
        for h in range(NH):
            for w in range(words):
                even = odd = jnp.zeros((many, T), jnp.int32)
                for first in range(0, cfg.K, 15):
                    got = jnp.zeros((many, T), jnp.int32)
                    for k in range(first, min(first + 15, cfg.K)):
                        hit = jnp.broadcast_to(R.lo[h, pl.ds(k, 1), :], (many, T)) == lane
                        got = got + jnp.where(hit, jnp.broadcast_to(R.inc[h, w, pl.ds(k, 1), :], (many, T)), 0)
                    even = even + (got & 0x0F0F0F0F)
                    odd = odd + ((got >> 4) & 0x0F0F0F0F)
                at = pl.ds(pl.multiple_of(i * many, many), many)
                R.cntt[h, 2 * w, at, :] = even
                R.cntt[h, 2 * w + 1, at, :] = odd
        return c

    lax.fori_loop(0, T // LANES, begin_block, 0)
    for h in range(NH):
        for a in range(2 * words):
            R.cnt[h, a] = R.cntt[h, a].T

    band_row = lax.dot_general(
        R.table[...], R.oh[...], (((1,), (0,)), ((), ())), precision=EXACT, preferred_element_type=F32
    )
    u_at = lax.broadcasted_iota(jnp.int32, (NH, KW), 1)
    band_row = jnp.where((u_at >= 1) & (u_at <= T), band_row, NEGATIVE)
    for h in range(NH):
        wide = jnp.broadcast_to(band_row[h : h + 1, :], (HB, KW))
        R.band[h] = pltpu.roll(wide, 0, 1, stride=1, stride_axis=0)

    for j in range(U // LANES):
        R.ibv[:, j * LANES : (j + 1) * LANES] = R.ib[j : j + 1, :].astype(F32)
    mix = jax.nn.sigmoid(R.gate[...])
    pl.semaphore_wait(barrier, want)
    loads.og.wait()
    grad_desc(0).start()

    for copy in (loads.ck, loads.cv, loads.mk, loads.mv, loads.wo, loads.wu):
        copy.wait()

    def near_probs(rb, h, raw):
        for r in range(0, HB, CHUNK):
            s = raw[r : r + CHUNK] * scale + R.band[h, r : r + CHUNK, :]
            e = jnp.exp(s - jnp.max(s, axis=-1, keepdims=True))
            p = e * (1.0 / jnp.sum(e, axis=-1, keepdims=True))
            R.pl[h, pl.ds(rb * HB + r, CHUNK), :] = p.astype(BF)

    def far_probs(rb, h, raw):
        for r in range(0, HB, CHUNK):
            at = pl.ds(rb * HB + r, CHUNK)
            fields = []
            for f in range(M // LANES):
                word = R.cnt[h, f // 8 * 2 + f % 2, at, :]
                fields.append(((word >> (8 * (f % 8 // 2))) & 255).astype(F32))
            c = jnp.concatenate(fields, axis=1)
            s = jnp.where(c > 0.0, raw[r : r + CHUNK] * scale, NEGATIVE)
            top = jnp.maximum(jnp.max(s, axis=-1, keepdims=True), 0.0)
            e = jnp.exp(s - top) * c
            total = jnp.exp(-top) + jnp.sum(e, axis=-1, keepdims=True)
            R.pm[h, at, :] = (e * (1.0 / total)).astype(BF)

    def attend(rb, hook):
        rows = pl.ds(rb * HB, HB)
        wide = pl.ds(rb * HB, KW)
        heads = [slice(h * DH, (h + 1) * DH) for h in range(NH)]
        ahead = list(range(U // TILE))

        def side():
            if ahead:
                cols = slice(ahead[0] * TILE, (ahead.pop(0) + 1) * TILE)
                R.ga[rows, cols] = nt(R.ogv[rows, :], R.wuv[cols, :])

        near_raw = nt(R.q[rows, heads[0]], R.kext[wide, heads[0]])
        for h in range(NH):
            cols = heads[h]
            q = R.q[rows, cols]
            far_raw = nt(q, R.mkv[:, cols])
            side()
            near_probs(rb, h, near_raw)
            if h + 1 < NH:
                near_raw = nt(R.q[rows, heads[h + 1]], R.kext[wide, heads[h + 1]])
            near = nn(R.pl[h, rows, :], R.vext[wide, cols])
            if h == 0:
                hook()
            side()
            far_probs(rb, h, far_raw)
            far = nn(R.pm[h, rows, :], R.mvv[:, cols])
            m = mix[:, h : h + 1]
            R.diff[rows, cols] = far - near
            R.joined[rows, cols] = (m * far + (1.0 - m) * near).astype(BF)
        while ahead:
            side()

    def project(rb):
        rows = pl.ds(rb * HB, HB)
        for j in range(D // TILE):
            cols = slice(j * TILE, (j + 1) * TILE)
            R.part[0, rows, cols] = nn(R.joined[rows, :], R.wov[:, cols]).astype(BF)

    attend(0, lambda: None)
    project(0)
    push(0, 0)
    attend(1, lambda: mid(0, 0))
    project(1)
    push(0, 1)

    loads.wi.wait()

    def tiles(count, fn):
        lax.fori_loop(0, count, lambda j, c: (fn(pl.ds(pl.multiple_of(j * TILE, TILE), TILE)), c)[1], 0)

    def second_norm(hf):
        def visit(rows, mine, total):
            x = R.tokv[rows, :].astype(F32) + total
            R.resid[mine, :] = x
            cen, rstd = row_stats(x)
            R.ntl[rows, :] = (cen * rstd * R.g2[...] + R.s2[...]).astype(BF)

        fin(0, hf, visit)
        share_desc(0, hf, R.ntl, core).start()

    def feed(hf):
        rows = pl.ds(hf * HB, HB)
        count = U // TILE
        places = [lax.rem(j + count // 2 * (1 - half), count) * TILE for j in range(count)]
        blocks = [pl.ds(pl.multiple_of(at, TILE), TILE) for at in places]

        def unit(cols, pre):
            bias = R.ibv[:, cols]
            sums = jnp.zeros((1, TILE), F32)
            for r in range(0, HB, CHUNK):
                at = pl.ds(hf * HB + r, CHUNK)
                x = pre[r : r + CHUNK] + bias
                x2 = x * x
                t = jnp.tanh(GELU_A * (x + GELU_B * x * x2))
                R.act[at, cols] = (0.5 * x * (1.0 + t)).astype(BF)
                slope = 0.5 * (1.0 + t) + 0.5 * x * (1.0 - t * t) * (GELU_A * (1.0 + 3.0 * GELU_B * x2))
                gi = (R.ga[at, cols] * slope).astype(BF)
                R.gi[at, cols] = gi
                sums = sums + jnp.sum(gi.astype(F32), axis=0, keepdims=True)
            R.gib[pl.ds(hf, 1), cols] = sums

        pre = nn(R.ntl[rows, :], R.wiv[:, blocks[0]])
        for j, cols in enumerate(blocks):
            later = nn(R.ntl[rows, :], R.wiv[:, blocks[j + 1]]) if j + 1 < count else None
            unit(cols, pre)
            pre = later
            if 2 * (j + 1) == count:
                active_desc(hf).start()
            elif 2 * j >= count:
                R.tr[pl.ds(j * TILE - UH, TILE), rows] = R.act[rows, cols].T
        R.trn[:, rows] = R.ntl[rows, :].T

        def back(cols):
            R.part[1, rows, cols] = nt(R.gi[rows, :], R.wiv[cols, :]).astype(BF)

        tiles(D // TILE, back)

    second_norm(0)
    mid(0, 1)
    share_desc(0, 0, R.ntl, 1 - core).wait_recv()
    feed(0)
    push(1, 0)
    grad_desc(0).wait_recv()
    grad_desc(1).start()
    second_norm(1)
    mid(1, 0)
    share_desc(0, 1, R.ntl, 1 - core).wait_recv()
    feed(1)
    push(1, 1)

    for j in range(U // TILE):
        g[D // TILE + j] = nn(R.trn[...], R.gi[:, j * TILE : (j + 1) * TILE]).astype(BF)
        dp_begin(D // TILE + j)
        if j == 1:
            mid(1, 1)
    for hf in range(HALVES):
        active_desc(hf).wait_recv()
        R.tr[UH:U, hf * HB : (hf + 1) * HB] = R.gt[hf * HB : (hf + 1) * HB, 0:UH].T
    grad_desc(1).wait_recv()
    mine = pl.ds(pl.multiple_of(half * UH, TILE), UH)
    for j in range(D // TILE):
        cols = slice(j * TILE, (j + 1) * TILE)
        g[j, mine, :] = (nn(R.tr[0:UH, :], R.ogv[0:T, cols]) + nn(R.tr[UH:U, :], R.ogv[T : 2 * T, cols])).astype(BF)
        dp_begin(j)
    sent(0)
    at_point(1)

    def fed(hf, j):
        rows = pl.ds(hf * HB, HB)
        cols = slice(j * TILE, (j + 1) * TILE)
        R.part[0, rows, cols] = nn(R.act[rows, :], R.wuv[:, cols]).astype(BF)

    for j in range(D // TILE):
        fed(0, j)
    push(2, 0)
    at_point(2)
    R.trn[...] = R.nrm[...].T
    at_point(3)

    def norm_back(p, hf, source, gain, base, keep, out, side=()):
        gain_sum, shift_sum = [jnp.zeros((1, D), F32)], [jnp.zeros((1, D), F32)]

        def visit(rows, mine, dy):
            cen, rstd = row_stats(source(rows, mine))
            xh = cen * rstd
            gain_sum[0] = gain_sum[0] + jnp.sum(dy * xh, axis=0, keepdims=True)
            shift_sum[0] = shift_sum[0] + jnp.sum(dy, axis=0, keepdims=True)
            dx = dy * gain
            dx = rstd * (
                dx - jnp.mean(dx, axis=-1, keepdims=True) - xh * jnp.mean(dx * xh, axis=-1, keepdims=True)
            )
            got = base(rows, mine) + dx
            if keep is not None:
                keep[mine, :] = got
            out[rows, :] = got.astype(BF)

        fin(p, hf, visit, side)
        share_desc(p, hf, out, core).start()
        return gain_sum[0], shift_sum[0]

    sums = []
    for hf in range(HALVES):
        sums.append(
            norm_back(
                1, hf, lambda rows, mine: R.resid[mine, :], R.g2[...],
                lambda rows, mine: R.ogv[rows, :].astype(F32), R.gres, R.gat,
                [functools.partial(fed, 1, j) for j in range(D // TILE)] if hf == 0 else (),
            )
        )
        if hf == 0:
            push(2, 1)
        at_point(4 + hf)
    R.small[0, 2:3, :] = sums[0][0] + sums[1][0]
    R.small[0, 3:4, :] = sums[0][1] + sums[1][1]
    for hf in range(HALVES):
        mid(2, hf)
    for hf in range(HALVES):
        share_desc(1, hf, R.gat, 1 - core).wait_recv()

    gate_sums = [jnp.zeros((1, 1), F32) for _ in range(NH)]
    for rb in range(2):
        rows = pl.ds(rb * HB, HB)
        gj = nt(R.gat[rows, :], R.wov[...])
        for h in range(NH):
            cols = slice(h * DH, (h + 1) * DH)
            m = mix[:, h : h + 1]
            gate_sums[h] = gate_sums[h] + jnp.sum(
                jnp.sum(gj[:, cols] * R.diff[rows, cols], axis=0, keepdims=True), axis=1, keepdims=True
            )
            R.gl[rows, cols] = ((1.0 - m) * gj[:, cols]).astype(BF)
            R.gm[rows, cols] = (m * gj[:, cols]).astype(BF)

    at_point(6)

    def own_keys(weights, other, out, point):
        for h in range(NH):
            cols = slice(h * DH, (h + 1) * DH)
            spot = slice(out * G + h * DH, out * G + (h + 1) * DH)
            top = tn(weights[h, 0:HB, T:KW], other[0:HB, cols]) + tn(weights[h, HB:T, HB:T], other[HB:T, cols])
            R.gqkv[0:HB, spot] = top.astype(BF)
            R.gqkv[HB:T, spot] = tn(weights[h, HB:T, T:KW], other[HB:T, cols]).astype(BF)
            if h == 0:
                at_point(point)

    def weight_seg(seg, out):
        g[seg] = nn(R.trn[...], R.gqkv[:, out * G : (out + 1) * G]).astype(BF)

    LATE = cfg.late
    for j in range(D // TILE):
        g[LATE, j * G : (j + 1) * G, :] = tn(R.joined[...], R.gat[:, j * TILE : (j + 1) * TILE]).astype(BF)
    dp_begin(LATE)
    at_point(7)
    own_keys(R.pl, R.gl, 2, 8)
    weight_seg(LATE + 1, 2)
    dp_begin(LATE + 1)
    at_point(9)
    parts = [(rb, h, far) for rb in range(2) for h in range(NH) for far in range(2)]
    near_grads = [None]

    def span(part):
        rb, h, _ = part
        return pl.ds(rb * HB, HB), pl.ds(rb * HB, KW), slice(h * DH, (h + 1) * DH)

    def first_product(part):
        rows, wide, cols = span(part)
        if part[2]:
            return nt(R.gm[rows, cols], R.mvv[:, cols])
        return nt(R.gl[rows, cols], R.vext[wide, cols])

    def last_product(part):
        rows, wide, cols = span(part)
        if part[2]:
            R.gqkv[rows, cols] = (near_grads[0] + nn(R.pm[part[1], rows, :], R.mkv[:, cols])).astype(BF)
        else:
            near_grads[0] = nn(R.pl[part[1], rows, :], R.kext[wide, cols])

    def score_grads(part, dp):
        rb, h, far = part
        probs = R.pm if far else R.pl
        for r in range(0, HB, CHUNK):
            at = pl.ds(rb * HB + r, CHUNK)
            p, d = probs[h, at, :].astype(F32), dp[r : r + CHUNK]
            ds = p * (d - jnp.sum(p * d, axis=-1, keepdims=True))
            if not far and rb == 0:
                R.band[h, pl.ds(r, CHUNK), :] = ds
            elif not far:
                R.band[h, pl.ds(r, CHUNK), :] += ds
            probs[h, at, :] = (ds * scale).astype(BF)

    dp = first_product(parts[0])
    for i, part in enumerate(parts):
        later = first_product(parts[i + 1]) if i + 1 < len(parts) else None
        if i > 0:
            last_product(parts[i - 1])
        score_grads(part, dp)
        dp = later
        at_point(10 + i)
    last_product(parts[-1])

    weight_seg(LATE + 2, 0)
    dp_begin(LATE + 2)
    at_point(18)
    own_keys(R.pl, R.q, 1, 19)
    weight_seg(LATE + 3, 1)
    dp_begin(LATE + 3)
    at_point(20)
    sent(1)
    at_row = lax.broadcasted_iota(jnp.int32, (8, KW), 0)
    table_grads = []

    def table_grad(h):
        half_rows = HB
        cur = R.band[h]
        while half_rows > 8:
            half_rows //= 2
            cur = cur[:half_rows] + pltpu.roll(cur[half_rows:], KW - half_rows, 1)
        for bit in (1, 2, 4):
            cur = jnp.where(lax.rem(at_row // bit, 2) == 1, pltpu.roll(cur, KW - bit, 1), cur)
        diag = jnp.sum(cur, axis=0, keepdims=True)
        table_grads.append(
            lax.dot_general(diag, R.oh[...], (((1,), (1,)), ((), ())), precision=EXACT, preferred_element_type=F32)
        )

    for hf in range(HALVES):
        rows = pl.ds(hf * HB, HB)

        for j in range(D // TILE):
            cols = slice(j * TILE, (j + 1) * TILE)
            R.part[1, rows, cols] = nt(R.gqkv[rows, :], R.wqkv[cols, :]).astype(BF)
        if hf < NH:
            table_grad(hf)
        push(3, hf)
        at_point(21 + hf)

    for hf in range(HALVES):

        def result(rows, mine, total):
            R.bo[rows, :] = (R.resid[mine, :] + total).astype(BF)

        fin(2, hf, result)
        share_desc(2, hf, R.bo, core).start()
    at_point(23)
    for hf in range(HALVES):
        mid(3, hf)
    at_point(24)

    at_point(25)
    at_point(26)
    for h in range(HALVES, NH):
        table_grad(h)
    smalls[0, 4:5, :] = R.gib[0:1, :] + R.gib[1:2, :]
    smalls[0, 5:8, :] = jnp.zeros((3, D), F32)
    for h in range(NH):
        s = mix[:, h : h + 1]
        smalls[0, 5:6, h * LANES : h * LANES + NB] = table_grads[h]
        smalls[0, 6:7, h * LANES : (h + 1) * LANES] = jnp.broadcast_to(gate_sums[h] * s * (1.0 - s), (1, LANES))

    at_point(27)
    sums = []
    for hf in range(HALVES):
        sums.append(
            norm_back(
                3, hf, lambda rows, mine: R.tokv[rows, :].astype(F32), R.g1[...],
                lambda rows, mine: R.gres[mine, :], None, R.gt,
            )
        )
        at_point(28 + hf)
    smalls[0, 0:1, :] = sums[0][0] + sums[1][0]
    smalls[0, 1:2, :] = sums[0][1] + sums[1][1]
    small_desc(0).start()

    for hf in range(HALVES):
        share_desc(2, hf, R.bo, 1 - core).wait_recv()
        share_desc(3, hf, R.gt, 1 - core).wait_recv()
    emit(R.bo, R.block_out)
    emit(R.gt, R.gtok)
    at_point(LAST_POINT)
    for _ in partners:
        small_step()

    sent(2)
    sent(3)
    grad_desc(0).wait_send()
    grad_desc(1).wait_send()
    for hf in range(HALVES):
        active_desc(hf).wait_send()
    for p in range(4):
        for hf in range(HALVES):
            share_desc(p, hf, (R.ntl, R.gat, R.bo, R.gt)[p], core).wait_send()
    for i in range(len(partners)):
        small_desc(i).wait_send()
    for seg in range(len(SEGMENTS)):
        dp_close(seg)
    for c in outs:
        c.wait()


def local(n, tokens, wq, wk, wv, wo, wi, ib, wu, g1, s1, g2, s2, table, gate, ck, cv, mk, mv, idx, fill, og):
    T, D = tokens.shape
    NH = table.shape[0]
    G = wq.shape[1]
    U = wi.shape[1]
    M = mk.shape[1]
    K = idx.shape[2]
    HB = T // 2
    KW = T + HB
    stages = stage_list(n)
    doubling = []
    s = 1
    while s < n:
        doubling.append(s)
        s *= 2
    ffn = (D + U) // TILE
    late = 1 + 3 * G // TILE
    nseg = ffn + late
    seg = D
    offsets, rows_needed = [], 0
    for kind in SEGMENTS:
        offsets.append(rows_needed)
        rows_needed += plan_of(kind, stages, seg)[1]
    inputs = dict(
        tok=tokens, idx=idx.transpose(1, 2, 0), wq=wq, wk=wk, wv=wv, wo=wo, wi=wi, wu=wu, ck=ck, cv=cv, mk=mk, mv=mv, og=og
    )
    vectors = dict(
        ib=ib.reshape(U // LANES, LANES), g1=g1.reshape(1, D), s1=s1.reshape(1, D), g2=g2.reshape(1, D), s2=s2.reshape(1, D),
        table=table, gate=gate.reshape(1, NH), oh=jnp.asarray(bucket_rows(T)),
    )
    outputs = dict(
        block_out=((T, D), BF), gtok=((T, D), BF), gwq=((D, G), BF), gwk=((D, G), BF), gwv=((D, G), BF),
        gwo=((G, D), BF), gwi=((D, U), BF), gwu=((U, D), BF), gsmall=((8, D), F32),
    )
    S = len(stages)
    sem = pltpu.SemaphoreType.DMA
    scratch = dict(
        tokv=pltpu.VMEM((T, D), BF), ogv=pltpu.VMEM((2 * T, D), BF), idxv=pltpu.VMEM((NH, K, T), jnp.int32),
        wqkv=pltpu.VMEM((D, 3 * G), BF), wov=pltpu.VMEM((G, D), BF), wiv=pltpu.VMEM((D, U), BF),
        wuv=pltpu.VMEM((U, D), BF), kext=pltpu.VMEM((2 * T, G), BF), vext=pltpu.VMEM((2 * T, G), BF),
        mkv=pltpu.VMEM((M, G), BF), mvv=pltpu.VMEM((M, G), BF),
        lo=pltpu.VMEM((NH, K, T), jnp.int32), inc=pltpu.VMEM((NH, M // LANES // 8, K, T), jnp.int32),
        cntt=pltpu.VMEM((NH, M // LANES // 4, LANES, T), jnp.int32),
        cnt=pltpu.VMEM((NH, M // LANES // 4, T, LANES), jnp.int32),
        nrm=pltpu.VMEM((T, D), BF), q=pltpu.VMEM((T, G), BF), band=pltpu.VMEM((NH, HB, KW), F32),
        pl=pltpu.VMEM((NH, T, KW), BF), pm=pltpu.VMEM((NH, T, M), BF), diff=pltpu.VMEM((T, G), F32),
        joined=pltpu.VMEM((T, G), BF), ga=pltpu.VMEM((T, U), F32), ntl=pltpu.VMEM((T, D), BF),
        resid=pltpu.VMEM((HB, D), F32), act=pltpu.VMEM((T, U), BF), gi=pltpu.VMEM((T, U), BF),
        gib=pltpu.VMEM((8, U), F32), ibv=pltpu.VMEM((1, U), F32), tr=pltpu.VMEM((U, T), BF), trn=pltpu.VMEM((D, T), BF), gres=pltpu.VMEM((HB, D), F32),
        gat=pltpu.VMEM((T, D), BF), gl=pltpu.VMEM((T, G), BF), gm=pltpu.VMEM((T, G), BF),
        gqkv=pltpu.VMEM((T, 3 * G), BF), bo=pltpu.VMEM((T, D), BF), gt=pltpu.VMEM((T, D), BF),
        part=pltpu.VMEM((2, T, D), BF), cbuf=pltpu.VMEM((2, HB, D), BF), ybuf=pltpu.VMEM((2, HB, D), BF),
        small=pltpu.VMEM((len(doubling) + 2, 8, D), F32), sbuf=pltpu.VMEM((len(doubling) + 1, 8, D), F32),
        g=pltpu.VMEM((nseg, seg, TILE), BF), res=pltpu.VMEM((nseg, seg, TILE), BF),
        rbuf=pltpu.VMEM((rows_needed, TILE), BF),
        in_sem=sem((13,)), out_sem=sem((2 + 2 * (D // TILE) + U // TILE + 4,)),
        c_send=sem((4, HALVES)), c_recv=sem((4, HALVES)), y_send=sem((4, HALVES)), y_recv=sem((4, HALVES)),
        a_send=sem((4, HALVES)), a_recv=sem((4, HALVES)),
        s_send=sem((len(doubling) + 1,)), s_recv=sem((len(doubling) + 1,)),
        dp_send=sem((nseg, S, 2, 3, 4)), dp_recv=sem((nseg, S, 2, 3, 2)),
        x_send=sem((HALVES + 2,)), x_recv=sem((HALVES + 2,)),
    )
    cfg = Space(
        n=n, T=T, D=D, G=G, U=U, M=M, NH=NH, K=K, stages=stages, doubling=doubling, seg=seg, offsets=offsets,
        late=ffn,
        names=[*inputs, *vectors, "fill", *outputs, *scratch],
    )
    any_spec = pl.BlockSpec(memory_space=pl.ANY)
    vec_spec = pl.BlockSpec(memory_space=pltpu.VMEM)
    outs = pl.pallas_call(
        functools.partial(kernel, cfg),
        out_shape=[jax.ShapeDtypeStruct(*v) for v in outputs.values()],
        in_specs=[any_spec] * len(inputs) + [vec_spec] * len(vectors) + [pl.BlockSpec(memory_space=pltpu.SMEM)],
        out_specs=[any_spec] * len(outputs),
        scratch_shapes=list(scratch.values()),
        compiler_params=pltpu.CompilerParams(
            collective_id=0, has_side_effects=True, vmem_limit_bytes=63 * MIB
        ),
        cost_estimate=pl.CostEstimate(flops=12 * 10**9, bytes_accessed=20 * 10**6, transcendentals=3 * 10**6),
    )(
        *inputs.values(), *vectors.values(), fill,
    )
    return widen(outs, NH)


def widen_kernel(NH, cuts, *refs):
    ins, outs, scratch = refs[:9], refs[9:24], refs[24:]
    boxes = len(cuts)
    low, (in_sem, out_sem), high = scratch[:boxes], scratch[boxes : boxes + 2], list(scratch[boxes + 2 :])
    high = [low[n] if cut[0] < 2 else high.pop(0) for n, cut in enumerate(cuts)]
    loads, stores = [], []
    for n, (i, at, rows, cols) in enumerate(cuts):
        loads.append(pltpu.make_async_copy(ins[i].at[pl.ds(at, rows)], low[n], in_sem.at[n]))
        stores.append(pltpu.make_async_copy(high[n], outs[i].at[pl.ds(at, rows)], out_sem.at[n]))
        loads[n].start()
    small = ins[8]
    for i in range(5):
        outs[8 + i][...] = small[i : i + 1, :]
    for h in range(NH):
        outs[13][h : h + 1, :] = small[5:6, h * LANES : h * LANES + NB]
        outs[14][:, h : h + 1] = small[6:7, h * LANES : h * LANES + 1]
    for n, (i, at, rows, cols) in enumerate(cuts):
        loads[n].wait()
        if high[n] is not low[n]:
            high[n][...] = low[n][...].astype(F32)
        stores[n].start()
    for c in stores:
        c.wait()


def widen(sums, NH):
    small = sums[8]
    D = small.shape[1]
    cuts = []
    for i in (2, 3, 4, 5, 6, 7, 0, 1):
        rows, cols = sums[i].shape
        step = max(16, min(rows, 2 * TILE * D // cols))
        cuts += [(i, at, step, cols) for at in range(0, rows, step)]
    shapes = [jax.ShapeDtypeStruct(x.shape, BF if i < 2 else F32) for i, x in enumerate(sums[:8])]
    tiny = [(1, D)] * 5 + [(NH, NB), (1, NH)]
    hbm = pl.BlockSpec(memory_space=pl.ANY)
    vec = pl.BlockSpec(memory_space=pltpu.VMEM)
    got = pl.pallas_call(
        functools.partial(widen_kernel, NH, cuts),
        in_specs=[hbm] * 8 + [vec],
        out_specs=[hbm] * 8 + [vec] * len(tiny),
        out_shape=shapes + [jax.ShapeDtypeStruct(x, F32) for x in tiny],
        scratch_shapes=[pltpu.VMEM((rows, cols), BF) for _, _, rows, cols in cuts]
        + [pltpu.SemaphoreType.DMA((len(cuts),))] * 2
        + [pltpu.VMEM((rows, cols), F32) for i, _, rows, cols in cuts if i >= 2],
        compiler_params=pltpu.CompilerParams(vmem_limit_bytes=60 * MIB),
        cost_estimate=pl.CostEstimate(flops=0, bytes_accessed=22 * 10**6, transcendentals=0),
    )(*sums)
    block_out, gtok, gwq, gwk, gwv, gwo, gwi, gwu, g1, s1, g2, s2, ib, bias, gates = got
    return (
        block_out, gtok, gwq, gwk, gwv, gwo, gwi, ib.reshape(-1), gwu, g1.reshape(D), s1.reshape(D), g2.reshape(D),
        s2.reshape(D), bias, gates.reshape(NH),
    )


def solution(mesh):
    return jax.shard_map(
        functools.partial(local, mesh.shape["dp"]),
        mesh=mesh,
        in_specs=(
            P("dp", None), P(None, "head"), P(None, "head"), P(None, "head"), P("head", None), P(None, "head"),
            P("head"), P("head", None), P(), P(), P(), P(), P("head", None), P("head"), P("dp", "head"),
            P("dp", "head"), P("dp", None, "head"), P("dp", None, "head"), P("dp", "head", None), P("dp"),
            P("dp", None),
        ),
        out_specs=(
            P("dp", None), P("dp", None), P(None, "head"), P(None, "head"), P(None, "head"), P("head", None),
            P(None, "head"), P("head"), P("head", None), P(), P(), P(), P(), P("head", None), P("head"),
        ),
        check_vma=False,
    )
```
